32 devices in a mesh: seq: 16 (over z, y, x), tensor: 2 (over core).
Axes of the slice: x: 2, y: 2, z: 4, core: 2. Of those that a mesh axis runs over, the one named last changes fastest.
Arguments:
- tokens: bfloat16 [4096, 2048], P('seq'), may hold values from -6 to 6
- gain_attn: bfloat16 [2048], P('seq'), may hold values from 0.5 to 1.5
- w_query: bfloat16 [2048, 256], P('seq', 'tensor'), may hold values from -0.125 to 0.125
- w_key: bfloat16 [2048, 256], P('seq', 'tensor'), may hold values from -0.125 to 0.125
- w_value: bfloat16 [2048, 2048], P('seq', 'tensor'), may hold values from -0.125 to 0.125
- w_output: bfloat16 [2048, 2048], P('tensor', 'seq'), may hold values from -2 to 2
- gain_mlp: bfloat16 [2048], P('seq'), may hold values from 0.5 to 1.5
- w_gate: bfloat16 [2048, 5504], P('seq', 'tensor'), may hold values from -0.125 to 0.125
- w_up: bfloat16 [2048, 5504], P('seq', 'tensor'), may hold values from -0.125 to 0.125
- w_down: bfloat16 [5504, 2048], P('tensor', 'seq'), may hold values from -0.078125 to 0.078125
- seq_lengths: int32 [3], replicated, may hold values from 64 to 3968, as said below
- cotangent: bfloat16 [4096, 2048], P('seq'), may hold values from -6 to 6
Outputs:
- output: bfloat16 [4096, 2048], P('seq')
- grad_tokens: float32 [4096, 2048], P('seq')
- grad_gain_attn: float32 [2048], P('seq')
- grad_w_query: float32 [2048, 256], P('seq', 'tensor')
- grad_w_key: float32 [2048, 256], P('seq', 'tensor')
- grad_w_value: float32 [2048, 2048], P('seq', 'tensor')
- grad_w_output: float32 [2048, 2048], P('tensor', 'seq')
- grad_gain_mlp: float32 [2048], P('seq')
- grad_w_gate: float32 [2048, 5504], P('seq', 'tensor')
- grad_w_up: float32 [2048, 5504], P('seq', 'tensor')
- grad_w_down: float32 [5504, 2048], P('tensor', 'seq')
The draws below stay inside these ranges and needn't reach their ends.
Inputs may be any that keep to these rules, and one draw needn't show every extreme that they name: `seq_lengths`: the lengths sum to 4096; the first and the last sequence each have fewer than 256 tokens, and the middle one holds the rest.
All inputs are finite; a program needn't handle non-finite values.
Results may differ from the reference program's by a relative error of at most 0.014.
Values may be sent and summed in bfloat16 or wider, within the bound.
A program may use at most 448 MiB of HBM per device.

```python
import math
import jax
import jax.numpy as jnp
from jax import lax

D = 2048
HEADS = 16
FEAT = 16
DV = 2048
FF = 5504
TOK_DEV = 256
FEATS = 273
TOKENS = 4096


def draw_seq_lengths(key, part):
    key = jax.random.fold_in(key, 7)
    first_key, last_key = jax.random.split(key)
    leading = jax.random.randint(first_key, (1,), TOK_DEV // 4, TOK_DEV, dtype=jnp.int32)
    trailing = jax.random.randint(last_key, (1,), TOK_DEV // 4, TOK_DEV, dtype=jnp.int32)
    middle = TOKENS - leading - trailing
    return jnp.concatenate([leading, middle, trailing]).astype(jnp.int32)


def spiked(values, stream_key, source, target, blocks, factor):
    def block_of(dim):
        return (jnp.arange(values.shape[dim]) // (values.shape[dim] // blocks)).reshape((-1,) + (1,) * (values.ndim - 1 - dim))

    near = jax.random.permutation(stream_key, blocks)[block_of(target)]
    second = (block_of(target) + blocks // 2) % blocks
    return jnp.where((block_of(source) == near) | (block_of(source) == second), factor * values, values)


def block_levels(rng, dims, pieces, low, high):
    factor_of, own = 1.0, jax.random.fold_in(rng, 6)
    for dim, shards_of in pieces:
        steps = jnp.exp(jax.random.uniform(jax.random.fold_in(own, dim), (shards_of,), jnp.float32, low / len(pieces), high / len(pieces)))
        factor_of = factor_of * jnp.repeat(steps, dims[dim] // shards_of).reshape([-1 if axis == dim else 1 for axis in range(len(dims))])
    return factor_of


def centred(stream_key, extent, spread, bound, shards=(), held_as=jnp.bfloat16):
    result = spread * jax.random.normal(stream_key, extent, jnp.float32)
    if shards:
        result = result * block_levels(stream_key, extent, shards, -0.22, 0.18)
    return jnp.clip(result, -bound, bound).astype(held_as)


def heavy_noise(key, shape, spread, limit, cuts, heavy, held_as=jnp.bfloat16):
    values = spread * jax.random.normal(key, shape, jnp.float32)
    if cuts:
        values = values * block_levels(key, shape, cuts, -0.22, 0.18)
    return jnp.clip(spiked(values, jax.random.fold_in(key, 3), *heavy), -limit, limit).astype(held_as)


def setup_inputs(seed: int = 0) -> dict:
    splits = jax.random.split(jax.random.key(seed), 13)
    return {
        "tokens": centred(splits[0], (TOKENS, D), 1.0, 6.0, ((0, 16),)),
        "gain_attn": jnp.clip(1.0 + 0.1 * jax.random.normal(splits[1], (D,), jnp.float32), 0.5, 1.5).astype(jnp.bfloat16),
        "w_query": centred(splits[2], (D, HEADS * FEAT), D ** -0.5, 0.125, ((0, 16), (1, 2))),
        "w_key": centred(splits[3], (D, HEADS * FEAT), D ** -0.5, 0.125, ((0, 16), (1, 2))),
        "w_value": centred(splits[4], (D, DV), D ** -0.5, 0.125, ((0, 16), (1, 2))),
        "w_output": centred(splits[5], (DV, D), (max(DV // 256, 4)) ** -0.5, 2.0, ((0, 2), (1, 16))),
        "gain_mlp": jnp.clip(1.0 + 0.1 * jax.random.normal(splits[6], (D,), jnp.float32), 0.5, 1.5).astype(jnp.bfloat16),
        "w_gate": centred(splits[7], (D, FF), D ** -0.5, 0.125, ((0, 16), (1, 2))),
        "w_up": centred(splits[8], (D, FF), D ** -0.5, 0.125, ((0, 16), (1, 2))),
        "w_down": centred(splits[9], (FF, D), FF ** -0.5, 0.078125, ((0, 2), (1, 16))),
        "seq_lengths": draw_seq_lengths(jax.random.fold_in(splits[12], 71), 0),
        "cotangent": heavy_noise(splits[11], (TOKENS, D), 1.0, 6.0, ((0, 16),), (0, 1, 16, 2.0)),
    }


EPS = 1e-06
HIGH = lax.Precision.HIGHEST

@jax.custom_vjp
def low(v):
    return lax.optimization_barrier(v.astype(jnp.bfloat16)).astype(jnp.float32)

@jax.custom_vjp
def low_back(v):
    return v

def low_keep(v):
    return (low(v), None)

def low_pass(kept, grad):
    return (grad,)

def back_keep(v):
    return (v, None)

def back_low(kept, grad):
    return (low(grad),)
low.defvjp(low_keep, low_pass)
low_back.defvjp(back_keep, back_low)

def features(scaled):
    feat_width = scaled.shape[-1]
    products = (scaled[..., :, None] * scaled[..., None, :]).reshape(scaled.shape[:-1] + (feat_width * feat_width,))
    constant = jnp.ones(scaled.shape[:-1] + (1,), jnp.float32)
    return jnp.concatenate([constant, scaled, products * 0.5 ** 0.5], axis=-1)

def attend(queries, keys_in, values_in, prefix_sum, prefix_norm, use_prefix, causal):
    scores = jnp.einsum('htf,hsf->hts', queries, keys_in, precision=HIGH)
    kernel = (1.0 + scores + 0.5 * scores * scores) * causal[None]
    numerator = jnp.einsum('hts,hse->hte', kernel, values_in, precision=HIGH)
    denominator = lax.optimization_barrier(jnp.sum(kernel, axis=-1))
    lifted = features(queries) * use_prefix[None, :, None]
    numerator = numerator + jnp.einsum('htp,hpe->hte', lifted, prefix_sum, precision=HIGH)
    denominator = denominator + jnp.einsum('htp,hp->ht', lifted, prefix_norm, precision=HIGH)
    return numerator / denominator[..., None]

def group_state(keys_in, values_in, contrib):
    lifted = features(keys_in) * contrib[None, :, None]
    return (jnp.einsum('htp,hte->hpe', lifted, values_in, precision=HIGH), lax.optimization_barrier(jnp.sum(lifted, axis=1)))

def token_masks(starts, position):
    group_first = position[0]
    group_last = position[-1]
    start_cols = starts[None, :]
    token_rows = position[:, None]
    seen_starts = lax.optimization_barrier(jnp.sum(((start_cols >= group_first) & (start_cols <= token_rows)).astype(jnp.int32), axis=1))
    later_starts = lax.optimization_barrier(jnp.sum(((start_cols > token_rows) & (start_cols <= group_last)).astype(jnp.int32), axis=1))
    reset_flag = jnp.max(((starts >= group_first) & (starts <= group_last)).astype(jnp.float32))
    segment = lax.optimization_barrier(jnp.sum((start_cols <= token_rows).astype(jnp.int32), axis=1))
    causal = ((position[None, :] <= position[:, None]) & (segment[None, :] == segment[:, None])).astype(jnp.float32)
    return ((seen_starts == 0).astype(jnp.float32), (later_starts == 0).astype(jnp.float32), reset_flag, causal)

def rms_norm(inputs, gain):
    inv_root = lax.rsqrt(lax.optimization_barrier(jnp.mean(inputs * inputs, axis=-1, keepdims=True)) + EPS)
    return inputs * inv_root * gain

def matmul(left, right):
    return jnp.dot(left, right, precision=HIGH)

def reference(tokens, gain_attn, w_query, w_key, w_value, w_output, gain_mlp, w_gate, w_up, w_down, seq_lengths, cotangent):
    starts = (jnp.cumsum(seq_lengths) - seq_lengths).astype(jnp.int32)
    block_rows = math.gcd(TOKENS, 512)
    block_count = TOKENS // block_rows
    mlp_rows = math.gcd(TOKENS, 4096)
    positions = jnp.arange(TOKENS, dtype=jnp.int32).reshape(block_count, block_rows)
    scale = FEAT ** (-0.25)
    head_dim = DV // HEADS

    def attention_block(carried, block_in):
        sum_before, norm_before = carried
        queries, keys_in, values_in, position = block_in
        use_prefix, contrib, reset_flag, causal = token_masks(starts, position)
        heads_out = attend(queries, keys_in, values_in, sum_before, norm_before, use_prefix, causal)
        local_sum, local_norm = group_state(keys_in, values_in, contrib)
        keep = 1.0 - reset_flag
        return ((local_sum + keep * sum_before, local_norm + keep * norm_before), heads_out)

    def to_blocks(matrix):
        return matrix.reshape(block_count, block_rows, HEADS, -1).transpose(0, 2, 1, 3)

    def layer(inputs, gain_one, query_w, key_w, value_w, output_w, gain_two, gate_w, up_w, down_w):
        low_one = low(rms_norm(inputs, gain_one))
        query_f = low_back(low(matmul(low_one, query_w)))
        key_f = low_back(low(matmul(low_one, key_w)))
        value_f = low_back(low(matmul(low_one, value_w)))
        start_state = (jnp.zeros((HEADS, FEATS, head_dim), jnp.float32), jnp.zeros((HEADS, FEATS), jnp.float32))
        final_state, heads_out = lax.scan(jax.checkpoint(attention_block), start_state, (to_blocks(query_f * scale), to_blocks(key_f * scale), to_blocks(value_f), positions))
        attn_low = low(heads_out.transpose(0, 2, 1, 3).reshape(TOKENS, DV))
        residual = inputs + low_back(matmul(attn_low, output_w))

        def mlp_block(rows_in):
            low_two = low(rms_norm(rows_in, gain_two))
            gate_pre = low_back(matmul(low_two, gate_w))
            up_pre = low_back(matmul(low_two, up_w))
            hidden = low(jax.nn.silu(gate_pre) * up_pre)
            return rows_in + low_back(matmul(hidden, down_w))
        blocks_out = lax.map(jax.checkpoint(mlp_block), residual.reshape(TOKENS // mlp_rows, mlp_rows, D))
        return blocks_out.reshape(TOKENS, D)
    output, layer_back = jax.vjp(layer, tokens.astype(jnp.float32), gain_attn.astype(jnp.float32), w_query.astype(jnp.float32), w_key.astype(jnp.float32), w_value.astype(jnp.float32), w_output.astype(jnp.float32), gain_mlp.astype(jnp.float32), w_gate.astype(jnp.float32), w_up.astype(jnp.float32), w_down.astype(jnp.float32))
    grads = layer_back(cotangent.astype(jnp.float32))
    return (output.astype(jnp.bfloat16), grads[0], grads[1], grads[2], grads[3], grads[4], grads[5], grads[6], grads[7], grads[8], grads[9])
```

```python
import functools

import jax
import jax.numpy as jnp
import numpy as np
from jax import lax
from jax.experimental import pallas as pl
from jax.experimental.pallas import tpu as pltpu
from jax.sharding import PartitionSpec as P

MESH = pl.DeviceIdType.MESH
HEADS = 16
FEAT = 16
CUBE = 8
UNITS = 352
EPS = 1e-06
F32 = jnp.float32
BF16 = jnp.bfloat16
ORDERS = ((0, 1, 2), (1, 2, 0), (2, 0, 1))
PIECES = ((0, 48), (48, 48), (96, 32))
MIB = 1 << 20


def flip(place, mask):
    total = 0
    for b in range(3):
        bit = (place // (1 << b)) % 2
        total = total + ((1 - bit) if (mask >> b) & 1 else bit) * (1 << b)
    return total


def subsets(dims):
    out = [0]
    for d in dims:
        out = out + [r | (1 << d) for r in out]
    return out


def whereabouts():
    s = lax.axis_index("seq")
    t = lax.axis_index("tensor")
    j = s % CUBE
    return s, t, j, s - j


def remote(src, dst, send, recv, device):
    return pltpu.make_async_remote_copy(
        src_ref=src, dst_ref=dst, send_sem=send, recv_sem=recv, device_id=device, device_id_type=MESH
    )


def greet(devices):
    barrier = pltpu.get_barrier_semaphore()
    for device in devices:
        pl.semaphore_signal(barrier, inc=1, device_id=device, device_id_type=MESH)
    pl.semaphore_wait(barrier, len(devices))


def near():
    s, t, j, base = whereabouts()
    return [(base + flip(j, 1 << d), t) for d in range(3)] + [(s, 1 - t)]


def greet_all(n):
    s, t, _, _ = whereabouts()
    barrier = pltpu.get_barrier_semaphore()

    def one(k, carry):
        pl.semaphore_signal(barrier, inc=1, device_id=((s + k) % n, t), device_id_type=MESH)
        return carry

    lax.fori_loop(1, n, one, 0)
    pl.semaphore_signal(barrier, inc=1, device_id=(s, 1 - t), device_id_type=MESH)
    pl.semaphore_wait(barrier, n)


class Gather:
    def __init__(self, own, full, sems):
        self.own, self.full = own, full
        self.ssem, self.rsem, self.csend, self.crecv, self.lsem = sems
        self.s, self.t, self.j, self.base = whereabouts()

    def view(self, r, i):
        off, rows = PIECES[i]
        return self.full.at[flip(self.j, r), self.t, pl.ds(off, rows)]

    def other(self, r, i):
        off, rows = PIECES[i]
        return self.full.at[flip(self.j, r), 1 - self.t, pl.ds(off, rows)]

    def hop(self, p, i, r):
        d = ORDERS[i][p]
        off, rows = PIECES[i]
        src = self.own.at[self.t, pl.ds(off, rows)] if r == 0 else self.view(r, i)
        k = r | (1 << d)
        return remote(src, self.view(r, i), self.ssem.at[i, k], self.rsem.at[i, k], (self.base + flip(self.j, 1 << d), self.t))

    def arrival(self, p, i, r):
        d = ORDERS[i][p]
        k = r | (1 << d)
        return remote(self.view(k, i), self.view(k, i), self.ssem.at[i, k], self.rsem.at[i, k], (self.base + flip(self.j, 1 << d), self.t))

    def across(self, r, i, mine):
        ref = self.view(r, i) if mine else self.other(r, i)
        return remote(ref, ref, self.csend.at[i, r], self.crecv.at[i, r], (self.s, 1 - self.t))

    def local(self):
        return pltpu.make_async_copy(self.own, self.full.at[self.j], self.lsem)

    def start(self, p):
        if p == 0:
            self.local().start()
        for i in range(3):
            for r in subsets(ORDERS[i][:p]):
                self.hop(p, i, r).start()

    def arrive(self, p):
        for i in range(3):
            for r in subsets(ORDERS[i][:p]):
                self.arrival(p, i, r).wait_recv()

    def share(self, p):
        for i in range(3):
            for r in subsets(ORDERS[i][:p]):
                self.across(r | (1 << ORDERS[i][p]), i, True).start()

    def finish(self):
        for i in range(3):
            for r in range(1, CUBE):
                self.across(r, i, False).wait_recv()
        for i in range(3):
            for r in range(1, CUBE):
                self.across(r, i, True).wait_send()
        for p in range(3):
            for i in range(3):
                for r in subsets(ORDERS[i][:p]):
                    self.hop(p, i, r).wait_send()
        self.local().wait()

    def run(self):
        for p in range(3):
            self.start(p)
            self.arrive(p)
            self.share(p)
        self.finish()


def gather_sems():
    return [pltpu.SemaphoreType.DMA((3, CUBE))] * 4 + [pltpu.SemaphoreType.DMA]


def gather_kernel(own, full, *sems):
    greet(near())
    Gather(own, full, sems).run()


def gather(x, number):
    rows, width = x.shape
    out = pl.pallas_call(
        gather_kernel,
        out_shape=jax.ShapeDtypeStruct((CUBE, 2, rows // 2, width), x.dtype),
        in_specs=[pl.BlockSpec(memory_space=pl.ANY)],
        out_specs=pl.BlockSpec(memory_space=pl.ANY),
        scratch_shapes=gather_sems(),
        compiler_params=pltpu.CompilerParams(collective_id=number, has_side_effects=True),
    )(x.reshape(2, rows // 2, width))
    return out.reshape(CUBE * rows, width)


SLOT = {0: 0, 1: 4, 2: 6}


def slot_of(p, i, r):
    kept = subsets(ORDERS[i][p + 1 :])
    return SLOT[p] + kept.index(r)


class Sum:
    def __init__(self, part, heap, total, sems):
        self.part, self.heap, self.total = part, heap, total
        self.csend, self.crecv, self.ssem, self.rsem, self.fsend, self.frecv = sems
        self.s, self.t, self.j, self.base = whereabouts()

    def across(self, r, mine):
        jj = flip(self.j, r)
        src = self.part.at[jj, 1 - self.t]
        return remote(src, self.heap.at[r], self.csend.at[r], self.crecv.at[r], (self.s, 1 - self.t))

    def hop(self, p, i, r):
        d = ORDERS[i][p]
        off, rows = PIECES[i]
        k = slot_of(p, i, r ^ (1 << d))
        return remote(
            self.part.at[flip(self.j, r), self.t, pl.ds(off, rows)],
            self.heap.at[CUBE + k, pl.ds(off, rows)],
            self.ssem.at[i, k],
            self.rsem.at[i, k],
            (self.base + flip(self.j, 1 << d), self.t),
        )

    def start(self):
        order = [7, 6, 5, 3, 4, 2, 1, 0]
        for r in order:
            self.across(r, True).start()
        for r in order:
            self.across(r, False).wait_recv()
            jj = flip(self.j, r)
            self.part[jj, self.t] = (self.part[jj, self.t].astype(F32) + self.heap[r].astype(F32)).astype(BF16)

    def phase(self, p):
        for i in range(3):
            d = ORDERS[i][p]
            for r in subsets(ORDERS[i][p + 1 :]):
                self.hop(p, i, r | (1 << d)).start()
        for i in range(3):
            d = ORDERS[i][p]
            off, rows = PIECES[i]
            for r in subsets(ORDERS[i][p + 1 :]):
                self.hop(p, i, r | (1 << d)).wait_recv()
                jj = flip(self.j, r)
                k = slot_of(p, i, r)
                mine = self.part[jj, self.t, pl.ds(off, rows)].astype(F32)
                new = mine + self.heap[CUBE + k, pl.ds(off, rows)].astype(F32)
                if p == 2:
                    self.total[self.t, pl.ds(off, rows)] = new
                else:
                    self.part[jj, self.t, pl.ds(off, rows)] = new.astype(BF16)

    def last(self):
        mine = self.total.at[self.t]
        cp = remote(mine, mine, self.fsend, self.frecv, (self.s, 1 - self.t))
        cp.start()
        theirs = self.total.at[1 - self.t]
        remote(theirs, theirs, self.fsend, self.frecv, (self.s, 1 - self.t)).wait_recv()
        cp.wait_send()

    def finish(self):
        for r in range(CUBE):
            self.across(r, True).wait_send()
        for p in range(3):
            for i in range(3):
                d = ORDERS[i][p]
                for r in subsets(ORDERS[i][p + 1 :]):
                    self.hop(p, i, r | (1 << d)).wait_send()

    def run(self):
        self.start()
        for p in range(3):
            self.phase(p)
        self.last()
        self.finish()


def sum_sems():
    return [
        pltpu.SemaphoreType.DMA((CUBE,)),
        pltpu.SemaphoreType.DMA((CUBE,)),
        pltpu.SemaphoreType.DMA((3, CUBE)),
        pltpu.SemaphoreType.DMA((3, CUBE)),
        pltpu.SemaphoreType.DMA,
        pltpu.SemaphoreType.DMA,
    ]


def sum_kernel(given, total, part, heap, lsem, *sems):
    greet(near())
    load = pltpu.make_async_copy(given, part, lsem)
    load.start()
    load.wait()
    Sum(part, heap, total, sems).run()


def cube_sum(x, number):
    rows, width = x.shape[0] // CUBE, x.shape[1]
    half = rows // 2
    out = pl.pallas_call(
        sum_kernel,
        out_shape=jax.ShapeDtypeStruct((2, half, width), F32),
        in_specs=[pl.BlockSpec(memory_space=pl.ANY)],
        out_specs=pl.BlockSpec(memory_space=pltpu.VMEM),
        scratch_shapes=[
            pltpu.VMEM((CUBE, 2, half, width), BF16),
            pltpu.VMEM((15, half, width), BF16),
            pltpu.SemaphoreType.DMA,
            *sum_sems(),
        ],
        compiler_params=pltpu.CompilerParams(collective_id=number, has_side_effects=True, vmem_limit_bytes=50 * MIB),
    )(x.reshape(CUBE, 2, half, width))
    return out.reshape(rows, width)


def columns_of(ref, s):
    if len(ref.shape) == 3:
        return ref.at[s]
    return ref.at[:, pl.ds(pl.multiple_of(s * 128, 128), 128)]


def columns_apart(n, rows, width):
    return (rows, width) if width // n % 128 == 0 else (n, rows, width // n)


def together(x):
    return x if x.ndim == 2 else x.transpose(1, 0, 2).reshape(x.shape[1], -1)


def apart(n, x):
    return x if x.shape[1] // n % 128 == 0 else x.reshape(x.shape[0], n, -1).transpose(1, 0, 2)


class Spread:
    def __init__(self, n, pack, full, sems):
        self.n, self.pack, self.full = n, pack, full
        self.ssem, self.rsem, self.lsem = sems
        self.s, self.t, self.j, self.base = whereabouts()

    def columns(self, s):
        return columns_of(self.full, s)

    def copy(self, k):
        to = (self.s + k) % self.n
        return remote(self.pack.at[to % CUBE], self.columns(self.s), self.ssem.at[k], self.rsem.at[k], (to, self.t))

    def arrival(self, k):
        at = (self.s + self.n - k) % self.n
        return remote(self.pack.at[0], self.columns(at), self.ssem.at[k], self.rsem.at[k], (at, self.t))

    def local(self):
        return pltpu.make_async_copy(self.pack.at[self.j], self.columns(self.s), self.lsem)

    def start(self):
        lax.fori_loop(1, self.n, lambda k, c: (self.copy(k).start(), c)[1], 0)
        self.local().start()

    def finish(self):
        self.local().wait()
        lax.fori_loop(1, self.n, lambda k, c: (self.arrival(k).wait_recv(), c)[1], 0)
        lax.fori_loop(1, self.n, lambda k, c: (self.copy(k).wait_send(), c)[1], 0)


class Back:
    def __init__(self, n, grads, tiles, sems):
        self.n, self.grads, self.tiles = n, grads, tiles
        self.ssem, self.rsem, self.lsem = sems
        self.s, self.t, self.j, self.base = whereabouts()

    def columns(self, s):
        return columns_of(self.grads, s)

    def copy(self, k):
        to = (self.s + k) % self.n
        return remote(self.columns(to), self.tiles.at[self.s], self.ssem.at[k], self.rsem.at[k], (to, self.t))

    def arrival(self, k):
        at = (self.s + self.n - k) % self.n
        return remote(self.tiles.at[at], self.tiles.at[at], self.ssem.at[k], self.rsem.at[k], (at, self.t))

    def local(self):
        return pltpu.make_async_copy(self.columns(self.s), self.tiles.at[self.s], self.lsem)

    start = Spread.start
    finish = Spread.finish


def spread_sems(n):
    return [pltpu.SemaphoreType.DMA((n,)), pltpu.SemaphoreType.DMA((n,)), pltpu.SemaphoreType.DMA]


def head_kernel(n, pack_a, pack_b, tokens, cot, w_a, w_b, tokens_all, cot_all, *sems):
    greet_all(n)
    first = Spread(n, pack_a, w_a, sems[0:3])
    second = Spread(n, pack_b, w_b, sems[3:6])
    g_tok = Gather(tokens, tokens_all, sems[6:11])
    g_cot = Gather(cot, cot_all, sems[11:16])
    first.start()
    g_tok.start(0)
    second.start()
    for p in range(3):
        g_tok.arrive(p)
        if p < 2:
            g_tok.start(p + 1)
        else:
            g_cot.start(0)
        g_tok.share(p)
    for p in range(3):
        g_cot.arrive(p)
        if p < 2:
            g_cot.start(p + 1)
        g_cot.share(p)
    g_tok.finish()
    g_cot.finish()
    first.finish()
    second.finish()


def head_call(n, pack_a, pack_b, tokens, cot):
    rows, width = tokens.shape
    shape = (CUBE, 2, rows // 2, width)
    any_space = pl.BlockSpec(memory_space=pl.ANY)
    w_a, w_b, tok, ct = pl.pallas_call(
        functools.partial(head_kernel, n),
        out_shape=[
            jax.ShapeDtypeStruct(columns_apart(n, pack_a.shape[1], width), BF16),
            jax.ShapeDtypeStruct(columns_apart(n, pack_b.shape[1], width), BF16),
            jax.ShapeDtypeStruct(shape, BF16),
            jax.ShapeDtypeStruct(shape, BF16),
        ],
        in_specs=[any_space] * 4,
        out_specs=[any_space] * 4,
        scratch_shapes=[*spread_sems(n), *spread_sems(n), *gather_sems(), *gather_sems()],
        compiler_params=pltpu.CompilerParams(collective_id=0, has_side_effects=True),
    )(pack_a, pack_b, tokens.reshape(2, rows // 2, width), cot.reshape(2, rows // 2, width))
    return together(w_a), together(w_b), tok.reshape(-1, width), ct.reshape(-1, width)


def back_kernel(n, grads, tiles, *sems):
    greet_all(n)
    back = Back(n, grads, tiles, sems)
    back.start()
    back.finish()


def back_call(n, grads, number):
    rows, width = grads.shape
    any_space = pl.BlockSpec(memory_space=pl.ANY)
    return pl.pallas_call(
        functools.partial(back_kernel, n),
        out_shape=jax.ShapeDtypeStruct((n, rows, width // n), BF16),
        in_specs=[any_space],
        out_specs=any_space,
        scratch_shapes=spread_sems(n),
        compiler_params=pltpu.CompilerParams(collective_id=number, has_side_effects=True),
    )(apart(n, grads))


def dot(a, b):
    return jnp.dot(a, b, preferred_element_type=F32)


def dot_nt(a, b):
    return lax.dot_general(a, b, (((1,), (1,)), ((), ())), preferred_element_type=F32)


def dot_tn(a, b):
    return lax.dot_general(a, b, (((0,), (0,)), ((), ())), preferred_element_type=F32)


def spreaders():
    first = np.repeat(np.eye(FEAT), FEAT, axis=1)
    second = np.tile(np.eye(FEAT), (1, FEAT))
    third = np.eye(FEAT, 128)
    return [jnp.asarray(m, BF16) for m in (first, second, third)]


ROOT_HALF = 0.5**0.5


def lift(u, keep, first, second, third):
    quad = dot(u, first) * dot(u, second) * (0.25 * ROOT_HALF) * keep
    lane = lax.broadcasted_iota(jnp.int32, (u.shape[0], 128), 1)
    line = (dot(u, third) * 0.5 + jnp.where(lane == FEAT, 1.0, 0.0)) * keep
    return quad.astype(BF16), line.astype(BF16)


def lift_back(u, d_quad, d_line, first, second):
    one, two = dot(u, first) * 0.5, dot(u, second) * 0.5
    back = dot_nt((d_quad * two).astype(BF16), first) + dot_nt((d_quad * one).astype(BF16), second)
    return back * ROOT_HALF + d_line[:, :FEAT]


def two_terms(x):
    high = x.astype(BF16)
    return high, (x - high.astype(F32)).astype(BF16)


def segments(start_two, start_three, first_position, count, axis):
    shape = (count, 1) if axis == 0 else (1, count)
    position = first_position + lax.broadcasted_iota(jnp.int32, shape, axis)
    return position, (position >= start_two).astype(jnp.int32) + (position >= start_three).astype(jnp.int32)


def pair_mask(two, three, at_t, at_s, block):
    pos_t, seg_t = segments(two, three, at_t, block, 0)
    pos_s, seg_s = segments(two, three, at_s, block, 1)
    return (pos_s <= pos_t) & (seg_s == seg_t)


def other_groups(groups):
    s, t, j, base = whereabouts()
    return [((s + CUBE * k) % (CUBE * groups), t) for k in range(1, groups)]


def exchange(groups, mine, theirs, ssem, rsem, before):
    s, t, j, base = whereabouts()
    c = s // CUBE
    for k, device in enumerate(other_groups(groups)):
        remote(mine, theirs.at[k], ssem.at[k], rsem.at[k], device).start()

    def finish():
        total = jnp.zeros(mine.shape, F32)
        for k, device in enumerate(other_groups(groups)):
            remote(mine, theirs.at[k], ssem.at[k], rsem.at[k], device).wait_recv()
            source = (c + groups - (k + 1)) % groups
            counts = (source < c) if before else (source > c)
            total = total + jnp.where(counts, theirs[k], 0.0)
        for k, device in enumerate(other_groups(groups)):
            remote(mine, theirs.at[k], ssem.at[k], rsem.at[k], device).wait_send()
        return total

    return finish


BLOCK = 256


def attend_kernel(
    groups, lengths, x_ref, w_ref, first, second, third,
    low_ref, q_ref, k_ref, v_ref, y_ref, den_ref, state_ref,
    state_mine, state_theirs, ssem, rsem,
):
    step = pl.program_id(0)
    steps = pl.num_programs(0)
    s, t, j, base = whereabouts()
    rows = x_ref.shape[0]
    two, three = lengths[0], lengths[0] + lengths[1]
    start = base * rows
    here = pl.ds(pl.multiple_of(step * rows, rows), rows)

    @pl.when(step == 0)
    def _():
        greet(other_groups(groups))
        state_mine[...] = jnp.zeros_like(state_mine)

    x = x_ref[...].astype(F32)
    root = lax.rsqrt(jnp.mean(x * x, axis=-1, keepdims=True) + EPS)
    low = (x * root * w_ref[160:161, :].astype(F32)).astype(BF16)
    low_ref[...] = low
    q = dot_nt(low, w_ref[128:144, :]).astype(BF16)
    k = dot_nt(low, w_ref[144:160, :]).astype(BF16)
    v = dot_nt(low, w_ref[0:128, :]).astype(BF16)
    lane = lax.broadcasted_iota(jnp.int32, (rows, 128), 1)
    v_ext = jnp.concatenate([v, jnp.where(lane < 2, 1.0, 0.0).astype(BF16)], axis=1)
    q_ref[here, :] = q
    k_ref[here, :] = k
    v_ref[here, :] = v_ext
    _, seg = segments(two, three, start + step * rows, rows, 0)
    quad, line = lift(k, (seg == 1).astype(F32), first[...], second[...], third[...])
    state_mine[0:256, :] += dot_tn(quad, v_ext)
    state_mine[256:384, :] += dot_tn(line, v_ext)

    @pl.when(step == steps - 1)
    def _():
        done = exchange(groups, state_mine, state_theirs, ssem, rsem, True)
        total = q_ref.shape[0]

        def outer(tb, carry):
            tq = pl.ds(pl.multiple_of(tb * BLOCK, BLOCK), BLOCK)
            qt = q_ref[tq, :]

            def inner(sb, acc):
                sq = pl.ds(pl.multiple_of(sb * BLOCK, BLOCK), BLOCK)
                score = dot_nt(qt, k_ref[sq, :]) * 0.25
                mask = pair_mask(two, three, start + tb * BLOCK, start + sb * BLOCK, BLOCK)
                weight = jnp.where(mask, 1.0 + score + 0.5 * score * score, 0.0).astype(BF16)
                return acc + dot(weight, v_ref[sq, :])

            acc = lax.fori_loop(0, tb + 1, inner, jnp.zeros((BLOCK, 256), F32))
            y_ref[tq, :] = acc[:, :128]
            den_ref[tq, :] = acc[:, 128:]
            return carry

        lax.fori_loop(0, total // BLOCK, outer, 0)
        state = done()
        state_ref[...] = state
        high, lowp = two_terms(state)

        def late(tb, carry):
            tq = pl.ds(pl.multiple_of(tb * BLOCK, BLOCK), BLOCK)
            _, seg = segments(two, three, start + tb * BLOCK, BLOCK, 0)
            quad, line = lift(q_ref[tq, :], (seg == 1).astype(F32), first[...], second[...], third[...])
            more = dot(quad, high[0:256]) + dot(quad, lowp[0:256]) + dot(line, high[256:384]) + dot(line, lowp[256:384])
            num = y_ref[tq, :] + more[:, :128]
            den = den_ref[tq, :] + more[:, 128:]
            den_ref[tq, :] = den
            y_ref[tq, :] = num / den[:, 0:1]
            return carry

        lax.fori_loop(0, total // BLOCK, late, 0)


def attend_call(n, lengths, x_all, w_a):
    groups = n // CUBE
    count, width = x_all.shape
    rows = count // CUBE
    vm = pl.BlockSpec(memory_space=pltpu.VMEM)
    whole = lambda *shape: pl.BlockSpec(shape, lambda i: (0,) * len(shape))
    peers = max(groups - 1, 1)
    return pl.pallas_call(
        functools.partial(attend_kernel, groups),
        grid=(CUBE,),
        out_shape=[
            jax.ShapeDtypeStruct((count, width), BF16),
            jax.ShapeDtypeStruct((count, FEAT), BF16),
            jax.ShapeDtypeStruct((count, FEAT), BF16),
            jax.ShapeDtypeStruct((count, 256), BF16),
            jax.ShapeDtypeStruct((count, 128), F32),
            jax.ShapeDtypeStruct((count, 128), F32),
            jax.ShapeDtypeStruct((384, 256), F32),
        ],
        in_specs=[
            pl.BlockSpec(memory_space=pltpu.SMEM),
            pl.BlockSpec((rows, width), lambda i: (i, 0)),
            whole(*w_a.shape),
            whole(FEAT, 256),
            whole(FEAT, 256),
            whole(FEAT, 128),
        ],
        out_specs=[
            pl.BlockSpec((rows, width), lambda i: (i, 0)),
            whole(count, FEAT),
            whole(count, FEAT),
            whole(count, 256),
            whole(count, 128),
            whole(count, 128),
            whole(384, 256),
        ],
        scratch_shapes=[
            pltpu.VMEM((384, 256), F32),
            pltpu.VMEM((peers, 384, 256), F32),
            pltpu.SemaphoreType.DMA((peers,)),
            pltpu.SemaphoreType.DMA((peers,)),
        ],
        compiler_params=pltpu.CompilerParams(collective_id=1, has_side_effects=True, vmem_limit_bytes=50 * MIB),
    )(lengths, x_all, w_a, *spreaders())


def attend_back_kernel(
    groups, lengths, q_ref, k_ref, v_ref, y_ref, den_ref, state_ref, dy_ref, first, second, third,
    dq_ref, dk_ref, dv_ref,
    c_ref, da, db, dv, state_mine, state_theirs, ssem, rsem,
):
    s, t, j, base = whereabouts()
    total = q_ref.shape[0]
    blocks = total // BLOCK
    two, three = lengths[0], lengths[0] + lengths[1]
    start = base * (total // CUBE)
    greet(other_groups(groups))
    state_mine[...] = jnp.zeros_like(state_mine)
    db[...] = jnp.zeros_like(db)
    dv[...] = jnp.zeros_like(dv)
    state = state_ref[...].astype(BF16)

    def early(tb, carry):
        tq = pl.ds(pl.multiple_of(tb * BLOCK, BLOCK), BLOCK)
        _, seg = segments(two, three, start + tb * BLOCK, BLOCK, 0)
        keep = (seg == 1).astype(F32)
        c = (dy_ref[tq, :].astype(F32) / den_ref[tq, 0:1]).astype(BF16)
        m = -jnp.sum(c.astype(F32) * y_ref[tq, :], axis=-1, keepdims=True)
        m_high = m.astype(BF16).astype(F32)
        lane = lax.broadcasted_iota(jnp.int32, (BLOCK, 128), 1)
        extra = jnp.where(lane == 0, m_high, jnp.where(lane == 1, m - m_high, 0.0)).astype(BF16)
        c_ext = jnp.concatenate([c, extra], axis=1)
        c_ref[tq, :] = c_ext
        u = q_ref[tq, :]
        quad, line = lift(u, keep, first[...], second[...], third[...])
        state_mine[0:256, :] += dot_tn(quad, c_ext)
        state_mine[256:384, :] += dot_tn(line, c_ext)
        d_quad = dot_nt(c_ext, state[0:256]) * keep
        d_line = dot_nt(c_ext, state[256:384]) * keep
        da[tq, :] = lift_back(u, d_quad, d_line, first[...], second[...])
        return carry

    lax.fori_loop(0, blocks, early, 0)
    done = exchange(groups, state_mine, state_theirs, ssem, rsem, False)

    def outer(tb, carry):
        tq = pl.ds(pl.multiple_of(tb * BLOCK, BLOCK), BLOCK)
        qt = q_ref[tq, :]
        ct = c_ref[tq, :]

        def inner(sb, acc):
            sq = pl.ds(pl.multiple_of(sb * BLOCK, BLOCK), BLOCK)
            ks = k_ref[sq, :]
            score = dot_nt(qt, ks) * 0.25
            d_w = dot_nt(ct, v_ref[sq, :])
            mask = pair_mask(two, three, start + tb * BLOCK, start + sb * BLOCK, BLOCK)
            weight = jnp.where(mask, 1.0 + score + 0.5 * score * score, 0.0).astype(BF16)
            inner_grad = jnp.where(mask, d_w * (1.0 + score), 0.0).astype(BF16)
            db[sq, :] += dot_tn(inner_grad, qt) * 0.5
            dv[sq, :] += dot_tn(weight, ct)[:, :128]
            return acc + dot(inner_grad, ks)

        acc = lax.fori_loop(0, tb + 1, inner, jnp.zeros((BLOCK, FEAT), F32))
        dq_ref[tq, :] = ((da[tq, :] + acc * 0.5) * 0.5).astype(BF16)
        return carry

    lax.fori_loop(0, blocks, outer, 0)
    state_back = done().astype(BF16)

    def late(sb, carry):
        sq = pl.ds(pl.multiple_of(sb * BLOCK, BLOCK), BLOCK)
        _, seg = segments(two, three, start + sb * BLOCK, BLOCK, 0)
        keep = (seg == 1).astype(F32)
        u = k_ref[sq, :]
        v = v_ref[sq, :]
        quad, line = lift(u, keep, first[...], second[...], third[...])
        d_quad = dot_nt(v, state_back[0:256]) * keep
        d_line = dot_nt(v, state_back[256:384]) * keep
        more = dot(quad, state_back[0:256]) + dot(line, state_back[256:384])
        dk_ref[sq, :] = ((db[sq, :] + lift_back(u, d_quad, d_line, first[...], second[...])) * 0.5).astype(BF16)
        dv_ref[sq, :] = (dv[sq, :] + more[:, :128]).astype(BF16)
        return carry

    lax.fori_loop(0, blocks, late, 0)


def attend_back_call(n, lengths, q, k, v, y, den, state, dy):
    groups = n // CUBE
    count = q.shape[0]
    vm = pl.BlockSpec(memory_space=pltpu.VMEM)
    peers = max(groups - 1, 1)
    return pl.pallas_call(
        functools.partial(attend_back_kernel, groups),
        out_shape=[
            jax.ShapeDtypeStruct((count, FEAT), BF16),
            jax.ShapeDtypeStruct((count, FEAT), BF16),
            jax.ShapeDtypeStruct((count, 128), BF16),
        ],
        in_specs=[pl.BlockSpec(memory_space=pltpu.SMEM)] + [vm] * 10,
        out_specs=[vm] * 3,
        scratch_shapes=[
            pltpu.VMEM((count, 256), BF16),
            pltpu.VMEM((count, FEAT), F32),
            pltpu.VMEM((count, FEAT), F32),
            pltpu.VMEM((count, 128), F32),
            pltpu.VMEM((384, 256), F32),
            pltpu.VMEM((peers, 384, 256), F32),
            pltpu.SemaphoreType.DMA((peers,)),
            pltpu.SemaphoreType.DMA((peers,)),
        ],
        compiler_params=pltpu.CompilerParams(collective_id=2, has_side_effects=True, vmem_limit_bytes=50 * MIB),
    )(lengths, q, k, v, y, den, state, dy, *spreaders())


def units_first(w):
    return jnp.pad(w, ((0, CUBE * UNITS - w.shape[0]), (0, 0))).reshape(CUBE, UNITS, w.shape[1])


def body(
    n, tokens, gain_attn, w_query, w_key, w_value, w_output, gain_mlp, w_gate, w_up, w_down, seq_lengths, cotangent
):
    per = HEADS // lax.axis_size("tensor")
    gains = jnp.concatenate([gain_attn[None], gain_mlp[None], jnp.zeros((14, gain_attn.shape[0]), BF16)], axis=0)
    pack_a = jnp.concatenate(
        [
            w_value.T.reshape(per, 128, -1),
            w_query.T.reshape(per, FEAT, -1),
            w_key.T.reshape(per, FEAT, -1),
            jnp.broadcast_to(gains[None], (per, *gains.shape)),
            w_output.reshape(per, 128, -1),
        ],
        axis=1,
    )
    pack_b = jnp.concatenate([units_first(w_gate.T), units_first(w_up.T), units_first(w_down)], axis=1)
    w_a, w_b, tokens_all, cot_all = head_call(n, pack_a, pack_b, tokens, cotangent)
    gate_w, up_w, down_w = w_b[:UNITS], w_b[UNITS : 2 * UNITS], w_b[2 * UNITS :]
    out_w = w_a[176:304]

    low_one, q, k, v, y, den, state = attend_call(n, seq_lengths, tokens_all, w_a)
    attn_low = y.astype(BF16)
    attn_out = cube_sum(dot(attn_low, out_w).astype(BF16), 3)

    inputs = tokens.astype(F32)
    mid = inputs + attn_out
    gain_two = w_a[161:162].astype(F32)
    root_two = lax.rsqrt(jnp.mean(mid * mid, axis=-1, keepdims=True) + EPS)
    normed_two = mid * root_two
    low_two = gather((normed_two * gain_two).astype(BF16), 4)

    gate = dot_nt(low_two, gate_w)
    up = dot_nt(low_two, up_w)
    sigma = jax.nn.sigmoid(gate)
    silu = gate * sigma
    hidden = (silu * up).astype(BF16)
    out_part = dot(hidden, down_w).astype(BF16)
    d_hidden = dot_nt(cot_all, down_w)
    d_gate = (d_hidden * up * sigma * (1.0 + gate * (1.0 - sigma))).astype(BF16)
    d_up = (d_hidden * silu).astype(BF16)
    d_low_part = (dot(d_gate, gate_w) + dot(d_up, up_w)).astype(BF16)
    d_low_two = cube_sum(d_low_part, 5)
    output = (mid + cube_sum(out_part, 6)).astype(BF16)
    grads_b = jnp.concatenate(
        [dot_tn(d_gate, low_two), dot_tn(d_up, low_two), dot_tn(hidden, cot_all)], axis=0
    ).astype(BF16)

    scaled = d_low_two * gain_two
    d_mid = cotangent.astype(F32) + root_two * (
        scaled - normed_two * jnp.mean(scaled * normed_two, axis=-1, keepdims=True)
    )
    d_attn = gather(d_mid.astype(BF16), 7)
    dy = dot_nt(d_attn, out_w).astype(BF16)
    dq, dk, dv = attend_back_call(n, seq_lengths, q, k, v, y, den, state, dy)
    d_low_one = cube_sum(
        (dot(dv, w_a[0:128]) + dot(dq, w_a[128:144]) + dot(dk, w_a[144:160])).astype(BF16), 8
    )
    grads_a = jnp.concatenate(
        [dot_tn(dv, low_one), dot_tn(dq, low_one), dot_tn(dk, low_one), dot_tn(attn_low, d_attn)], axis=0
    ).astype(BF16)
    root_one = lax.rsqrt(jnp.mean(inputs * inputs, axis=-1, keepdims=True) + EPS)
    normed_one = inputs * root_one
    scaled = d_low_one * w_a[160:161].astype(F32)
    grad_tokens = d_mid + root_one * (
        scaled - normed_one * jnp.mean(scaled * normed_one, axis=-1, keepdims=True)
    )

    def arrived(grads, number):
        tiles = back_call(n, grads, number)
        return tiles.reshape(-1, CUBE, *tiles.shape[1:]).astype(F32).sum(axis=0)

    back_b = arrived(grads_b, 9)
    back_a = arrived(grads_a, 10)

    def units(part):
        return part.reshape(CUBE * UNITS, -1)[: w_gate.shape[1]]

    grad_gate = units(back_b[:, :UNITS]).T
    grad_up = units(back_b[:, UNITS : 2 * UNITS]).T
    grad_down = units(back_b[:, 2 * UNITS :])
    grad_value = back_a[:, 0:128].reshape(per * 128, -1).T
    grad_query = back_a[:, 128:144].reshape(per * FEAT, -1).T
    grad_key = back_a[:, 144:160].reshape(per * FEAT, -1).T
    grad_output = back_a[:, 160:288].reshape(per * 128, -1)

    def weighed(*pairs):
        return sum(jnp.sum(w.astype(F32) * g, axis=1) for w, g in pairs)

    gain_one_part = weighed((w_value, grad_value), (w_query, grad_query), (w_key, grad_key))
    gain_two_part = weighed((w_gate, grad_gate), (w_up, grad_up))
    both = lax.psum(jnp.stack([gain_one_part, gain_two_part]), "tensor")
    grad_gain_one = both[0] / gain_attn.astype(F32)
    grad_gain_two = both[1] / gain_mlp.astype(F32)
    return (
        output,
        grad_tokens,
        grad_gain_one,
        grad_query,
        grad_key,
        grad_value,
        grad_output,
        grad_gain_two,
        grad_gate,
        grad_up,
        grad_down,
    )


def solution(mesh):
    return jax.shard_map(
        functools.partial(body, mesh.shape["seq"]),
        mesh=mesh,
        in_specs=(
            P("seq", None),
            P("seq"),
            P("seq", "tensor"),
            P("seq", "tensor"),
            P("seq", "tensor"),
            P("tensor", "seq"),
            P("seq"),
            P("seq", "tensor"),
            P("seq", "tensor"),
            P("tensor", "seq"),
            P(),
            P("seq", None),
        ),
        out_specs=(
            P("seq", None),
            P("seq", None),
            P("seq"),
            P("seq", "tensor"),
            P("seq", "tensor"),
            P("seq", "tensor"),
            P("tensor", "seq"),
            P("seq"),
            P("seq", "tensor"),
            P("seq", "tensor"),
            P("tensor", "seq"),
        ),
        check_vma=False,
    )
```

```python
import functools

import jax
import jax.numpy as jnp
import numpy as np
from jax import lax
from jax.experimental import pallas as pl
from jax.experimental.pallas import tpu as pltpu
from jax.sharding import PartitionSpec as P

MESH = pl.DeviceIdType.MESH
HEADS = 16
FEAT = 16
CUBE = 8
UNITS = 352
EPS = 1e-06
F32 = jnp.float32
BF16 = jnp.bfloat16
ORDERS = ((0, 1, 2), (1, 2, 0), (2, 0, 1))
PIECES = ((0, 48), (48, 48), (96, 32))
MIB = 1 << 20


def flip(place, mask):
    total = 0
    for b in range(3):
        bit = (place // (1 << b)) % 2
        total = total + ((1 - bit) if (mask >> b) & 1 else bit) * (1 << b)
    return total


def subsets(dims):
    out = [0]
    for d in dims:
        out = out + [r | (1 << d) for r in out]
    return out


def whereabouts():
    s = lax.axis_index("seq")
    t = lax.axis_index("tensor")
    j = s % CUBE
    return s, t, j, s - j


def remote(src, dst, send, recv, device):
    return pltpu.make_async_remote_copy(
        src_ref=src, dst_ref=dst, send_sem=send, recv_sem=recv, device_id=device, device_id_type=MESH
    )


def greet(devices):
    barrier = pltpu.get_barrier_semaphore()
    for device in devices:
        pl.semaphore_signal(barrier, inc=1, device_id=device, device_id_type=MESH)
    pl.semaphore_wait(barrier, len(devices))


def near():
    s, t, j, base = whereabouts()
    return [(base + flip(j, 1 << d), t) for d in range(3)] + [(s, 1 - t)]


def greet_all(n):
    s, t, _, _ = whereabouts()
    barrier = pltpu.get_barrier_semaphore()

    def one(k, carry):
        pl.semaphore_signal(barrier, inc=1, device_id=((s + k) % n, t), device_id_type=MESH)
        return carry

    lax.fori_loop(1, n, one, 0)
    pl.semaphore_signal(barrier, inc=1, device_id=(s, 1 - t), device_id_type=MESH)
    pl.semaphore_wait(barrier, n)


class Gather:
    def __init__(self, own, full, sems):
        self.own, self.full = own, full
        self.ssem, self.rsem, self.csend, self.crecv, self.lsem = sems
        self.s, self.t, self.j, self.base = whereabouts()

    def view(self, r, i):
        off, rows = PIECES[i]
        return self.full.at[flip(self.j, r), self.t, pl.ds(off, rows)]

    def other(self, r, i):
        off, rows = PIECES[i]
        return self.full.at[flip(self.j, r), 1 - self.t, pl.ds(off, rows)]

    def hop(self, p, i, r):
        d = ORDERS[i][p]
        off, rows = PIECES[i]
        src = self.own.at[self.t, pl.ds(off, rows)] if r == 0 else self.view(r, i)
        k = r | (1 << d)
        return remote(src, self.view(r, i), self.ssem.at[i, k], self.rsem.at[i, k], (self.base + flip(self.j, 1 << d), self.t))

    def arrival(self, p, i, r):
        d = ORDERS[i][p]
        k = r | (1 << d)
        return remote(self.view(k, i), self.view(k, i), self.ssem.at[i, k], self.rsem.at[i, k], (self.base + flip(self.j, 1 << d), self.t))

    def across(self, r, i, mine):
        ref = self.view(r, i) if mine else self.other(r, i)
        return remote(ref, ref, self.csend.at[i, r], self.crecv.at[i, r], (self.s, 1 - self.t))

    def local(self):
        return pltpu.make_async_copy(self.own, self.full.at[self.j], self.lsem)

    def start(self, p):
        if p == 0:
            self.local().start()
        for i in range(3):
            for r in subsets(ORDERS[i][:p]):
                self.hop(p, i, r).start()

    def arrive(self, p):
        for i in range(3):
            for r in subsets(ORDERS[i][:p]):
                self.arrival(p, i, r).wait_recv()

    def share(self, p):
        for i in range(3):
            for r in subsets(ORDERS[i][:p]):
                self.across(r | (1 << ORDERS[i][p]), i, True).start()

    def finish(self):
        for i in range(3):
            for r in range(1, CUBE):
                self.across(r, i, False).wait_recv()
        for i in range(3):
            for r in range(1, CUBE):
                self.across(r, i, True).wait_send()
        for p in range(3):
            for i in range(3):
                for r in subsets(ORDERS[i][:p]):
                    self.hop(p, i, r).wait_send()
        self.local().wait()

    def run(self):
        for p in range(3):
            self.start(p)
            self.arrive(p)
            self.share(p)
        self.finish()


def gather_sems():
    return [pltpu.SemaphoreType.DMA((3, CUBE))] * 4 + [pltpu.SemaphoreType.DMA]


def gather_kernel(own, full, *sems):
    greet(near())
    Gather(own, full, sems).run()


def gather(x, number):
    rows, width = x.shape
    out = pl.pallas_call(
        gather_kernel,
        out_shape=jax.ShapeDtypeStruct((CUBE, 2, rows // 2, width), x.dtype),
        in_specs=[pl.BlockSpec(memory_space=pl.ANY)],
        out_specs=pl.BlockSpec(memory_space=pl.ANY),
        scratch_shapes=gather_sems(),
        compiler_params=pltpu.CompilerParams(collective_id=number, has_side_effects=True),
    )(x.reshape(2, rows // 2, width))
    return out.reshape(CUBE * rows, width)


SLOT = {0: 0, 1: 4, 2: 6}


def slot_of(p, i, r):
    kept = subsets(ORDERS[i][p + 1 :])
    return SLOT[p] + kept.index(r)


class Sum:
    ORDER = (7, 6, 5, 3, 4, 2, 1, 0)

    def __init__(self, part, heap, total, sems):
        self.part, self.heap, self.total = part, heap, total
        self.csend, self.crecv, self.ssem, self.rsem, self.fsend, self.frecv = sems
        self.s, self.t, self.j, self.base = whereabouts()

    def across(self, r):
        src = self.part.at[flip(self.j, r), 1 - self.t]
        return remote(src, self.heap.at[r], self.csend.at[r], self.crecv.at[r], (self.s, 1 - self.t))

    def hop(self, p, i, r):
        d = ORDERS[i][p]
        off, rows = PIECES[i]
        k = slot_of(p, i, r ^ (1 << d))
        return remote(
            self.part.at[flip(self.j, r), self.t, pl.ds(off, rows)],
            self.heap.at[CUBE + k, pl.ds(off, rows)],
            self.ssem.at[i, k],
            self.rsem.at[i, k],
            (self.base + flip(self.j, 1 << d), self.t),
        )

    def send(self, r):
        self.across(r).start()

    def take(self, r):
        self.across(r).wait_recv()
        jj = flip(self.j, r)
        step = 32

        def one(m, c):
            at = pl.ds(pl.multiple_of(m * step, step), step)
            self.part[jj, self.t, at] = (
                self.part[jj, self.t, at].astype(F32) + self.heap[r, at].astype(F32)
            ).astype(BF16)
            return c

        lax.fori_loop(0, self.part.shape[2] // step, one, 0)
        for i in range(3):
            if r >> ORDERS[i][0] & 1:
                self.hop(0, i, r).start()

    def phase(self, p):
        for i in range(3):
            d = ORDERS[i][p]
            off, rows = PIECES[i]
            for r in reversed(subsets(ORDERS[i][p + 1 :])):
                self.hop(p, i, r | (1 << d)).wait_recv()
                jj = flip(self.j, r)
                k = slot_of(p, i, r)
                for q in range(0, rows, 16):
                    at = pl.ds(off + q, 16)
                    new = self.part[jj, self.t, at].astype(F32) + self.heap[CUBE + k, at].astype(F32)
                    if p == 2:
                        self.total[self.t, at] = new
                    else:
                        self.part[jj, self.t, at] = new.astype(BF16)
                if p < 2 and r >> ORDERS[i][p + 1] & 1:
                    self.hop(p + 1, i, r).start()

    def both(self, half):
        ref = self.total.at[half]
        return remote(ref, ref, self.fsend, self.frecv, (self.s, 1 - self.t))

    def trade(self):
        self.both(self.t).start()

    def finish(self):
        self.both(1 - self.t).wait_recv()
        self.both(self.t).wait_send()
        for r in range(CUBE):
            self.across(r).wait_send()
        for p in range(3):
            for i in range(3):
                d = ORDERS[i][p]
                for r in subsets(ORDERS[i][p + 1 :]):
                    self.hop(p, i, r | (1 << d)).wait_send()

    def run(self):
        for r in self.ORDER:
            self.send(r)
        for r in self.ORDER:
            self.take(r)
        for p in range(3):
            self.phase(p)
        self.trade()
        self.finish()


def sum_sems():
    return [
        pltpu.SemaphoreType.DMA((CUBE,)),
        pltpu.SemaphoreType.DMA((CUBE,)),
        pltpu.SemaphoreType.DMA((3, CUBE)),
        pltpu.SemaphoreType.DMA((3, CUBE)),
        pltpu.SemaphoreType.DMA,
        pltpu.SemaphoreType.DMA,
    ]


def sum_kernel(given, total, part, heap, lsem, *sems):
    greet(near())
    load = pltpu.make_async_copy(given, part, lsem)
    load.start()
    load.wait()
    Sum(part, heap, total, sems).run()


def cube_sum(x, number):
    rows, width = x.shape[0] // CUBE, x.shape[1]
    half = rows // 2
    out = pl.pallas_call(
        sum_kernel,
        out_shape=jax.ShapeDtypeStruct((2, half, width), F32),
        in_specs=[pl.BlockSpec(memory_space=pl.ANY)],
        out_specs=pl.BlockSpec(memory_space=pltpu.VMEM),
        scratch_shapes=[
            pltpu.VMEM((CUBE, 2, half, width), BF16),
            pltpu.VMEM((15, half, width), BF16),
            pltpu.SemaphoreType.DMA,
            *sum_sems(),
        ],
        compiler_params=pltpu.CompilerParams(collective_id=number, has_side_effects=True, vmem_limit_bytes=50 * MIB),
    )(x.reshape(CUBE, 2, half, width))
    return out.reshape(rows, width)


def columns_of(ref, s):
    if len(ref.shape) == 3:
        return ref.at[s]
    return ref.at[:, pl.ds(pl.multiple_of(s * 128, 128), 128)]


def columns_apart(n, rows, width):
    return (rows, width) if width // n % 128 == 0 else (n, rows, width // n)


def together(x):
    return x if x.ndim == 2 else x.transpose(1, 0, 2).reshape(x.shape[1], -1)


def apart(n, x):
    return x if x.shape[1] // n % 128 == 0 else x.reshape(x.shape[0], n, -1).transpose(1, 0, 2)


class Spread:
    def __init__(self, n, pack, full, sems):
        self.n, self.pack, self.full = n, pack, full
        self.ssem, self.rsem, self.lsem = sems
        self.s, self.t, self.j, self.base = whereabouts()

    def columns(self, s):
        return columns_of(self.full, s)

    def copy(self, k):
        to = (self.s + k) % self.n
        return remote(self.pack.at[to % CUBE], self.columns(self.s), self.ssem.at[k], self.rsem.at[k], (to, self.t))

    def arrival(self, k):
        at = (self.s + self.n - k) % self.n
        return remote(self.pack.at[0], self.columns(at), self.ssem.at[k], self.rsem.at[k], (at, self.t))

    def local(self):
        return pltpu.make_async_copy(self.pack.at[self.j], self.columns(self.s), self.lsem)

    def start(self):
        lax.fori_loop(1, self.n, lambda k, c: (self.copy(k).start(), c)[1], 0)
        self.local().start()

    def finish(self):
        self.local().wait()
        lax.fori_loop(1, self.n, lambda k, c: (self.arrival(k).wait_recv(), c)[1], 0)
        lax.fori_loop(1, self.n, lambda k, c: (self.copy(k).wait_send(), c)[1], 0)


class Back:
    def __init__(self, n, grads, tiles, sems):
        self.n, self.grads, self.tiles = n, grads, tiles
        self.ssem, self.rsem, self.lsem = sems
        self.s, self.t, self.j, self.base = whereabouts()

    def columns(self, s):
        return columns_of(self.grads, s)

    def copy(self, k):
        to = (self.s + k) % self.n
        return remote(self.columns(to), self.tiles.at[self.s], self.ssem.at[k], self.rsem.at[k], (to, self.t))

    def arrival(self, k):
        at = (self.s + self.n - k) % self.n
        return remote(self.tiles.at[at], self.tiles.at[at], self.ssem.at[k], self.rsem.at[k], (at, self.t))

    def local(self):
        return pltpu.make_async_copy(self.columns(self.s), self.tiles.at[self.s], self.lsem)

    start = Spread.start
    finish = Spread.finish


def spread_sems(n):
    return [pltpu.SemaphoreType.DMA((n,)), pltpu.SemaphoreType.DMA((n,)), pltpu.SemaphoreType.DMA]


def head_kernel(n, pack_a, pack_b, tokens, cot, w_a, w_b, tokens_all, cot_all, *sems):
    greet_all(n)
    first = Spread(n, pack_a, w_a, sems[0:3])
    second = Spread(n, pack_b, w_b, sems[3:6])
    g_tok = Gather(tokens, tokens_all, sems[6:11])
    g_cot = Gather(cot, cot_all, sems[11:16])
    first.start()
    g_tok.start(0)
    second.start()
    for p in range(3):
        g_tok.arrive(p)
        if p < 2:
            g_tok.start(p + 1)
        else:
            g_cot.start(0)
        g_tok.share(p)
    for p in range(3):
        g_cot.arrive(p)
        if p < 2:
            g_cot.start(p + 1)
        g_cot.share(p)
    g_tok.finish()
    g_cot.finish()
    first.finish()
    second.finish()


def head_call(n, pack_a, pack_b, tokens, cot):
    rows, width = tokens.shape
    shape = (CUBE, 2, rows // 2, width)
    any_space = pl.BlockSpec(memory_space=pl.ANY)
    w_a, w_b, tok, ct = pl.pallas_call(
        functools.partial(head_kernel, n),
        out_shape=[
            jax.ShapeDtypeStruct(columns_apart(n, pack_a.shape[1], width), BF16),
            jax.ShapeDtypeStruct(columns_apart(n, pack_b.shape[1], width), BF16),
            jax.ShapeDtypeStruct(shape, BF16),
            jax.ShapeDtypeStruct(shape, BF16),
        ],
        in_specs=[any_space] * 4,
        out_specs=[any_space] * 4,
        scratch_shapes=[*spread_sems(n), *spread_sems(n), *gather_sems(), *gather_sems()],
        compiler_params=pltpu.CompilerParams(collective_id=0, has_side_effects=True),
    )(pack_a, pack_b, tokens.reshape(2, rows // 2, width), cot.reshape(2, rows // 2, width))
    return together(w_a), together(w_b), tok.reshape(-1, width), ct.reshape(-1, width)


def back_kernel(n, grads, tiles, *sems):
    greet_all(n)
    back = Back(n, grads, tiles, sems)
    back.start()
    back.finish()


def back_call(n, grads, number):
    rows, width = grads.shape
    any_space = pl.BlockSpec(memory_space=pl.ANY)
    return pl.pallas_call(
        functools.partial(back_kernel, n),
        out_shape=jax.ShapeDtypeStruct((n, rows, width // n), BF16),
        in_specs=[any_space],
        out_specs=any_space,
        scratch_shapes=spread_sems(n),
        compiler_params=pltpu.CompilerParams(collective_id=number, has_side_effects=True),
    )(apart(n, grads))


def dot(a, b):
    return jnp.dot(a, b, preferred_element_type=F32)


def dot_nt(a, b):
    return lax.dot_general(a, b, (((1,), (1,)), ((), ())), preferred_element_type=F32)


def dot_tn(a, b):
    return lax.dot_general(a, b, (((0,), (0,)), ((), ())), preferred_element_type=F32)


def spreaders():
    first = np.repeat(np.eye(FEAT), FEAT, axis=1)
    second = np.tile(np.eye(FEAT), (1, FEAT))
    third = np.eye(FEAT, 128)
    return [jnp.asarray(m, BF16) for m in (first, second, third)]


ROOT_HALF = 0.5**0.5


def lift(u, keep, first, second, third):
    quad = dot(u, first) * dot(u, second) * (0.25 * ROOT_HALF) * keep
    lane = lax.broadcasted_iota(jnp.int32, (u.shape[0], 128), 1)
    line = (dot(u, third) * 0.5 + jnp.where(lane == FEAT, 1.0, 0.0)) * keep
    return quad.astype(BF16), line.astype(BF16)


def lift_back(u, d_quad, d_line, first, second):
    one, two = dot(u, first) * 0.5, dot(u, second) * 0.5
    back = dot_nt((d_quad * two).astype(BF16), first) + dot_nt((d_quad * one).astype(BF16), second)
    return back * ROOT_HALF + d_line[:, :FEAT]


def two_terms(x):
    high = x.astype(BF16)
    return high, (x - high.astype(F32)).astype(BF16)


def segments(start_two, start_three, first_position, count, axis):
    shape = (count, 1) if axis == 0 else (1, count)
    position = first_position + lax.broadcasted_iota(jnp.int32, shape, axis)
    return position, (position >= start_two).astype(jnp.int32) + (position >= start_three).astype(jnp.int32)


def pair_mask(two, three, at_t, at_s, block):
    pos_t, seg_t = segments(two, three, at_t, block, 0)
    pos_s, seg_s = segments(two, three, at_s, block, 1)
    return (pos_s <= pos_t) & (seg_s == seg_t)


def other_groups(groups):
    s, t, j, base = whereabouts()
    return [((s + CUBE * k) % (CUBE * groups), t) for k in range(1, groups)]


def exchange(groups, mine, theirs, ssem, rsem, before):
    s, t, j, base = whereabouts()
    c = s // CUBE
    for k, device in enumerate(other_groups(groups)):
        remote(mine, theirs.at[k], ssem.at[k], rsem.at[k], device).start()

    def finish():
        total = jnp.zeros(mine.shape, F32)
        for k, device in enumerate(other_groups(groups)):
            remote(mine, theirs.at[k], ssem.at[k], rsem.at[k], device).wait_recv()
            source = (c + groups - (k + 1)) % groups
            counts = (source < c) if before else (source > c)
            total = total + jnp.where(counts, theirs[k], 0.0)
        for k, device in enumerate(other_groups(groups)):
            remote(mine, theirs.at[k], ssem.at[k], rsem.at[k], device).wait_send()
        return total

    return finish


BLOCK = 256


def attend_kernel(
    groups, lengths, x_ref, w_ref, first, second, third,
    low_ref, q_ref, k_ref, v_ref, y_ref, den_ref, state_ref,
    state_mine, state_theirs, ssem, rsem,
):
    step = pl.program_id(0)
    steps = pl.num_programs(0)
    s, t, j, base = whereabouts()
    rows = x_ref.shape[0]
    two, three = lengths[0], lengths[0] + lengths[1]
    start = base * rows
    here = pl.ds(pl.multiple_of(step * rows, rows), rows)

    @pl.when(step == 0)
    def _():
        greet(other_groups(groups))
        state_mine[...] = jnp.zeros_like(state_mine)

    x = x_ref[...].astype(F32)
    root = lax.rsqrt(jnp.mean(x * x, axis=-1, keepdims=True) + EPS)
    low = (x * root * w_ref[160:161, :].astype(F32)).astype(BF16)
    low_ref[...] = low
    q = dot_nt(low, w_ref[128:144, :]).astype(BF16)
    k = dot_nt(low, w_ref[144:160, :]).astype(BF16)
    v = dot_nt(low, w_ref[0:128, :]).astype(BF16)
    lane = lax.broadcasted_iota(jnp.int32, (rows, 128), 1)
    v_ext = jnp.concatenate([v, jnp.where(lane < 2, 1.0, 0.0).astype(BF16)], axis=1)
    q_ref[here, :] = q
    k_ref[here, :] = k
    v_ref[here, :] = v_ext
    _, seg = segments(two, three, start + step * rows, rows, 0)
    quad, line = lift(k, (seg == 1).astype(F32), first[...], second[...], third[...])
    state_mine[0:256, :] += dot_tn(quad, v_ext)
    state_mine[256:384, :] += dot_tn(line, v_ext)

    @pl.when(step == steps - 1)
    def _():
        done = exchange(groups, state_mine, state_theirs, ssem, rsem, True)
        total = q_ref.shape[0]

        def outer(tb, carry):
            tq = pl.ds(pl.multiple_of(tb * BLOCK, BLOCK), BLOCK)
            qt = q_ref[tq, :]

            def inner(sb, acc):
                sq = pl.ds(pl.multiple_of(sb * BLOCK, BLOCK), BLOCK)
                score = dot_nt(qt, k_ref[sq, :]) * 0.25
                mask = pair_mask(two, three, start + tb * BLOCK, start + sb * BLOCK, BLOCK)
                weight = jnp.where(mask, 1.0 + score + 0.5 * score * score, 0.0).astype(BF16)
                return acc + dot(weight, v_ref[sq, :])

            acc = lax.fori_loop(0, tb + 1, inner, jnp.zeros((BLOCK, 256), F32))
            y_ref[tq, :] = acc[:, :128]
            den_ref[tq, :] = acc[:, 128:]
            return carry

        lax.fori_loop(0, total // BLOCK, outer, 0)
        state = done()
        state_ref[...] = state
        high, lowp = two_terms(state)

        def late(tb, carry):
            tq = pl.ds(pl.multiple_of(tb * BLOCK, BLOCK), BLOCK)
            _, seg = segments(two, three, start + tb * BLOCK, BLOCK, 0)
            quad, line = lift(q_ref[tq, :], (seg == 1).astype(F32), first[...], second[...], third[...])
            more = dot(quad, high[0:256]) + dot(quad, lowp[0:256]) + dot(line, high[256:384]) + dot(line, lowp[256:384])
            num = y_ref[tq, :] + more[:, :128]
            den = den_ref[tq, :] + more[:, 128:]
            den_ref[tq, :] = den
            y_ref[tq, :] = num / den[:, 0:1]
            return carry

        lax.fori_loop(0, total // BLOCK, late, 0)


def attend_call(n, lengths, x_all, w_a):
    groups = n // CUBE
    count, width = x_all.shape
    rows = count // CUBE
    vm = pl.BlockSpec(memory_space=pltpu.VMEM)
    whole = lambda *shape: pl.BlockSpec(shape, lambda i: (0,) * len(shape))
    peers = max(groups - 1, 1)
    return pl.pallas_call(
        functools.partial(attend_kernel, groups),
        grid=(CUBE,),
        out_shape=[
            jax.ShapeDtypeStruct((count, width), BF16),
            jax.ShapeDtypeStruct((count, FEAT), BF16),
            jax.ShapeDtypeStruct((count, FEAT), BF16),
            jax.ShapeDtypeStruct((count, 256), BF16),
            jax.ShapeDtypeStruct((count, 128), F32),
            jax.ShapeDtypeStruct((count, 128), F32),
            jax.ShapeDtypeStruct((384, 256), F32),
        ],
        in_specs=[
            pl.BlockSpec(memory_space=pltpu.SMEM),
            pl.BlockSpec((rows, width), lambda i: (i, 0)),
            whole(*w_a.shape),
            whole(FEAT, 256),
            whole(FEAT, 256),
            whole(FEAT, 128),
        ],
        out_specs=[
            pl.BlockSpec((rows, width), lambda i: (i, 0)),
            whole(count, FEAT),
            whole(count, FEAT),
            whole(count, 256),
            whole(count, 128),
            whole(count, 128),
            whole(384, 256),
        ],
        scratch_shapes=[
            pltpu.VMEM((384, 256), F32),
            pltpu.VMEM((peers, 384, 256), F32),
            pltpu.SemaphoreType.DMA((peers,)),
            pltpu.SemaphoreType.DMA((peers,)),
        ],
        compiler_params=pltpu.CompilerParams(collective_id=1, has_side_effects=True, vmem_limit_bytes=50 * MIB),
    )(lengths, x_all, w_a, *spreaders())


def row_loop(count, step, work):
    def one(m, c):
        work(pl.ds(pl.multiple_of(m * step, step), step))
        return c

    lax.fori_loop(0, count // step, one, 0)


def tail_kernel(
    n, lengths, q_ref, k_ref, v_ref, y_ref, den_ref, state_ref, w_ref, mid_ref, cot_ref, tok_ref,
    dlow_hbm, out_hbm, low_hbm, grads_b, first, second, third,
    output_ref, grad_ref, tiles_b, tiles_a,
    part, heap_a, heap_b, wide, own, total, d_mid, c_ref, dy_ref, da, db, dv, dqkv, grads_a,
    state_mine, state_theirs, xsend, xrecv, lsem, *sems,
):
    groups = n // CUBE
    s, t, j, base = whereabouts()
    tokens = q_ref.shape[0]
    rows = tokens // CUBE
    half = rows // 2
    width = w_ref.shape[1]
    two, three = lengths[0], lengths[0] + lengths[1]
    start = base * rows
    in_kernel = len(tiles_a.shape) == 3
    sum_low, sum_out, sum_one = sems[0:6], sems[6:12], sems[12:18]
    gsems, bsems, asems = sems[18:23], sems[23:26], sems[26:29]

    load = pltpu.make_async_copy(dlow_hbm, part, lsem.at[0])
    load.start()
    greet_all(n)
    load.wait()
    low_sum = Sum(part, heap_a, total, sum_low)
    low_sum.run()
    back_b = Back(n, grads_b, tiles_b, bsems) if in_kernel else None
    if in_kernel:
        back_b.start()
    load_out = pltpu.make_async_copy(out_hbm, part, lsem.at[1])
    load_out.start()

    gain_two = w_ref[161:162, :].astype(F32)
    for h in range(2):

        def norm_back_two(at):
            mid = mid_ref[h, at]
            root = lax.rsqrt(jnp.mean(mid * mid, axis=-1, keepdims=True) + EPS)
            normed = mid * root
            scaled = total[h, at] * gain_two
            grad = cot_ref[h, at].astype(F32) + root * (
                scaled - normed * jnp.mean(scaled * normed, axis=-1, keepdims=True)
            )
            d_mid[h, at] = grad
            own[h, at] = grad.astype(BF16)

        row_loop(half, 16, norm_back_two)

    Gather(own, wide, gsems).run()

    def project(jj, c):
        for h in range(2):
            at = pl.ds(pl.multiple_of(jj * rows + h * half, half), half)
            dy_ref[at, :] = dot_nt(wide[jj, h], w_ref[176:304, :]).astype(BF16)
        return c

    lax.fori_loop(0, CUBE, project, 0)
    load_out.wait()
    out_sum = Sum(part, heap_b, total, sum_out)
    for r in Sum.ORDER:
        out_sum.send(r)

    state_mine[...] = jnp.zeros_like(state_mine)
    db[...] = jnp.zeros_like(db)
    dv[...] = jnp.zeros_like(dv)
    state = state_ref[...].astype(BF16)
    blocks = tokens // BLOCK

    def early(tb, carry):
        tq = pl.ds(pl.multiple_of(tb * BLOCK, BLOCK), BLOCK)
        _, seg = segments(two, three, start + tb * BLOCK, BLOCK, 0)
        keep = (seg == 1).astype(F32)
        c = (dy_ref[tq, :].astype(F32) / den_ref[tq, 0:1]).astype(BF16)
        m = -jnp.sum(c.astype(F32) * y_ref[tq, :], axis=-1, keepdims=True)
        m_high = m.astype(BF16).astype(F32)
        lane = lax.broadcasted_iota(jnp.int32, (BLOCK, 128), 1)
        extra = jnp.where(lane == 0, m_high, jnp.where(lane == 1, m - m_high, 0.0)).astype(BF16)
        c_ext = jnp.concatenate([c, extra], axis=1)
        c_ref[tq, :] = c_ext
        u = q_ref[tq, :]
        quad, line = lift(u, keep, first[...], second[...], third[...])
        state_mine[0:256, :] += dot_tn(quad, c_ext)
        state_mine[256:384, :] += dot_tn(line, c_ext)
        d_quad = dot_nt(c_ext, state[0:256]) * keep
        d_line = dot_nt(c_ext, state[256:384]) * keep
        da[tq, :] = lift_back(u, d_quad, d_line, first[...], second[...])
        return carry

    lax.fori_loop(0, blocks, early, 0)
    done = exchange(groups, state_mine, state_theirs, xsend, xrecv, False)
    for r in Sum.ORDER:
        out_sum.take(r)

    for col in range(0, width, 512):
        acc = jnp.zeros((128, 512), F32)
        for jj in range(CUBE):
            for h in range(2):
                at = pl.ds(jj * rows + h * half, half)
                acc = acc + dot_tn(y_ref[at, :].astype(BF16), wide[jj, h, :, pl.ds(col, 512)])
        grads_a[160:288, col : col + 512] = acc.astype(BF16)
    load_low = pltpu.make_async_copy(low_hbm, wide, lsem.at[2])
    load_low.start()

    def outer(tb, carry):
        tq = pl.ds(pl.multiple_of(tb * BLOCK, BLOCK), BLOCK)
        qt = q_ref[tq, :]
        ct = c_ref[tq, :]

        def inner(sb, acc):
            sq = pl.ds(pl.multiple_of(sb * BLOCK, BLOCK), BLOCK)
            ks = k_ref[sq, :]
            score = dot_nt(qt, ks) * 0.25
            d_w = dot_nt(ct, v_ref[sq, :])
            mask = pair_mask(two, three, start + tb * BLOCK, start + sb * BLOCK, BLOCK)
            weight = jnp.where(mask, 1.0 + score + 0.5 * score * score, 0.0).astype(BF16)
            inner_grad = jnp.where(mask, d_w * (1.0 + score), 0.0).astype(BF16)
            db[sq, :] += dot_tn(inner_grad, qt) * 0.5
            dv[sq, :] += dot_tn(weight, ct)[:, :128]
            return acc + dot(inner_grad, ks)

        acc = lax.fori_loop(0, tb + 1, inner, jnp.zeros((BLOCK, FEAT), F32))
        da[tq, :] = (da[tq, :] + acc * 0.5) * 0.5
        return carry

    cuts = [0, blocks // 2, 3 * blocks // 4, blocks]
    for p in range(3):
        lax.fori_loop(cuts[p], cuts[p + 1], outer, 0)
        out_sum.phase(p)
    out_sum.trade()
    state_back = done().astype(BF16)

    def late(sb, carry):
        sq = pl.ds(pl.multiple_of(sb * BLOCK, BLOCK), BLOCK)
        _, seg = segments(two, three, start + sb * BLOCK, BLOCK, 0)
        keep = (seg == 1).astype(F32)
        u = k_ref[sq, :]
        v = v_ref[sq, :]
        quad, line = lift(u, keep, first[...], second[...], third[...])
        d_quad = dot_nt(v, state_back[0:256]) * keep
        d_line = dot_nt(v, state_back[256:384]) * keep
        more = dot(quad, state_back[0:256]) + dot(line, state_back[256:384])
        dk = (db[sq, :] + lift_back(u, d_quad, d_line, first[...], second[...])) * 0.5
        dqkv[sq, 0:128] = (dv[sq, :] + more[:, :128]).astype(BF16)
        side = dot(da[sq, :].astype(BF16), third[...]) + dot(dk.astype(BF16), third_shifted(third[...]))
        dqkv[sq, 128:256] = side.astype(BF16)
        return carry

    lax.fori_loop(0, blocks, late, 0)
    out_sum.finish()
    for h in range(2):

        def finish_output(at):
            output_ref[h, at] = (mid_ref[h, at] + total[h, at]).astype(BF16)

        row_loop(half, 16, finish_output)

    load_low.wait()
    one_sum = Sum(part, heap_a, total, sum_one)
    w_one = w_ref[0:160, :]
    for idx, r in enumerate(Sum.ORDER):
        jj = flip(j, r)
        for h in range(2):
            at = pl.ds(pl.multiple_of(jj * rows + h * half, half), half)
            part[jj, h] = dot(dqkv[at, 0:160], w_one).astype(BF16)
        one_sum.send(r)
        if idx:
            one_sum.take(Sum.ORDER[idx - 1])
    one_sum.take(Sum.ORDER[-1])
    for col in range(0, width, 512):
        acc = jnp.zeros((256, 512), F32)
        for jj in range(CUBE):
            for h in range(2):
                at = pl.ds(jj * rows + h * half, half)
                acc = acc + dot_tn(dqkv[at, :], wide[jj, h, :, pl.ds(col, 512)])
        grads_a[0:160, col : col + 512] = acc[0:160].astype(BF16)
    if in_kernel:
        back_a = Back(n, grads_a, tiles_a, asems)
        back_a.start()
    else:
        copy = pltpu.make_async_copy(grads_a, tiles_a, lsem.at[3])
        copy.start()
    for p in range(3):
        one_sum.phase(p)
    one_sum.trade()
    one_sum.finish()

    gain_one = w_ref[160:161, :].astype(F32)
    for h in range(2):

        def norm_back_one(at):
            x = tok_ref[h, at].astype(F32)
            root = lax.rsqrt(jnp.mean(x * x, axis=-1, keepdims=True) + EPS)
            normed = x * root
            scaled = total[h, at] * gain_one
            grad_ref[h, at] = d_mid[h, at] + root * (
                scaled - normed * jnp.mean(scaled * normed, axis=-1, keepdims=True)
            )

        row_loop(half, 16, norm_back_one)

    if in_kernel:
        back_b.finish()
        back_a.finish()
    else:
        copy.wait()


def third_shifted(third):
    return jnp.concatenate([jnp.zeros_like(third[:, :FEAT]), third[:, : 128 - FEAT]], axis=1)


def tail_call(n, lengths, q, k, v, y, den, state, w_a, mid, cot, tokens, d_low, out_part, low_one, grads_b):
    groups = n // CUBE
    count, width = low_one.shape
    rows = count // CUBE
    half = rows // 2
    wide_columns = width // n % 128 == 0
    vm = pl.BlockSpec(memory_space=pltpu.VMEM)
    any_space = pl.BlockSpec(memory_space=pl.ANY)
    peers = max(groups - 1, 1)
    cut = lambda x: x.reshape(-1, 2, half, width) if x.shape[0] > rows else x.reshape(2, half, width)
    out_shape = [
        jax.ShapeDtypeStruct((2, half, width), BF16),
        jax.ShapeDtypeStruct((2, half, width), F32),
        jax.ShapeDtypeStruct((n, grads_b.shape[0], width // n) if wide_columns else (8, 128), BF16),
        jax.ShapeDtypeStruct((n, 288, width // n) if wide_columns else (288, width), BF16),
    ]
    output, grad, tiles_b, tiles_a = pl.pallas_call(
        functools.partial(tail_kernel, n),
        out_shape=out_shape,
        in_specs=[pl.BlockSpec(memory_space=pltpu.SMEM)] + [vm] * 10 + [any_space] * 4 + [vm] * 3,
        out_specs=[vm, vm, any_space, any_space],
        scratch_shapes=[
            pltpu.VMEM((CUBE, 2, half, width), BF16),
            pltpu.VMEM((15, half, width), BF16),
            pltpu.VMEM((15, half, width), BF16),
            pltpu.VMEM((CUBE, 2, half, width), BF16),
            pltpu.VMEM((2, half, width), BF16),
            pltpu.VMEM((2, half, width), F32),
            pltpu.VMEM((2, half, width), F32),
            pltpu.VMEM((count, 256), BF16),
            pltpu.VMEM((count, 128), BF16),
            pltpu.VMEM((count, FEAT), F32),
            pltpu.VMEM((count, FEAT), F32),
            pltpu.VMEM((count, 128), F32),
            pltpu.VMEM((count, 256), BF16),
            pltpu.VMEM((288, width), BF16),
            pltpu.VMEM((384, 256), F32),
            pltpu.VMEM((peers, 384, 256), F32),
            pltpu.SemaphoreType.DMA((peers,)),
            pltpu.SemaphoreType.DMA((peers,)),
            pltpu.SemaphoreType.DMA((4,)),
            *sum_sems(),
            *sum_sems(),
            *sum_sems(),
            *gather_sems(),
            *spread_sems(n),
            *spread_sems(n),
        ],
        compiler_params=pltpu.CompilerParams(collective_id=2, has_side_effects=True, vmem_limit_bytes=62 * MIB),
    )(
        lengths, q, k, v, y, den, state, w_a, cut(mid), cut(cot), cut(tokens), cut(d_low), cut(out_part),
        cut(low_one), grads_b, *spreaders(),
    )
    if not wide_columns:
        tiles_b = back_call(n, grads_b, 9)
        tiles_a = back_call(n, tiles_a, 10)
    return output.reshape(rows, width), grad.reshape(rows, width), tiles_b, tiles_a


def units_first(w):
    return jnp.pad(w, ((0, CUBE * UNITS - w.shape[0]), (0, 0))).reshape(CUBE, UNITS, w.shape[1])


def body(
    n, tokens, gain_attn, w_query, w_key, w_value, w_output, gain_mlp, w_gate, w_up, w_down, seq_lengths, cotangent
):
    per = HEADS // lax.axis_size("tensor")
    gains = jnp.concatenate([gain_attn[None], gain_mlp[None], jnp.zeros((14, gain_attn.shape[0]), BF16)], axis=0)
    pack_a = jnp.concatenate(
        [
            w_value.T.reshape(per, 128, -1),
            w_query.T.reshape(per, FEAT, -1),
            w_key.T.reshape(per, FEAT, -1),
            jnp.broadcast_to(gains[None], (per, *gains.shape)),
            w_output.reshape(per, 128, -1),
        ],
        axis=1,
    )
    pack_b = jnp.concatenate([units_first(w_gate.T), units_first(w_up.T), units_first(w_down)], axis=1)
    w_a, w_b, tokens_all, cot_all = head_call(n, pack_a, pack_b, tokens, cotangent)
    gate_w, up_w, down_w = w_b[:UNITS], w_b[UNITS : 2 * UNITS], w_b[2 * UNITS :]
    out_w = w_a[176:304]

    low_one, q, k, v, y, den, state = attend_call(n, seq_lengths, tokens_all, w_a)
    attn_low = y.astype(BF16)
    attn_out = cube_sum(dot(attn_low, out_w).astype(BF16), 3)

    inputs = tokens.astype(F32)
    mid = inputs + attn_out
    gain_two = w_a[161:162].astype(F32)
    root_two = lax.rsqrt(jnp.mean(mid * mid, axis=-1, keepdims=True) + EPS)
    normed_two = mid * root_two
    low_two = gather((normed_two * gain_two).astype(BF16), 4)

    gate = dot_nt(low_two, gate_w)
    up = dot_nt(low_two, up_w)
    sigma = jax.nn.sigmoid(gate)
    silu = gate * sigma
    hidden = (silu * up).astype(BF16)
    out_part = dot(hidden, down_w).astype(BF16)
    d_hidden = dot_nt(cot_all, down_w)
    d_gate = (d_hidden * up * sigma * (1.0 + gate * (1.0 - sigma))).astype(BF16)
    d_up = (d_hidden * silu).astype(BF16)
    d_low_part = (dot(d_gate, gate_w) + dot(d_up, up_w)).astype(BF16)
    grads_b = jnp.concatenate(
        [dot_tn(d_gate, low_two), dot_tn(d_up, low_two), dot_tn(hidden, cot_all)], axis=0
    ).astype(BF16)
    output, grad_tokens, tiles_b, tiles_a = tail_call(
        n, seq_lengths, q, k, v, y, den, state, w_a, mid, cotangent, tokens, d_low_part, out_part, low_one, grads_b
    )

    def arrived(tiles):
        return tiles.reshape(-1, CUBE, *tiles.shape[1:]).astype(F32).sum(axis=0)

    back_b, back_a = arrived(tiles_b), arrived(tiles_a)

    def units(part):
        return part.reshape(CUBE * UNITS, -1)[: w_gate.shape[1]]

    grad_gate = units(back_b[:, :UNITS]).T
    grad_up = units(back_b[:, UNITS : 2 * UNITS]).T
    grad_down = units(back_b[:, 2 * UNITS :])
    grad_value = back_a[:, 0:128].reshape(per * 128, -1).T
    grad_query = back_a[:, 128:144].reshape(per * FEAT, -1).T
    grad_key = back_a[:, 144:160].reshape(per * FEAT, -1).T
    grad_output = back_a[:, 160:288].reshape(per * 128, -1)

    def weighed(*pairs):
        return sum(jnp.sum(w.astype(F32) * g, axis=1) for w, g in pairs)

    gain_one_part = weighed((w_value, grad_value), (w_query, grad_query), (w_key, grad_key))
    gain_two_part = weighed((w_gate, grad_gate), (w_up, grad_up))
    both = lax.psum(jnp.stack([gain_one_part, gain_two_part]), "tensor")
    grad_gain_one = both[0] / gain_attn.astype(F32)
    grad_gain_two = both[1] / gain_mlp.astype(F32)
    return (
        output,
        grad_tokens,
        grad_gain_one,
        grad_query,
        grad_key,
        grad_value,
        grad_output,
        grad_gain_two,
        grad_gate,
        grad_up,
        grad_down,
    )


def solution(mesh):
    return jax.shard_map(
        functools.partial(body, mesh.shape["seq"]),
        mesh=mesh,
        in_specs=(
            P("seq", None),
            P("seq"),
            P("seq", "tensor"),
            P("seq", "tensor"),
            P("seq", "tensor"),
            P("tensor", "seq"),
            P("seq"),
            P("seq", "tensor"),
            P("seq", "tensor"),
            P("tensor", "seq"),
            P(),
            P("seq", None),
        ),
        out_specs=(
            P("seq", None),
            P("seq", None),
            P("seq"),
            P("seq", "tensor"),
            P("seq", "tensor"),
            P("seq", "tensor"),
            P("tensor", "seq"),
            P("seq"),
            P("seq", "tensor"),
            P("seq", "tensor"),
            P("tensor", "seq"),
        ),
        check_vma=False,
    )
```

```python
import functools

import jax
import jax.numpy as jnp
import numpy as np
from jax import lax
from jax.experimental import pallas as pl
from jax.experimental.pallas import tpu as pltpu
from jax.sharding import PartitionSpec as P

MESH = pl.DeviceIdType.MESH
HEADS = 16
FEAT = 16
CUBE = 8
UNITS = 352
EPS = 1e-06
F32 = jnp.float32
BF16 = jnp.bfloat16
ORDERS = ((0, 1, 2), (1, 2, 0), (2, 0, 1))
PIECES = ((0, 48), (48, 48), (96, 32))
UP_FIRST = ((2, 0, 1), (2, 1, 0))
UP_LAST = ((0, 1, 2), (1, 0, 2))
HALVES = ((0, 64), (64, 64))
MIB = 1 << 20


def flip(place, mask):
    total = 0
    for b in range(3):
        bit = (place // (1 << b)) % 2
        total = total + ((1 - bit) if (mask >> b) & 1 else bit) * (1 << b)
    return total


def subsets(dims):
    out = [0]
    for d in dims:
        out = out + [r | (1 << d) for r in out]
    return out


def whereabouts():
    s = lax.axis_index("seq")
    t = lax.axis_index("tensor")
    j = s % CUBE
    return s, t, j, s - j


def remote(src, dst, send, recv, device):
    return pltpu.make_async_remote_copy(
        src_ref=src, dst_ref=dst, send_sem=send, recv_sem=recv, device_id=device, device_id_type=MESH
    )


def greet(devices):
    barrier = pltpu.get_barrier_semaphore()
    for device in devices:
        pl.semaphore_signal(barrier, inc=1, device_id=device, device_id_type=MESH)
    pl.semaphore_wait(barrier, len(devices))


def near():
    s, t, j, base = whereabouts()
    return [(base + flip(j, 1 << d), t) for d in range(3)] + [(s, 1 - t)]


def greet_all(n):
    s, t, _, _ = whereabouts()
    barrier = pltpu.get_barrier_semaphore()

    def one(k, carry):
        pl.semaphore_signal(barrier, inc=1, device_id=((s + k) % n, t), device_id_type=MESH)
        return carry

    lax.fori_loop(1, n, one, 0)
    pl.semaphore_signal(barrier, inc=1, device_id=(s, 1 - t), device_id_type=MESH)
    pl.semaphore_wait(barrier, n)


class Gather:
    def __init__(self, own, full, sems, orders=ORDERS, pieces=PIECES):
        self.own, self.full, self.orders, self.pieces = own, full, orders, pieces
        self.ssem, self.rsem, self.csend, self.crecv, self.lsem = sems
        self.s, self.t, self.j, self.base = whereabouts()

    def view(self, r, i):
        off, rows = self.pieces[i]
        return self.full.at[flip(self.j, r), self.t, pl.ds(off, rows)]

    def other(self, r, i):
        off, rows = self.pieces[i]
        return self.full.at[flip(self.j, r), 1 - self.t, pl.ds(off, rows)]

    def hop(self, p, i, r):
        d = self.orders[i][p]
        off, rows = self.pieces[i]
        src = self.own.at[self.t, pl.ds(off, rows)] if r == 0 else self.view(r, i)
        k = r | (1 << d)
        return remote(src, self.view(r, i), self.ssem.at[i, k], self.rsem.at[i, k], (self.base + flip(self.j, 1 << d), self.t))

    def arrival(self, p, i, r):
        d = self.orders[i][p]
        k = r | (1 << d)
        return remote(self.view(k, i), self.view(k, i), self.ssem.at[i, k], self.rsem.at[i, k], (self.base + flip(self.j, 1 << d), self.t))

    def across(self, r, i, mine):
        ref = self.view(r, i) if mine else self.other(r, i)
        return remote(ref, ref, self.csend.at[i, r], self.crecv.at[i, r], (self.s, 1 - self.t))

    def local(self):
        return pltpu.make_async_copy(self.own, self.full.at[self.j], self.lsem)

    def start(self, p):
        if p == 0:
            self.local().start()
        for i in range(len(self.pieces)):
            for r in subsets(self.orders[i][:p]):
                self.hop(p, i, r).start()

    def arrive(self, p):
        for i in range(len(self.pieces)):
            for r in subsets(self.orders[i][:p]):
                self.arrival(p, i, r).wait_recv()

    def share(self, p):
        for i in range(len(self.pieces)):
            for r in subsets(self.orders[i][:p]):
                self.across(r | (1 << self.orders[i][p]), i, True).start()

    def finish(self):
        for i in range(len(self.pieces)):
            for r in range(1, CUBE):
                self.across(r, i, False).wait_recv()
        for i in range(len(self.pieces)):
            for r in range(1, CUBE):
                self.across(r, i, True).wait_send()
        for p in range(3):
            for i in range(len(self.pieces)):
                for r in subsets(self.orders[i][:p]):
                    self.hop(p, i, r).wait_send()
        self.local().wait()

    def advance(self, p, tick=lambda: None):
        for i in range(len(self.pieces)):
            for r in subsets(self.orders[i][:p]):
                k = r | (1 << self.orders[i][p])
                self.arrival(p, i, r).wait_recv()
                if p < 2:
                    self.hop(p + 1, i, r).start()
                    self.hop(p + 1, i, k).start()
                self.across(k, i, True).start()
                tick()

    def run(self, tick=lambda: None):
        self.start(0)
        for p in range(3):
            self.advance(p, tick)
        self.finish()


def gather_sems():
    return [pltpu.SemaphoreType.DMA((3, CUBE))] * 4 + [pltpu.SemaphoreType.DMA]


SLOT = {0: 0, 1: 4, 2: 6}


def slot_of(order, p, r):
    return SLOT[p] + subsets(order[p + 1 :]).index(r)


class Sum:
    ORDER = (7, 6, 5, 3, 4, 2, 1, 0)

    def __init__(self, part, heap, total, sems, orders=ORDERS, pieces=PIECES):
        self.part, self.heap, self.total = part, heap, total
        self.orders, self.pieces = orders, pieces
        self.csend, self.crecv, self.ssem, self.rsem, self.fsend, self.frecv = sems
        self.s, self.t, self.j, self.base = whereabouts()

    def across(self, r):
        src = self.part.at[flip(self.j, r), 1 - self.t]
        return remote(src, self.heap.at[r], self.csend.at[r], self.crecv.at[r], (self.s, 1 - self.t))

    def hop(self, p, i, r):
        d = self.orders[i][p]
        off, rows = self.pieces[i]
        k = slot_of(self.orders[i], p, r ^ (1 << d))
        return remote(
            self.part.at[flip(self.j, r), self.t, pl.ds(off, rows)],
            self.heap.at[CUBE + k, pl.ds(off, rows)],
            self.ssem.at[i, k],
            self.rsem.at[i, k],
            (self.base + flip(self.j, 1 << d), self.t),
        )

    def send(self, r):
        self.across(r).start()

    def take(self, r):
        self.across(r).wait_recv()
        jj = flip(self.j, r)
        step = 32

        def one(m, c):
            at = pl.ds(pl.multiple_of(m * step, step), step)
            self.part[jj, self.t, at] = (
                self.part[jj, self.t, at].astype(F32) + self.heap[r, at].astype(F32)
            ).astype(BF16)
            return c

        lax.fori_loop(0, self.part.shape[2] // step, one, 0)
        for i in range(len(self.pieces)):
            if r >> self.orders[i][0] & 1:
                self.hop(0, i, r).start()

    def phase(self, p, tick=lambda: None):
        for i in range(len(self.pieces)):
            d = self.orders[i][p]
            off, rows = self.pieces[i]
            for r in reversed(subsets(self.orders[i][p + 1 :])):
                self.hop(p, i, r | (1 << d)).wait_recv()
                jj = flip(self.j, r)
                k = slot_of(self.orders[i], p, r)
                for q in range(0, rows, 16):
                    at = pl.ds(off + q, 16)
                    new = self.part[jj, self.t, at].astype(F32) + self.heap[CUBE + k, at].astype(F32)
                    if p == 2:
                        self.total[self.t, at] = new
                    else:
                        self.part[jj, self.t, at] = new.astype(BF16)
                if p < 2 and r >> self.orders[i][p + 1] & 1:
                    self.hop(p + 1, i, r).start()
                tick()

    def both(self, half):
        ref = self.total.at[half]
        return remote(ref, ref, self.fsend, self.frecv, (self.s, 1 - self.t))

    def trade(self):
        self.both(self.t).start()

    def finish(self):
        self.both(1 - self.t).wait_recv()
        self.both(self.t).wait_send()
        for r in range(CUBE):
            self.across(r).wait_send()
        for p in range(3):
            for i in range(len(self.pieces)):
                d = self.orders[i][p]
                for r in subsets(self.orders[i][p + 1 :]):
                    self.hop(p, i, r | (1 << d)).wait_send()

    def run(self):
        for r in self.ORDER:
            self.send(r)
        for r in self.ORDER:
            self.take(r)
        for p in range(3):
            self.phase(p)
        self.trade()
        self.finish()


def sum_sems():
    return [
        pltpu.SemaphoreType.DMA((CUBE,)),
        pltpu.SemaphoreType.DMA((CUBE,)),
        pltpu.SemaphoreType.DMA((3, CUBE)),
        pltpu.SemaphoreType.DMA((3, CUBE)),
        pltpu.SemaphoreType.DMA,
        pltpu.SemaphoreType.DMA,
    ]


def columns_of(ref, s):
    if len(ref.shape) == 3:
        return ref.at[s]
    return ref.at[:, pl.ds(pl.multiple_of(s * 128, 128), 128)]


def columns_apart(n, rows, width):
    return (rows, width) if width // n % 128 == 0 else (n, rows, width // n)


def together(x):
    return x if x.ndim == 2 else x.transpose(1, 0, 2).reshape(x.shape[1], -1)


def apart(n, x):
    return x if x.shape[1] // n % 128 == 0 else x.reshape(x.shape[0], n, -1).transpose(1, 0, 2)


class Trickle:
    def __init__(self, copies):
        self.copies = list(copies)

    def __call__(self, count=1):
        for _ in range(min(count, len(self.copies))):
            self.copies.pop(0).start()

    def flush(self):
        self(len(self.copies))


def far_and_near(n):
    near, far = list(range(1, n // 2)), list(range(n // 2, n))
    return [k for pair in zip(far, near + [None]) for k in pair if k is not None]


class Spread:
    def __init__(self, n, pack, full, sems):
        self.n, self.pack, self.full = n, pack, full
        self.ssem, self.rsem, self.lsem = sems
        self.s, self.t, self.j, self.base = whereabouts()

    def columns(self, s):
        return columns_of(self.full, s)

    def copy(self, k):
        to = (self.s + k) % self.n
        return remote(self.pack.at[to % CUBE], self.columns(self.s), self.ssem.at[k], self.rsem.at[k], (to, self.t))

    def arrival(self, k):
        at = (self.s + self.n - k) % self.n
        return remote(self.pack.at[0], self.columns(at), self.ssem.at[k], self.rsem.at[k], (at, self.t))

    def local(self):
        return pltpu.make_async_copy(self.pack.at[self.j], self.columns(self.s), self.lsem)

    def start(self):
        lax.fori_loop(1, self.n, lambda k, c: (self.copy(k).start(), c)[1], 0)
        self.local().start()

    def trickle(self):
        return [self.local()] + [self.copy(k) for k in far_and_near(self.n)]

    def finish(self):
        self.local().wait()
        lax.fori_loop(1, self.n, lambda k, c: (self.arrival(k).wait_recv(), c)[1], 0)
        lax.fori_loop(1, self.n, lambda k, c: (self.copy(k).wait_send(), c)[1], 0)


class Back:
    def __init__(self, n, grads, tiles, sems):
        self.n, self.grads, self.tiles = n, grads, tiles
        self.ssem, self.rsem, self.lsem = sems
        self.s, self.t, self.j, self.base = whereabouts()

    def columns(self, s):
        return columns_of(self.grads, s)

    def copy(self, k):
        to = (self.s + k) % self.n
        return remote(self.columns(to), self.tiles.at[self.s], self.ssem.at[k], self.rsem.at[k], (to, self.t))

    def arrival(self, k):
        at = (self.s + self.n - k) % self.n
        return remote(self.tiles.at[at], self.tiles.at[at], self.ssem.at[k], self.rsem.at[k], (at, self.t))

    def local(self):
        return pltpu.make_async_copy(self.columns(self.s), self.tiles.at[self.s], self.lsem)

    start = Spread.start
    trickle = Spread.trickle
    finish = Spread.finish


def spread_sems(n):
    return [pltpu.SemaphoreType.DMA((n,)), pltpu.SemaphoreType.DMA((n,)), pltpu.SemaphoreType.DMA]


def spread_kernel(n, pack, full, *sems):
    greet_all(n)
    spread = Spread(n, pack, full, sems)
    spread.start()
    spread.finish()


def spread_call(n, pack, width, number):
    any_space = pl.BlockSpec(memory_space=pl.ANY)
    full = pl.pallas_call(
        functools.partial(spread_kernel, n),
        out_shape=jax.ShapeDtypeStruct(columns_apart(n, pack.shape[1], width), BF16),
        in_specs=[any_space],
        out_specs=any_space,
        scratch_shapes=spread_sems(n),
        compiler_params=pltpu.CompilerParams(collective_id=number, has_side_effects=True),
    )(pack)
    return together(full)


def back_kernel(n, grads, tiles, *sems):
    greet_all(n)
    back = Back(n, grads, tiles, sems)
    back.start()
    back.finish()


def back_call(n, grads, number):
    rows, width = grads.shape
    any_space = pl.BlockSpec(memory_space=pl.ANY)
    return pl.pallas_call(
        functools.partial(back_kernel, n),
        out_shape=jax.ShapeDtypeStruct((n, rows, width // n), BF16),
        in_specs=[any_space],
        out_specs=any_space,
        scratch_shapes=spread_sems(n),
        compiler_params=pltpu.CompilerParams(collective_id=number, has_side_effects=True),
    )(apart(n, grads))


def dot(a, b):
    return jnp.dot(a, b, preferred_element_type=F32)


def dot_nt(a, b):
    return lax.dot_general(a, b, (((1,), (1,)), ((), ())), preferred_element_type=F32)


def dot_tn(a, b):
    return lax.dot_general(a, b, (((0,), (0,)), ((), ())), preferred_element_type=F32)


def spreaders():
    first = np.repeat(np.eye(FEAT), FEAT, axis=1)
    second = np.tile(np.eye(FEAT), (1, FEAT))
    third = np.eye(FEAT, 128)
    return [jnp.asarray(m, BF16) for m in (first, second, third)]


ROOT_HALF = 0.5**0.5


def lift(u, keep, first, second, third):
    quad = dot(u, first) * dot(u, second) * (0.25 * ROOT_HALF) * keep
    lane = lax.broadcasted_iota(jnp.int32, (u.shape[0], 128), 1)
    line = (dot(u, third) * 0.5 + jnp.where(lane == FEAT, 1.0, 0.0)) * keep
    return quad.astype(BF16), line.astype(BF16)


def lift_back(u, d_quad, d_line, first, second):
    one, two = dot(u, first) * 0.5, dot(u, second) * 0.5
    back = dot_nt((d_quad * two).astype(BF16), first) + dot_nt((d_quad * one).astype(BF16), second)
    return back * ROOT_HALF + d_line[:, :FEAT]


def two_terms(x):
    high = x.astype(BF16)
    return high, (x - high.astype(F32)).astype(BF16)


def segments(start_two, start_three, first_position, count, axis):
    shape = (count, 1) if axis == 0 else (1, count)
    position = first_position + lax.broadcasted_iota(jnp.int32, shape, axis)
    return position, (position >= start_two).astype(jnp.int32) + (position >= start_three).astype(jnp.int32)


def pair_mask(two, three, at_t, at_s, block):
    pos_t, seg_t = segments(two, three, at_t, block, 0)
    pos_s, seg_s = segments(two, three, at_s, block, 1)
    return (pos_s <= pos_t) & (seg_s == seg_t)


def pair_mask_turned(two, three, at_s, at_t, block):
    pos_s, seg_s = segments(two, three, at_s, block, 0)
    pos_t, seg_t = segments(two, three, at_t, block, 1)
    return (pos_s <= pos_t) & (seg_s == seg_t)


def other_groups(groups):
    s, t, j, base = whereabouts()
    return [((s + CUBE * k) % (CUBE * groups), t) for k in range(1, groups)]


def exchange(groups, mine, theirs, ssem, rsem, before):
    s, t, j, base = whereabouts()
    c = s // CUBE
    for k, device in enumerate(other_groups(groups)):
        remote(mine, theirs.at[k], ssem.at[k], rsem.at[k], device).start()

    def finish():
        total = jnp.zeros(mine.shape, F32)
        for k, device in enumerate(other_groups(groups)):
            remote(mine, theirs.at[k], ssem.at[k], rsem.at[k], device).wait_recv()
            source = (c + groups - (k + 1)) % groups
            counts = (source < c) if before else (source > c)
            total = total + jnp.where(counts, theirs[k], 0.0)
        for k, device in enumerate(other_groups(groups)):
            remote(mine, theirs.at[k], ssem.at[k], rsem.at[k], device).wait_send()
        return total

    return finish


BLOCK = 256


def row_loop(count, step, work):
    def one(m, c):
        work(pl.ds(pl.multiple_of(m * step, step), step))
        return c

    lax.fori_loop(0, count // step, one, 0)


def pair_weight(score):
    return (score * 0.5 + 1.0) * score + 1.0


def head_kernel(
    n, lengths, tok_ref, pack_a, pack_b, cot_hbm, first, second, third,
    w_ref, w_b, cot_all, low_hbm, own, mid_ref, q_ref, k_ref, v_ref, y_ref, y_turned, den_ref, state_ref,
    wide, part, heap, total, kept, state_mine, state_theirs, xsend, xrecv, lsem, *sems,
):
    groups = n // CUBE
    s, t, j, base = whereabouts()
    half, width = tok_ref.shape[1:]
    rows = 2 * half
    tokens = CUBE * rows
    two, three = lengths[0], lengths[0] + lengths[1]
    start = base * rows
    in_kernel = len(pack_a.shape) == 3
    sum_sem, tok_sem, cot_sem, a_sem, b_sem = sems[0:6], sems[6:11], sems[11:16], sems[16:19], sems[19:22]

    greet_all(n)
    g_tok = Gather(tok_ref, wide, tok_sem)
    g_cot = Gather(cot_hbm, cot_all, cot_sem, UP_FIRST, HALVES)
    if in_kernel:
        spread_a = Spread(n, pack_a, w_ref, a_sem)
        spread_b = Spread(n, pack_b, w_b, b_sem)
        spread_a.start()
        tick = Trickle(spread_b.trickle())
    else:
        copy_a = pltpu.make_async_copy(pack_a, w_ref, lsem.at[CUBE])
        copy_b = pltpu.make_async_copy(pack_b, w_b, lsem.at[CUBE + 1])
        copy_a.start()
        tick = Trickle([copy_b])
    g_tok.start(0)
    for p in range(3):
        g_tok.advance(p)
    tick.flush()
    g_cot.start(0)
    g_tok.finish()
    if in_kernel:
        spread_a.finish()
    else:
        copy_a.wait()

    state_mine[...] = jnp.zeros_like(state_mine)
    gain_one = w_ref[160:161, :].astype(F32)

    def project(jj, c):
        for h in range(2):

            def norm(at):
                x = wide[jj, h, at].astype(F32)
                root = lax.rsqrt(jnp.mean(x * x, axis=-1, keepdims=True) + EPS)
                wide[jj, h, at] = (x * root * gain_one).astype(BF16)

            row_loop(half, 16, norm)
            low = wide[jj, h]
            at = pl.ds(pl.multiple_of(jj * rows + h * half, half), half)
            k = dot_nt(low, w_ref[144:160, :]).astype(BF16)
            v = dot_nt(low, w_ref[0:128, :]).astype(BF16)
            lane = lax.broadcasted_iota(jnp.int32, (half, 128), 1)
            v_ext = jnp.concatenate([v, jnp.where(lane < 2, 1.0, 0.0).astype(BF16)], axis=1)
            q_ref[at, :] = dot_nt(low, w_ref[128:144, :]).astype(BF16)
            k_ref[at, :] = k
            v_ref[at, :] = v_ext
            _, seg = segments(two, three, start + jj * rows + h * half, half, 0)
            keep = (seg == 1).astype(F32)
            kept[at, :] = v_ext * keep.astype(BF16)
            quad, line = lift(k, keep, first[...], second[...], third[...])
            state_mine[0:256, :] += dot_tn(quad, v_ext)
            state_mine[256:384, :] += dot_tn(line, v_ext)
        return c

    lax.fori_loop(0, CUBE, project, 0)
    save = pltpu.make_async_copy(wide, low_hbm, lsem.at[0])
    save.start()
    done = exchange(groups, state_mine, state_theirs, xsend, xrecv, True)
    g_cot.advance(0)

    blocks = tokens // BLOCK
    for tb in range(blocks):
        tq = pl.ds(tb * BLOCK, BLOCK)
        qt = q_ref[tq, :] * BF16(0.25)
        score = dot_nt(qt, k_ref[tq, :])
        mask = pair_mask(two, three, start + tb * BLOCK, start + tb * BLOCK, BLOCK)
        acc = dot(jnp.where(mask, pair_weight(score), 0.0).astype(BF16), v_ref[tq, :])
        if tb:
            _, seg = segments(two, three, start + tb * BLOCK, BLOCK, 0)
            far = jnp.zeros((BLOCK, 256), F32)
            for lo in range(0, tb * BLOCK, 512):
                sq = pl.ds(lo, min(512, tb * BLOCK - lo))
                far = far + dot(pair_weight(dot_nt(qt, k_ref[sq, :])).astype(BF16), kept[sq, :])
            acc = acc + far * (seg == 1).astype(F32)
        y_ref[tq, :] = acc[:, :128]
        den_ref[tq, :] = acc[:, 128:]

    g_cot.advance(1)
    state = done()
    state_ref[...] = state
    high, lowp = two_terms(state)
    out_sum = Sum(part, heap, total, sum_sem)
    out_w = w_ref[176:304, :]

    for idx, r in enumerate(Sum.ORDER):
        jj = flip(j, r)
        tq = pl.ds(pl.multiple_of(jj * rows, rows), rows)
        _, seg = segments(two, three, start + jj * rows, rows, 0)
        quad, line = lift(q_ref[tq, :], (seg == 1).astype(F32), first[...], second[...], third[...])
        more = dot(quad, high[0:256]) + dot(quad, lowp[0:256]) + dot(line, high[256:384]) + dot(line, lowp[256:384])
        den = den_ref[tq, :] + more[:, 128:]
        den_ref[tq, :] = den
        y = (y_ref[tq, :] + more[:, :128]) / den[:, 0:1]
        y_ref[tq, :] = y
        y_low = y.astype(BF16)
        y_turned[:, tq] = y_low.T
        for h in range(2):
            part[jj, h] = dot(y_low[h * half : (h + 1) * half], out_w).astype(BF16)
        out_sum.send(r)
        if idx:
            out_sum.take(Sum.ORDER[idx - 1])
    out_sum.take(Sum.ORDER[-1])
    for p in range(3):
        out_sum.phase(p)
    out_sum.trade()
    out_sum.finish()

    gain_two = w_ref[161:162, :].astype(F32)
    for h in range(2):

        def second_norm(at):
            mid = tok_ref[h, at].astype(F32) + total[h, at]
            mid_ref[h, at] = mid
            root = lax.rsqrt(jnp.mean(mid * mid, axis=-1, keepdims=True) + EPS)
            own[h, at] = (mid * root * gain_two).astype(BF16)

        row_loop(half, 16, second_norm)

    g_cot.advance(2)
    g_cot.finish()
    save.wait()
    if in_kernel:
        spread_b.finish()
    else:
        copy_b.wait()


def head_call(n, lengths, pack_a, pack_b, tokens, cot):
    groups = n // CUBE
    rows, width = tokens.shape
    half = rows // 2
    count = CUBE * rows
    vm = pl.BlockSpec(memory_space=pltpu.VMEM)
    any_space = pl.BlockSpec(memory_space=pl.ANY)
    peers = max(groups - 1, 1)
    w_rows = (pack_a.shape[1], pack_b.shape[1])
    if width // n % 128:
        pack_a, pack_b = spread_call(n, pack_a, width, 4), spread_call(n, pack_b, width, 5)
    shape = (CUBE, 2, half, width)
    return pl.pallas_call(
        functools.partial(head_kernel, n),
        out_shape=[
            jax.ShapeDtypeStruct((w_rows[0], width), BF16),
            jax.ShapeDtypeStruct((w_rows[1], width), BF16),
            jax.ShapeDtypeStruct(shape, BF16),
            jax.ShapeDtypeStruct(shape, BF16),
            jax.ShapeDtypeStruct((2, half, width), BF16),
            jax.ShapeDtypeStruct((2, half, width), F32),
            jax.ShapeDtypeStruct((count, FEAT), BF16),
            jax.ShapeDtypeStruct((count, FEAT), BF16),
            jax.ShapeDtypeStruct((count, 256), BF16),
            jax.ShapeDtypeStruct((count, 128), F32),
            jax.ShapeDtypeStruct((128, count), BF16),
            jax.ShapeDtypeStruct((count, 128), F32),
            jax.ShapeDtypeStruct((384, 256), F32),
        ],
        in_specs=[pl.BlockSpec(memory_space=pltpu.SMEM), vm, any_space, any_space, any_space, vm, vm, vm],
        out_specs=[vm, any_space, any_space, any_space] + [vm] * 9,
        scratch_shapes=[
            pltpu.VMEM(shape, BF16),
            pltpu.VMEM(shape, BF16),
            pltpu.VMEM((15, half, width), BF16),
            pltpu.VMEM((2, half, width), F32),
            pltpu.VMEM((count, 256), BF16),
            pltpu.VMEM((384, 256), F32),
            pltpu.VMEM((peers, 384, 256), F32),
            pltpu.SemaphoreType.DMA((peers,)),
            pltpu.SemaphoreType.DMA((peers,)),
            pltpu.SemaphoreType.DMA((CUBE + 2,)),
            *sum_sems(),
            *gather_sems(),
            *gather_sems(),
            *spread_sems(n),
            *spread_sems(n),
        ],
        compiler_params=pltpu.CompilerParams(collective_id=1, has_side_effects=True, vmem_limit_bytes=62 * MIB),
    )(lengths, tokens.reshape(2, half, width), pack_a, pack_b, cot.reshape(2, half, width), *spreaders())


def mlp_kernel(
    n, own, w_ref, y_turned, mid_hbm, w_hbm, pack_d, cot_hbm,
    hidden, down, grads_b, tiles_d, grads_o, d_mid, dy_ref,
    wide, wide_g, part, heap, total, w_gu, by_gate, by_up, d_gate, d_up, grads_d, lsem, *sems,
):
    s, t, j, base = whereabouts()
    half, width = own.shape[1:]
    rows = 2 * half
    in_kernel = len(pack_d.shape) == 3
    two_sem, attn_sem, low_sem, d_sem, back_sem = sems[0:5], sems[5:10], sems[10:16], sems[16:19], sems[19:22]

    load_w = pltpu.make_async_copy(w_hbm, w_gu, lsem.at[0])
    load_mid = pltpu.make_async_copy(mid_hbm, d_mid, lsem.at[1])
    load_w.start()
    load_mid.start()
    greet_all(n)
    load_cot = pltpu.make_async_copy(cot_hbm, wide_g, lsem.at[6])
    load_cot.start()
    g_two = Gather(own, wide, two_sem)
    g_two.start(0)
    if in_kernel:
        spread_d = Spread(n, pack_d, down, d_sem)
        tick = Trickle(spread_d.trickle())
    else:
        copy_d = pltpu.make_async_copy(pack_d, down, lsem.at[2])
        tick = Trickle([copy_d])
    for p in range(3):
        g_two.advance(p, tick)
    tick.flush()
    g_two.finish()
    load_w.wait()

    def forward(jj, c):
        at = pl.ds(pl.multiple_of(jj * rows, rows), rows)
        low = wide[jj].reshape(rows, width)
        gate = dot_nt(w_gu[0:UNITS, :], low)
        up = dot_nt(w_gu[UNITS:, :], low)
        sigma = jax.nn.sigmoid(gate)
        silu = gate * sigma
        hidden[:, at] = (silu * up).astype(BF16)
        by_gate[:, at] = (up * sigma * (1.0 + gate * (1.0 - sigma))).astype(BF16)
        by_up[:, at] = silu.astype(BF16)
        return c

    lax.fori_loop(0, CUBE, forward, 0)
    load_cot.wait()
    if in_kernel:
        spread_d.finish()
    else:
        copy_d.wait()

    low_sum = Sum(part, heap, total, low_sem)
    for idx, r in enumerate(Sum.ORDER):
        jj = flip(j, r)
        at = pl.ds(pl.multiple_of(jj * rows, rows), rows)
        grad = dot_nt(down[...], wide_g[jj].reshape(rows, width))
        dg = (grad * by_gate[:, at].astype(F32)).astype(BF16)
        du = (grad * by_up[:, at].astype(F32)).astype(BF16)
        d_gate[:, at] = dg
        d_up[:, at] = du
        for col in range(0, width, 512):
            cols = pl.ds(col, 512)
            block = dot_tn(dg, w_gu[0:UNITS, cols]) + dot_tn(du, w_gu[UNITS:, cols])
            part[jj, :, :, cols] = block.astype(BF16).reshape(2, half, 512)
        low_sum.send(r)
        if idx:
            low_sum.take(Sum.ORDER[idx - 1])
    low_sum.take(Sum.ORDER[-1])

    def weight_grad(left, right, out, first_row):
        def one(m, c):
            cols = pl.ds(pl.multiple_of(m * 256, 256), 256)
            block = dot(left[...], right[:, :, :, cols].reshape(CUBE * rows, 256))
            out[first_row : first_row + UNITS, cols] = block.astype(BF16)
            return c

        lax.fori_loop(0, width // 256, one, 0)

    weight_grad(hidden, wide_g, grads_d, 0)
    low_sum.phase(0)
    weight_grad(d_gate, wide, w_gu, 0)
    low_sum.phase(1)
    weight_grad(d_up, wide, w_gu, UNITS)
    save_gu = pltpu.make_async_copy(w_gu, grads_b, lsem.at[3])
    save_gu.start()
    if in_kernel:
        back_d = Back(n, grads_d, tiles_d, back_sem)
        tick = Trickle(back_d.trickle())
    else:
        save_d = pltpu.make_async_copy(grads_d, tiles_d, lsem.at[4])
        tick = Trickle([save_d])
    low_sum.phase(2)
    low_sum.trade()
    low_sum.finish()
    load_mid.wait()

    gain_two = w_ref[161:162, :].astype(F32)
    for h in range(2):

        def norm_back_two(at):
            mid = d_mid[h, at]
            root = lax.rsqrt(jnp.mean(mid * mid, axis=-1, keepdims=True) + EPS)
            normed = mid * root
            scaled = total[h, at] * gain_two
            grad = wide_g[j, h, at].astype(F32) + root * (
                scaled - normed * jnp.mean(scaled * normed, axis=-1, keepdims=True)
            )
            d_mid[h, at] = grad
            own[h, at] = grad.astype(BF16)

        row_loop(half, 16, norm_back_two)

    Gather(own, wide_g, attn_sem).run(tick)
    tick.flush()

    def project(jj, c):
        at = pl.ds(pl.multiple_of(jj * rows, rows), rows)
        dy_ref[at, :] = dot_nt(wide_g[jj].reshape(rows, width), w_ref[176:304, :]).astype(BF16)
        return c

    lax.fori_loop(0, CUBE, project, 0)

    def output_grad(m, c):
        cols = pl.ds(pl.multiple_of(m * 256, 256), 256)
        block = dot(y_turned[...], wide_g[:, :, :, cols].reshape(CUBE * rows, 256))
        grads_o[:, cols] = block.astype(BF16)
        return c

    lax.fori_loop(0, width // 256, output_grad, 0)
    save_gu.wait()
    if in_kernel:
        back_d.finish()
    else:
        save_d.wait()


def mlp_call(n, own, w_a, y_turned, mid, w_gu, pack_d, cot_all):
    half, width = own.shape[1:]
    count = CUBE * 2 * half
    vm = pl.BlockSpec(memory_space=pltpu.VMEM)
    any_space = pl.BlockSpec(memory_space=pl.ANY)
    if width // n % 128:
        pack_d = spread_call(n, pack_d, width, 6)
    shape = (CUBE, 2, half, width)
    return pl.pallas_call(
        functools.partial(mlp_with_own, n),
        out_shape=[
            jax.ShapeDtypeStruct((UNITS, count), BF16),
            jax.ShapeDtypeStruct((UNITS, width), BF16),
            jax.ShapeDtypeStruct((2 * UNITS, width), BF16),
            jax.ShapeDtypeStruct((UNITS, width) if width // n % 128 else (n, UNITS, width // n), BF16),
            jax.ShapeDtypeStruct((128, width), BF16),
            jax.ShapeDtypeStruct((2, half, width), F32),
            jax.ShapeDtypeStruct((count, 128), BF16),
        ],
        in_specs=[any_space, vm, vm] + [any_space] * 4,
        out_specs=[vm, vm, any_space, any_space, vm, vm, vm],
        scratch_shapes=[
            pltpu.VMEM((2, half, width), BF16),
            pltpu.VMEM(shape, BF16),
            pltpu.VMEM(shape, BF16),
            pltpu.VMEM(shape, BF16),
            pltpu.VMEM((15, half, width), BF16),
            pltpu.VMEM((2, half, width), F32),
            pltpu.VMEM((2 * UNITS, width), BF16),
            pltpu.VMEM((UNITS, count), BF16),
            pltpu.VMEM((UNITS, count), BF16),
            pltpu.VMEM((UNITS, count), BF16),
            pltpu.VMEM((UNITS, count), BF16),
            pltpu.VMEM((UNITS, width), BF16),
            pltpu.SemaphoreType.DMA((7,)),
            *gather_sems(),
            *gather_sems(),
            *sum_sems(),
            *spread_sems(n),
            *spread_sems(n),
        ],
        compiler_params=pltpu.CompilerParams(collective_id=3, has_side_effects=True, vmem_limit_bytes=63 * MIB),
    )(own, w_a, y_turned, mid, w_gu, pack_d, cot_all)


def mlp_with_own(n, own_hbm, w_ref, y_turned, mid_hbm, w_hbm, pack_d, cot_hbm, *rest):
    outs, (own, *scratch) = rest[:7], rest[7:]
    lsem = scratch[11]
    load = pltpu.make_async_copy(own_hbm, own, lsem.at[5])
    load.start()
    load.wait()
    mlp_kernel(n, own, w_ref, y_turned, mid_hbm, w_hbm, pack_d, cot_hbm, *outs, *scratch)


def tail_kernel(
    n, lengths, q_ref, k_ref, v_ref, y_ref, den_ref, state_ref, w_ref, tok_ref, dy_ref, hidden, down,
    grads_o, mid, d_mid, low_hbm, grads_b, first, second, third,
    output_ref, grad_ref, tiles_b, tiles_a,
    part, heap_a, heap_b, wide, total, c_ref, c_kept, v_kept, side, dv, turned, dqkv, grads_a,
    state_mine, state_theirs, xsend, xrecv, lsem, *sems,
):
    groups = n // CUBE
    s, t, j, base = whereabouts()
    tokens = q_ref.shape[0]
    rows = tokens // CUBE
    half = rows // 2
    width = w_ref.shape[1]
    two, three = lengths[0], lengths[0] + lengths[1]
    start = base * rows
    in_kernel = len(tiles_a.shape) == 3
    sum_out, sum_one, bsems, asems = sems[0:6], sems[6:12], sems[12:15], sems[15:18]

    load_low = pltpu.make_async_copy(low_hbm, wide, lsem.at[2])
    load_low.start()
    load_mid = pltpu.make_async_copy(mid, grad_ref, lsem.at[0])
    load_mid.start()
    greet_all(n)
    out_sum = Sum(part, heap_b, total, sum_out, UP_LAST, HALVES)
    back_b = Back(n, grads_b, tiles_b, bsems) if in_kernel else None

    tick = Trickle(back_b.trickle()) if in_kernel else Trickle([])

    state_mine[...] = jnp.zeros_like(state_mine)
    state = state_ref[...].astype(BF16)
    blocks = tokens // BLOCK

    def early(tb, carry):
        tq = pl.ds(pl.multiple_of(tb * BLOCK, BLOCK), BLOCK)
        _, seg = segments(two, three, start + tb * BLOCK, BLOCK, 0)
        keep = (seg == 1).astype(F32)
        c = (dy_ref[tq, :].astype(F32) / den_ref[tq, 0:1]).astype(BF16)
        m = -jnp.sum(c.astype(F32) * y_ref[tq, :], axis=-1, keepdims=True)
        m_high = m.astype(BF16).astype(F32)
        lane = lax.broadcasted_iota(jnp.int32, (BLOCK, 128), 1)
        extra = jnp.where(lane == 0, m_high, jnp.where(lane == 1, m - m_high, 0.0)).astype(BF16)
        c_ext = jnp.concatenate([c, extra], axis=1)
        c_ref[tq, :] = c_ext
        c_kept[tq, :] = c_ext * keep.astype(BF16)
        v_kept[tq, :] = v_ref[tq, :] * keep.astype(BF16)
        u = q_ref[tq, :]
        quad, line = lift(u, keep, first[...], second[...], third[...])
        state_mine[0:256, :] += dot_tn(quad, c_ext)
        state_mine[256:384, :] += dot_tn(line, c_ext)
        d_quad = dot_nt(c_ext, state[0:256]) * keep
        d_line = dot_nt(c_ext, state[256:384]) * keep
        side[tq, 0:FEAT] = lift_back(u, d_quad, d_line, first[...], second[...])
        return carry

    tick(4)
    lax.fori_loop(0, blocks, early, 0)
    done = exchange(groups, state_mine, state_theirs, xsend, xrecv, False)
    for r in Sum.ORDER:
        jj = flip(j, r)
        at = pl.ds(pl.multiple_of(jj * rows, rows), rows)
        for col in range(0, width, 512):
            cols = pl.ds(col, 512)
            part[jj, :, :, cols] = dot_tn(hidden[:, at], down[:, cols]).astype(BF16).reshape(2, half, 512)
        out_sum.send(r)
    for r in Sum.ORDER:
        out_sum.take(r)

    for tb in range(blocks):
        tq = pl.ds(tb * BLOCK, BLOCK)
        qt = q_ref[tq, :] * BF16(0.25)
        score = dot_nt(qt, k_ref[tq, :])
        mask = pair_mask(two, three, start + tb * BLOCK, start + tb * BLOCK, BLOCK)
        grad = jnp.where(mask, dot_nt(c_ref[tq, :], v_ref[tq, :]) * (1.0 + score), 0.0).astype(BF16)
        acc = dot(grad, k_ref[tq, :])
        for lo in range(0, tb * BLOCK, 512):
            sq = pl.ds(lo, min(512, tb * BLOCK - lo))
            score = dot_nt(qt, k_ref[sq, :])
            grad = (dot_nt(c_kept[tq, :], v_kept[sq, :]) * (1.0 + score)).astype(BF16)
            acc = acc + dot(grad, k_ref[sq, :])
        side[tq, 0:FEAT] = (side[tq, 0:FEAT] + acc * 0.5) * 0.5
        tick()
    out_sum.phase(0)
    for sb in range(blocks):
        sq = pl.ds(sb * BLOCK, BLOCK)
        ks = k_ref[sq, :] * BF16(0.25)
        score = dot_nt(ks, q_ref[sq, :])
        mask = pair_mask_turned(two, three, start + sb * BLOCK, start + sb * BLOCK, BLOCK)
        grad = jnp.where(mask, dot_nt(v_ref[sq, :], c_ref[sq, :]) * (1.0 + score), 0.0).astype(BF16)
        weight = jnp.where(mask, pair_weight(score), 0.0).astype(BF16)
        acc = dot(grad, q_ref[sq, :])
        near = dot(weight, c_ref[sq, :])
        far = jnp.zeros((BLOCK, 256), F32)
        for lo in range((sb + 1) * BLOCK, tokens, 512):
            tq = pl.ds(lo, min(512, tokens - lo))
            score = dot_nt(ks, q_ref[tq, :])
            grad = (dot_nt(v_kept[sq, :], c_kept[tq, :]) * (1.0 + score)).astype(BF16)
            acc = acc + dot(grad, q_ref[tq, :])
            far = far + dot(pair_weight(score).astype(BF16), c_kept[tq, :])
        _, seg = segments(two, three, start + sb * BLOCK, BLOCK, 0)
        side[sq, FEAT : 2 * FEAT] = acc * 0.5
        dv[sq, :] = (near + far * (seg == 1).astype(F32))[:, :128]
        tick()
        if sb == blocks // 2:
            out_sum.phase(1)
    tick.flush()
    out_sum.phase(2)
    out_sum.trade()
    state_back = done().astype(BF16)

    def late(sb, carry):
        sq = pl.ds(pl.multiple_of(sb * BLOCK, BLOCK), BLOCK)
        _, seg = segments(two, three, start + sb * BLOCK, BLOCK, 0)
        keep = (seg == 1).astype(F32)
        u = k_ref[sq, :]
        v = v_ref[sq, :]
        quad, line = lift(u, keep, first[...], second[...], third[...])
        d_quad = dot_nt(v, state_back[0:256]) * keep
        d_line = dot_nt(v, state_back[256:384]) * keep
        more = dot(quad, state_back[0:256]) + dot(line, state_back[256:384])
        dk = (side[sq, FEAT : 2 * FEAT] + lift_back(u, d_quad, d_line, first[...], second[...])) * 0.5
        dqkv[sq, 0:128] = (dv[sq, :] + more[:, :128]).astype(BF16)
        packed = dot(side[sq, 0:FEAT].astype(BF16), third[...]) + dot(dk.astype(BF16), third_shifted(third[...]))
        dqkv[sq, 128:256] = packed.astype(BF16)
        turned[:, sq] = dqkv[sq, :].T
        return carry

    lax.fori_loop(0, blocks, late, 0)
    out_sum.finish()
    load_mid.wait()
    for h in range(2):

        def finish_output(at):
            output_ref[h, at] = (grad_ref[h, at] + total[h, at]).astype(BF16)

        row_loop(half, 16, finish_output)
    load_mid = pltpu.make_async_copy(d_mid, grad_ref, lsem.at[1])
    load_mid.start()

    load_low.wait()
    one_sum = Sum(part, heap_a, total, sum_one)
    w_one = w_ref[0:160, :]
    for idx, r in enumerate(Sum.ORDER):
        jj = flip(j, r)
        for h in range(2):
            at = pl.ds(pl.multiple_of(jj * rows + h * half, half), half)
            part[jj, h] = dot(dqkv[at, 0:160], w_one).astype(BF16)
        one_sum.send(r)
        if idx:
            one_sum.take(Sum.ORDER[idx - 1])
    one_sum.take(Sum.ORDER[-1])

    def one_grad(m, c):
        cols = pl.ds(pl.multiple_of(m * 256, 256), 256)
        block = dot(turned[0:160, :], wide[:, :, :, cols].reshape(tokens, 256))
        grads_a[0:160, cols] = block.astype(BF16)
        return c

    lax.fori_loop(0, width // 256, one_grad, 0)
    grads_a[160:288, :] = grads_o[...]
    if in_kernel:
        back_a = Back(n, grads_a, tiles_a, asems)
        back_a.start()
    else:
        copy = pltpu.make_async_copy(grads_a, tiles_a, lsem.at[3])
        copy.start()
    for p in range(3):
        one_sum.phase(p)
    one_sum.trade()
    one_sum.finish()

    gain_one = w_ref[160:161, :].astype(F32)
    load_mid.wait()
    for h in range(2):

        def norm_back_one(at):
            x = tok_ref[h, at].astype(F32)
            root = lax.rsqrt(jnp.mean(x * x, axis=-1, keepdims=True) + EPS)
            normed = x * root
            scaled = total[h, at] * gain_one
            grad_ref[h, at] = grad_ref[h, at] + root * (
                scaled - normed * jnp.mean(scaled * normed, axis=-1, keepdims=True)
            )

        row_loop(half, 16, norm_back_one)

    if in_kernel:
        back_b.finish()
        back_a.finish()
    else:
        copy.wait()


def third_shifted(third):
    return jnp.concatenate([jnp.zeros_like(third[:, :FEAT]), third[:, : 128 - FEAT]], axis=1)


def tail_call(n, lengths, q, k, v, y, den, state, w_a, mid, tokens, d_mid, dy, hidden, down, grads_o, low_one, grads_b):
    groups = n // CUBE
    _, half, width = mid.shape
    rows = 2 * half
    count = CUBE * rows
    wide_columns = width // n % 128 == 0
    vm = pl.BlockSpec(memory_space=pltpu.VMEM)
    any_space = pl.BlockSpec(memory_space=pl.ANY)
    peers = max(groups - 1, 1)
    out_shape = [
        jax.ShapeDtypeStruct((2, half, width), BF16),
        jax.ShapeDtypeStruct((2, half, width), F32),
        jax.ShapeDtypeStruct((n, grads_b.shape[0], width // n) if wide_columns else (8, 128), BF16),
        jax.ShapeDtypeStruct((n, 288, width // n) if wide_columns else (288, width), BF16),
    ]
    output, grad, tiles_b, tiles_a = pl.pallas_call(
        functools.partial(tail_kernel, n),
        out_shape=out_shape,
        in_specs=[pl.BlockSpec(memory_space=pltpu.SMEM)] + [vm] * 12 + [any_space] * 4 + [vm] * 3,
        out_specs=[vm, vm, any_space, any_space],
        scratch_shapes=[
            pltpu.VMEM((CUBE, 2, half, width), BF16),
            pltpu.VMEM((15, half, width), BF16),
            pltpu.VMEM((15, half, width), BF16),
            pltpu.VMEM((CUBE, 2, half, width), BF16),
            pltpu.VMEM((2, half, width), F32),
            pltpu.VMEM((count, 256), BF16),
            pltpu.VMEM((count, 256), BF16),
            pltpu.VMEM((count, 256), BF16),
            pltpu.VMEM((count, 128), F32),
            pltpu.VMEM((count, 128), F32),
            pltpu.VMEM((256, count), BF16),
            pltpu.VMEM((count, 256), BF16),
            pltpu.VMEM((288, width), BF16),
            pltpu.VMEM((384, 256), F32),
            pltpu.VMEM((peers, 384, 256), F32),
            pltpu.SemaphoreType.DMA((peers,)),
            pltpu.SemaphoreType.DMA((peers,)),
            pltpu.SemaphoreType.DMA((4,)),
            *sum_sems(),
            *sum_sems(),
            *spread_sems(n),
            *spread_sems(n),
        ],
        compiler_params=pltpu.CompilerParams(collective_id=2, has_side_effects=True, vmem_limit_bytes=63 * MIB),
    )(
        lengths, q, k, v, y, den, state, w_a, tokens.reshape(2, half, width), dy, hidden, down, grads_o,
        mid, d_mid, low_one, grads_b, *spreaders(),
    )
    if not wide_columns:
        tiles_b = back_call(n, grads_b, 9)
        tiles_a = back_call(n, tiles_a, 10)
    return output.reshape(rows, width), grad.reshape(rows, width), tiles_b, tiles_a


def units_first(w):
    return jnp.pad(w, ((0, CUBE * UNITS - w.shape[0]), (0, 0))).reshape(CUBE, UNITS, w.shape[1])


def body(
    n, tokens, gain_attn, w_query, w_key, w_value, w_output, gain_mlp, w_gate, w_up, w_down, seq_lengths, cotangent
):
    per = HEADS // lax.axis_size("tensor")
    gains = jnp.concatenate([gain_attn[None], gain_mlp[None], jnp.zeros((14, gain_attn.shape[0]), BF16)], axis=0)
    pack_a = jnp.concatenate(
        [
            w_value.T.reshape(per, 128, -1),
            w_query.T.reshape(per, FEAT, -1),
            w_key.T.reshape(per, FEAT, -1),
            jnp.broadcast_to(gains[None], (per, *gains.shape)),
            w_output.reshape(per, 128, -1),
        ],
        axis=1,
    )
    pack_b = jnp.concatenate([units_first(w_gate.T), units_first(w_up.T)], axis=1)
    w_a, w_gu, cot_all, low_one, low_two, mid, q, k, v, y, y_turned, den, state = head_call(
        n, seq_lengths, pack_a, pack_b, tokens, cotangent
    )
    hidden, down, grads_b, tiles_d, grads_o, d_mid, dy = mlp_call(
        n, low_two, w_a, y_turned, mid, w_gu, units_first(w_down), cot_all
    )
    if tiles_d.ndim == 2:
        tiles_d = back_call(n, tiles_d, 7)
    output, grad_tokens, tiles_b, tiles_a = tail_call(
        n, seq_lengths, q, k, v, y, den, state, w_a, mid, tokens, d_mid, dy, hidden, down, grads_o, low_one, grads_b
    )

    def arrived(tiles):
        return tiles.reshape(-1, CUBE, *tiles.shape[1:]).astype(F32).sum(axis=0)

    back_b, back_d, back_a = arrived(tiles_b), arrived(tiles_d), arrived(tiles_a)

    def units(part):
        return part.reshape(CUBE * UNITS, -1)[: w_gate.shape[1]]

    grad_gate = units(back_b[:, :UNITS]).T
    grad_up = units(back_b[:, UNITS : 2 * UNITS]).T
    grad_down = units(back_d)
    grad_value = back_a[:, 0:128].reshape(per * 128, -1).T
    grad_query = back_a[:, 128:144].reshape(per * FEAT, -1).T
    grad_key = back_a[:, 144:160].reshape(per * FEAT, -1).T
    grad_output = back_a[:, 160:288].reshape(per * 128, -1)

    def weighed(*pairs):
        return sum(jnp.sum(w.astype(F32) * g, axis=1) for w, g in pairs)

    gain_one_part = weighed((w_value, grad_value), (w_query, grad_query), (w_key, grad_key))
    gain_two_part = weighed((w_gate, grad_gate), (w_up, grad_up))
    both = lax.psum(jnp.stack([gain_one_part, gain_two_part]), "tensor")
    grad_gain_one = both[0] / gain_attn.astype(F32)
    grad_gain_two = both[1] / gain_mlp.astype(F32)
    return (
        output,
        grad_tokens,
        grad_gain_one,
        grad_query,
        grad_key,
        grad_value,
        grad_output,
        grad_gain_two,
        grad_gate,
        grad_up,
        grad_down,
    )


def solution(mesh):
    return jax.shard_map(
        functools.partial(body, mesh.shape["seq"]),
        mesh=mesh,
        in_specs=(
            P("seq", None),
            P("seq"),
            P("seq", "tensor"),
            P("seq", "tensor"),
            P("seq", "tensor"),
            P("tensor", "seq"),
            P("seq"),
            P("seq", "tensor"),
            P("seq", "tensor"),
            P("tensor", "seq"),
            P(),
            P("seq", None),
        ),
        out_specs=(
            P("seq", None),
            P("seq", None),
            P("seq"),
            P("seq", "tensor"),
            P("seq", "tensor"),
            P("seq", "tensor"),
            P("tensor", "seq"),
            P("seq"),
            P("seq", "tensor"),
            P("seq", "tensor"),
            P("tensor", "seq"),
        ),
        check_vma=False,
    )
```

```python
import functools

import jax
import jax.numpy as jnp
import numpy as np
from jax import lax
from jax.experimental import pallas as pl
from jax.experimental.pallas import tpu as pltpu
from jax.sharding import PartitionSpec as P

MESH = pl.DeviceIdType.MESH
HEADS = 16
FEAT = 16
CUBE = 8
UNITS = 352
EPS = 1e-06
F32 = jnp.float32
BF16 = jnp.bfloat16
ORDERS = ((0, 1, 2), (1, 2, 0), (2, 0, 1))
PIECES = ((0, 48), (48, 48), (96, 32))
WAVES = ((4, 1, 2), (6, 5, 3), (7,))
UP_FIRST = ((2, 0, 1), (2, 1, 0))
UP_LAST = ((0, 1, 2), (1, 0, 2))
HALVES = ((0, 64), (64, 64))
MIB = 1 << 20


def flip(place, mask):
    total = 0
    for b in range(3):
        bit = (place // (1 << b)) % 2
        total = total + ((1 - bit) if (mask >> b) & 1 else bit) * (1 << b)
    return total


def subsets(dims):
    out = [0]
    for d in dims:
        out = out + [r | (1 << d) for r in out]
    return out


def whereabouts():
    s = lax.axis_index("seq")
    t = lax.axis_index("tensor")
    j = s % CUBE
    return s, t, j, s - j


def remote(src, dst, send, recv, device):
    return pltpu.make_async_remote_copy(
        src_ref=src, dst_ref=dst, send_sem=send, recv_sem=recv, device_id=device, device_id_type=MESH
    )


def greet(devices):
    barrier = pltpu.get_barrier_semaphore()
    for device in devices:
        pl.semaphore_signal(barrier, inc=1, device_id=device, device_id_type=MESH)
    pl.semaphore_wait(barrier, len(devices))


def near():
    s, t, j, base = whereabouts()
    return [(base + flip(j, 1 << d), t) for d in range(3)] + [(s, 1 - t)]


def greet_all(n):
    s, t, _, _ = whereabouts()
    barrier = pltpu.get_barrier_semaphore()

    def one(k, carry):
        pl.semaphore_signal(barrier, inc=1, device_id=((s + k) % n, t), device_id_type=MESH)
        return carry

    lax.fori_loop(1, n, one, 0)
    pl.semaphore_signal(barrier, inc=1, device_id=(s, 1 - t), device_id_type=MESH)
    pl.semaphore_wait(barrier, n)


class Gather:
    def __init__(self, own, full, sems, orders=ORDERS, pieces=PIECES):
        self.own, self.full, self.orders, self.pieces = own, full, orders, pieces
        self.ssem, self.rsem, self.csend, self.crecv, self.lsem = sems
        self.s, self.t, self.j, self.base = whereabouts()

    def view(self, r, i):
        off, rows = self.pieces[i]
        return self.full.at[flip(self.j, r), self.t, pl.ds(off, rows)]

    def hop(self, p, i, r):
        d = self.orders[i][p]
        off, rows = self.pieces[i]
        src = self.own.at[self.t, pl.ds(off, rows)] if r == 0 else self.view(r, i)
        k = r | (1 << d)
        return remote(src, self.view(r, i), self.ssem.at[i, k], self.rsem.at[i, k], (self.base + flip(self.j, 1 << d), self.t))

    def came(self, i, k):
        p = max(q for q in range(3) if k >> self.orders[i][q] & 1)
        return p, k ^ (1 << self.orders[i][p])

    def arrival(self, i, k):
        p, _ = self.came(i, k)
        device = (self.base + flip(self.j, 1 << self.orders[i][p]), self.t)
        return remote(self.view(k, i), self.view(k, i), self.ssem.at[i, k], self.rsem.at[i, k], device)

    def across(self, r, mine):
        ref = self.full.at[flip(self.j, r), self.t if mine else 1 - self.t]
        return remote(ref, ref, self.csend.at[r], self.crecv.at[r], (self.s, 1 - self.t))

    def local(self):
        return pltpu.make_async_copy(self.own, self.full.at[self.j], self.lsem)

    def start(self):
        self.local().start()
        for q in range(3):
            for i in range(len(self.pieces)):
                self.hop(q, i, 0).start()

    def arrived(self, k):
        for i in range(len(self.pieces)):
            p, _ = self.came(i, k)
            self.arrival(i, k).wait_recv()
            for q in range(p + 1, 3):
                self.hop(q, i, k).start()
        self.across(k, True).start()

    def wave(self, w, tick=lambda: None):
        for k in WAVES[w]:
            self.arrived(k)
            tick()

    def settle(self, r):
        self.across(r, False).wait_recv()

    def sent(self):
        for k in range(1, CUBE):
            self.across(k, True).wait_send()
            for i in range(len(self.pieces)):
                p, r = self.came(i, k)
                self.hop(p, i, r).wait_send()

    def finish(self):
        for r in range(1, CUBE):
            self.settle(r)
        self.sent()
        self.local().wait()

    def blocks(self, tick=lambda: None):
        self.start()
        self.local().wait()
        yield 0
        before = None
        for k in WAVES[0] + WAVES[1] + WAVES[2]:
            self.arrived(k)
            tick()
            if before:
                self.settle(before)
                yield before
            before = k
        self.settle(before)
        yield before
        self.sent()


def gather_sems():
    return [pltpu.SemaphoreType.DMA((3, CUBE))] * 2 + [pltpu.SemaphoreType.DMA((CUBE,))] * 2 + [pltpu.SemaphoreType.DMA]


SLOT = {0: 0, 1: 4, 2: 6}


def slot_of(order, p, r):
    return SLOT[p] + subsets(order[p + 1 :]).index(r)


class Sum:
    ORDER = (7, 6, 5, 3, 4, 2, 1, 0)

    def __init__(self, part, heap, total, sems, orders=ORDERS, pieces=PIECES):
        self.part, self.heap, self.total = part, heap, total
        self.orders, self.pieces = orders, pieces
        self.csend, self.crecv, self.ssem, self.rsem, self.fsend, self.frecv = sems
        self.s, self.t, self.j, self.base = whereabouts()

    def across(self, r):
        src = self.part.at[flip(self.j, r), 1 - self.t]
        return remote(src, self.heap.at[r], self.csend.at[r], self.crecv.at[r], (self.s, 1 - self.t))

    def hop(self, p, i, r):
        d = self.orders[i][p]
        off, rows = self.pieces[i]
        k = slot_of(self.orders[i], p, r ^ (1 << d))
        return remote(
            self.part.at[flip(self.j, r), self.t, pl.ds(off, rows)],
            self.heap.at[CUBE + k, pl.ds(off, rows)],
            self.ssem.at[i, k],
            self.rsem.at[i, k],
            (self.base + flip(self.j, 1 << d), self.t),
        )

    def send(self, r):
        self.across(r).start()

    def take(self, r, leave=True):
        self.across(r).wait_recv()
        jj = flip(self.j, r)
        step = 32

        def one(m, c):
            at = pl.ds(pl.multiple_of(m * step, step), step)
            self.part[jj, self.t, at] = (
                self.part[jj, self.t, at].astype(F32) + self.heap[r, at].astype(F32)
            ).astype(BF16)
            return c

        lax.fori_loop(0, self.part.shape[2] // step, one, 0)
        if leave:
            self.leave(r)

    def leave(self, r):
        for i in range(len(self.pieces)):
            if r >> self.orders[i][0] & 1 and r != 1 << self.orders[i][0]:
                self.hop(0, i, r).start()

    def phase(self, p, tick=lambda: None):
        count = len(self.pieces)
        for i, r in [(i, subsets(self.orders[i][p + 1 :])[-1 - m]) for m in range((4 >> p) - 1) for i in range(count)]:
            d = self.orders[i][p]
            off, rows = self.pieces[i]
            self.hop(p, i, r | (1 << d)).wait_recv()
            jj = flip(self.j, r)
            k = slot_of(self.orders[i], p, r)
            for q in range(0, rows, 16):
                at = pl.ds(off + q, 16)
                new = self.part[jj, self.t, at].astype(F32) + self.heap[CUBE + k, at].astype(F32)
                self.part[jj, self.t, at] = new.astype(BF16)
            e = self.orders[i][p + 1]
            if r >> e & 1 and (p == 1 or r != 1 << e):
                self.hop(p + 1, i, r).start()
            tick()
        for i in range(count):
            self.hop(p, i, 1 << self.orders[i][p]).start()

    def close(self, tick=lambda: None):
        for i in range(len(self.pieces)):
            off, rows = self.pieces[i]
            for p in range(3):
                self.hop(p, i, 1 << self.orders[i][p]).wait_recv()
            slots = [CUBE + slot_of(self.orders[i], p, 0) for p in range(3)]
            for q in range(0, rows, 16):
                at = pl.ds(off + q, 16)
                new = self.part[self.j, self.t, at].astype(F32)
                for k in slots:
                    new = new + self.heap[k, at].astype(F32)
                self.total[self.t, at] = new
            tick()
        self.trade()

    def both(self, half):
        ref = self.total.at[half]
        return remote(ref, ref, self.fsend, self.frecv, (self.s, 1 - self.t))

    def trade(self):
        self.both(self.t).start()

    def crossed(self):
        for r in range(CUBE):
            self.across(r).wait_send()

    def finish(self, crossed=False):
        self.both(1 - self.t).wait_recv()
        self.both(self.t).wait_send()
        if not crossed:
            self.crossed()
        for p in range(3):
            for i in range(len(self.pieces)):
                d = self.orders[i][p]
                for r in subsets(self.orders[i][p + 1 :]):
                    self.hop(p, i, r | (1 << d)).wait_send()

    def run(self):
        for r in self.ORDER:
            self.send(r)
        for r in self.ORDER:
            self.take(r)
        self.phase(0)
        self.phase(1)
        self.close()
        self.finish()


def sum_sems():
    return [
        pltpu.SemaphoreType.DMA((CUBE,)),
        pltpu.SemaphoreType.DMA((CUBE,)),
        pltpu.SemaphoreType.DMA((3, CUBE)),
        pltpu.SemaphoreType.DMA((3, CUBE)),
        pltpu.SemaphoreType.DMA,
        pltpu.SemaphoreType.DMA,
    ]


def columns_of(ref, s):
    if len(ref.shape) == 3:
        return ref.at[s]
    return ref.at[:, pl.ds(pl.multiple_of(s * 128, 128), 128)]


def columns_apart(n, rows, width):
    return (rows, width) if width // n % 128 == 0 else (n, rows, width // n)


def together(x):
    return x if x.ndim == 2 else x.transpose(1, 0, 2).reshape(x.shape[1], -1)


def apart(n, x):
    return x if x.shape[1] // n % 128 == 0 else x.reshape(x.shape[0], n, -1).transpose(1, 0, 2)


class Trickle:
    def __init__(self, copies):
        self.copies = list(copies)

    def __call__(self, count=1):
        for _ in range(min(count, len(self.copies))):
            self.copies.pop(0).start()

    def flush(self):
        self(len(self.copies))


def far_and_near(n):
    near, far = list(range(1, n // 2)), list(range(n // 2, n))
    return [k for pair in zip(far, near + [None]) for k in pair if k is not None]


class Spread:
    def __init__(self, n, pack, full, sems):
        self.n, self.pack, self.full = n, pack, full
        self.ssem, self.rsem, self.lsem = sems
        self.s, self.t, self.j, self.base = whereabouts()

    def columns(self, s):
        return columns_of(self.full, s)

    def copy(self, k):
        to = (self.s + k) % self.n
        return remote(self.pack.at[to % CUBE], self.columns(self.s), self.ssem.at[k], self.rsem.at[k], (to, self.t))

    def arrival(self, k):
        at = (self.s + self.n - k) % self.n
        return remote(self.pack.at[0], self.columns(at), self.ssem.at[k], self.rsem.at[k], (at, self.t))

    def local(self):
        return pltpu.make_async_copy(self.pack.at[self.j], self.columns(self.s), self.lsem)

    def start(self):
        lax.fori_loop(1, self.n, lambda k, c: (self.copy(k).start(), c)[1], 0)
        self.local().start()

    def trickle(self):
        return [self.local()] + [self.copy(k) for k in far_and_near(self.n)]

    def finish(self):
        self.local().wait()
        lax.fori_loop(1, self.n, lambda k, c: (self.arrival(k).wait_recv(), c)[1], 0)
        lax.fori_loop(1, self.n, lambda k, c: (self.copy(k).wait_send(), c)[1], 0)


class Back:
    def __init__(self, n, grads, tiles, sems):
        self.n, self.grads, self.tiles = n, grads, tiles
        self.ssem, self.rsem, self.lsem = sems
        self.s, self.t, self.j, self.base = whereabouts()

    def columns(self, s):
        return columns_of(self.grads, s)

    def copy(self, k):
        to = (self.s + k) % self.n
        return remote(self.columns(to), self.tiles.at[self.s], self.ssem.at[k], self.rsem.at[k], (to, self.t))

    def arrival(self, k):
        at = (self.s + self.n - k) % self.n
        return remote(self.tiles.at[at], self.tiles.at[at], self.ssem.at[k], self.rsem.at[k], (at, self.t))

    def local(self):
        return pltpu.make_async_copy(self.columns(self.s), self.tiles.at[self.s], self.lsem)

    start = Spread.start
    trickle = Spread.trickle
    finish = Spread.finish


def spread_sems(n):
    return [pltpu.SemaphoreType.DMA((n,)), pltpu.SemaphoreType.DMA((n,)), pltpu.SemaphoreType.DMA]


def spread_kernel(n, pack, full, *sems):
    greet_all(n)
    spread = Spread(n, pack, full, sems)
    spread.start()
    spread.finish()


def spread_call(n, pack, width, number):
    any_space = pl.BlockSpec(memory_space=pl.ANY)
    full = pl.pallas_call(
        functools.partial(spread_kernel, n),
        out_shape=jax.ShapeDtypeStruct(columns_apart(n, pack.shape[1], width), BF16),
        in_specs=[any_space],
        out_specs=any_space,
        scratch_shapes=spread_sems(n),
        compiler_params=pltpu.CompilerParams(collective_id=number, has_side_effects=True),
    )(pack)
    return together(full)


def back_kernel(n, grads, tiles, *sems):
    greet_all(n)
    back = Back(n, grads, tiles, sems)
    back.start()
    back.finish()


def back_call(n, grads, number):
    rows, width = grads.shape
    any_space = pl.BlockSpec(memory_space=pl.ANY)
    return pl.pallas_call(
        functools.partial(back_kernel, n),
        out_shape=jax.ShapeDtypeStruct((n, rows, width // n), BF16),
        in_specs=[any_space],
        out_specs=any_space,
        scratch_shapes=spread_sems(n),
        compiler_params=pltpu.CompilerParams(collective_id=number, has_side_effects=True),
    )(apart(n, grads))


def dot(a, b):
    return jnp.dot(a, b, preferred_element_type=F32)


def dot_nt(a, b):
    return lax.dot_general(a, b, (((1,), (1,)), ((), ())), preferred_element_type=F32)


def dot_tn(a, b):
    return lax.dot_general(a, b, (((0,), (0,)), ((), ())), preferred_element_type=F32)


def spreaders():
    first = np.repeat(np.eye(FEAT), FEAT, axis=1)
    second = np.tile(np.eye(FEAT), (1, FEAT))
    third = np.eye(FEAT, 128)
    return [jnp.asarray(m, BF16) for m in (first, second, third)]


ROOT_HALF = 0.5**0.5


def lift(u, keep, first, second, third):
    quad = dot(u, first) * dot(u, second) * (0.25 * ROOT_HALF) * keep
    lane = lax.broadcasted_iota(jnp.int32, (u.shape[0], 128), 1)
    line = (dot(u, third) * 0.5 + jnp.where(lane == FEAT, 1.0, 0.0)) * keep
    return quad.astype(BF16), line.astype(BF16)


def lift_back(u, d_quad, d_line, first, second):
    one, two = dot(u, first) * 0.5, dot(u, second) * 0.5
    back = dot_nt((d_quad * two).astype(BF16), first) + dot_nt((d_quad * one).astype(BF16), second)
    return back * ROOT_HALF + d_line[:, :FEAT]


def two_terms(x):
    high = x.astype(BF16)
    return high, (x - high.astype(F32)).astype(BF16)


def segments(start_two, start_three, first_position, count, axis):
    shape = (count, 1) if axis == 0 else (1, count)
    position = first_position + lax.broadcasted_iota(jnp.int32, shape, axis)
    return position, (position >= start_two).astype(jnp.int32) + (position >= start_three).astype(jnp.int32)


def pair_mask(two, three, at_t, at_s, block):
    pos_t, seg_t = segments(two, three, at_t, block, 0)
    pos_s, seg_s = segments(two, three, at_s, block, 1)
    return (pos_s <= pos_t) & (seg_s == seg_t)


def pair_mask_turned(two, three, at_s, at_t, block):
    pos_s, seg_s = segments(two, three, at_s, block, 0)
    pos_t, seg_t = segments(two, three, at_t, block, 1)
    return (pos_s <= pos_t) & (seg_s == seg_t)


def other_groups(groups):
    s, t, j, base = whereabouts()
    return [((s + CUBE * k) % (CUBE * groups), t) for k in range(1, groups)]


def exchange(groups, mine, theirs, ssem, rsem, before):
    s, t, j, base = whereabouts()
    c = s // CUBE
    for k, device in enumerate(other_groups(groups)):
        remote(mine, theirs.at[k], ssem.at[k], rsem.at[k], device).start()

    def finish():
        total = jnp.zeros(mine.shape, F32)
        for k, device in enumerate(other_groups(groups)):
            remote(mine, theirs.at[k], ssem.at[k], rsem.at[k], device).wait_recv()
            source = (c + groups - (k + 1)) % groups
            counts = (source < c) if before else (source > c)
            total = total + jnp.where(counts, theirs[k], 0.0)
        for k, device in enumerate(other_groups(groups)):
            remote(mine, theirs.at[k], ssem.at[k], rsem.at[k], device).wait_send()
        return total

    return finish


BLOCK = 256


def row_loop(count, step, work):
    def one(m, c):
        work(pl.ds(pl.multiple_of(m * step, step), step))
        return c

    lax.fori_loop(0, count // step, one, 0)


def pair_weight(score):
    return (score * 0.5 + 1.0) * score + 1.0


def head_kernel(
    n, lengths, tok_ref, pack_a, pack_o, pack_b, cot_hbm, first, second, third,
    w_ref, wo_ref, w_b, cot_all, low_hbm, own, mid_ref, q_ref, k_ref, v_ref, y_ref, y_turned, den_ref, state_ref,
    wide, part, heap, total, kept, state_mine, state_theirs, xsend, xrecv, lsem, *sems,
):
    groups = n // CUBE
    s, t, j, base = whereabouts()
    half, width = tok_ref.shape[1:]
    rows = 2 * half
    tokens = CUBE * rows
    two, three = lengths[0], lengths[0] + lengths[1]
    start = base * rows
    in_kernel = len(pack_a.shape) == 3
    sum_sem, tok_sem, cot_sem = sems[0:6], sems[6:11], sems[11:16]
    a_sem, b_sem, o_sem = sems[16:19], sems[19:22], sems[22:25]

    greet_all(n)
    g_tok = Gather(tok_ref, wide, tok_sem)
    g_cot = Gather(cot_hbm, cot_all, cot_sem, UP_FIRST, HALVES)
    if in_kernel:
        spread_a = Spread(n, pack_a, w_ref, a_sem)
        spread_b = Spread(n, pack_b, w_b, b_sem)
        spread_o = Spread(n, pack_o, wo_ref, o_sem)
        spread_a.start()
        tick = Trickle(spread_o.trickle() + spread_b.trickle())
    else:
        copy_a = pltpu.make_async_copy(pack_a, w_ref, lsem.at[CUBE])
        copy_b = pltpu.make_async_copy(pack_b, w_b, lsem.at[CUBE + 1])
        copy_o = pltpu.make_async_copy(pack_o, wo_ref, lsem.at[CUBE + 2])
        copy_a.start()
        tick = Trickle([copy_o, copy_b])
    g_tok.start()
    for w in range(3):
        g_tok.wave(w)
    tick.flush()
    g_cot.start()
    g_tok.finish()
    if in_kernel:
        spread_a.finish()
    else:
        copy_a.wait()

    state_mine[...] = jnp.zeros_like(state_mine)
    gain_one = w_ref[160:161, :].astype(F32)

    def project(jj, c):
        for h in range(2):

            def norm(at):
                x = wide[jj, h, at].astype(F32)
                root = lax.rsqrt(jnp.mean(x * x, axis=-1, keepdims=True) + EPS)
                wide[jj, h, at] = (x * root * gain_one).astype(BF16)

            row_loop(half, 64, norm)
        at = pl.ds(pl.multiple_of(jj * rows, rows), rows)
        qkv = dot_nt(wide[jj].reshape(rows, width), w_ref[0:160, :]).astype(BF16)
        v, k = qkv[:, 0:128], qkv[:, 144:160]
        lane = lax.broadcasted_iota(jnp.int32, (rows, 128), 1)
        v_ext = jnp.concatenate([v, jnp.where(lane < 2, 1.0, 0.0).astype(BF16)], axis=1)
        q_ref[at, :] = qkv[:, 128:144]
        k_ref[at, :] = k
        v_ref[at, :] = v_ext
        _, seg = segments(two, three, start + jj * rows, rows, 0)
        keep = (seg == 1).astype(F32)
        kept[at, :] = v_ext * keep.astype(BF16)
        quad, line = lift(k, keep, first[...], second[...], third[...])
        state_mine[0:256, :] += dot_tn(quad, v_ext)
        state_mine[256:384, :] += dot_tn(line, v_ext)
        return c

    lax.fori_loop(0, CUBE, project, 0)
    save = pltpu.make_async_copy(wide, low_hbm, lsem.at[0])
    save.start()
    done = exchange(groups, state_mine, state_theirs, xsend, xrecv, True)
    g_cot.wave(0)

    blocks = tokens // BLOCK
    for tb in range(blocks):
        tq = pl.ds(tb * BLOCK, BLOCK)
        qt = q_ref[tq, :] * BF16(0.25)
        score = dot_nt(qt, k_ref[tq, :])
        mask = pair_mask(two, three, start + tb * BLOCK, start + tb * BLOCK, BLOCK)
        acc = dot(jnp.where(mask, pair_weight(score), 0.0).astype(BF16), v_ref[tq, :])
        if tb:
            _, seg = segments(two, three, start + tb * BLOCK, BLOCK, 0)
            far = jnp.zeros((BLOCK, 256), F32)
            for lo in range(0, tb * BLOCK, 512):
                sq = pl.ds(lo, min(512, tb * BLOCK - lo))
                far = far + dot(pair_weight(dot_nt(qt, k_ref[sq, :])).astype(BF16), kept[sq, :])
            acc = acc + far * (seg == 1).astype(F32)
        y_ref[tq, :] = acc[:, :128]
        den_ref[tq, :] = acc[:, 128:]

    g_cot.wave(1)
    state = done()
    state_ref[...] = state
    high, lowp = two_terms(state)
    out_sum = Sum(part, heap, total, sum_sem)
    if in_kernel:
        spread_o.finish()
    else:
        copy_o.wait()
    out_w = wo_ref[...]

    for idx, r in enumerate(Sum.ORDER):
        jj = flip(j, r)
        tq = pl.ds(pl.multiple_of(jj * rows, rows), rows)
        _, seg = segments(two, three, start + jj * rows, rows, 0)
        quad, line = lift(q_ref[tq, :], (seg == 1).astype(F32), first[...], second[...], third[...])
        more = dot(quad, high[0:256]) + dot(quad, lowp[0:256]) + dot(line, high[256:384]) + dot(line, lowp[256:384])
        den = den_ref[tq, :] + more[:, 128:]
        den_ref[tq, :] = den
        y = (y_ref[tq, :] + more[:, :128]) / den[:, 0:1]
        y_ref[tq, :] = y
        y_low = y.astype(BF16)
        y_turned[:, tq] = y_low.T
        for h in range(2):
            part[jj, h] = dot(y_low[h * half : (h + 1) * half], out_w).astype(BF16)
        out_sum.send(r)
        if idx:
            out_sum.take(Sum.ORDER[idx - 1])
    out_sum.take(Sum.ORDER[-1])
    out_sum.phase(0)
    out_sum.phase(1)
    out_sum.close()
    out_sum.finish()

    gain_two = w_ref[161:162, :].astype(F32)
    for h in range(2):

        def second_norm(at):
            mid = tok_ref[h, at].astype(F32) + total[h, at]
            mid_ref[h, at] = mid
            root = lax.rsqrt(jnp.mean(mid * mid, axis=-1, keepdims=True) + EPS)
            own[h, at] = (mid * root * gain_two).astype(BF16)

        row_loop(half, 16, second_norm)

    g_cot.wave(2)
    g_cot.finish()
    save.wait()
    if in_kernel:
        spread_b.finish()
    else:
        copy_b.wait()


def head_call(n, lengths, pack_a, pack_o, pack_b, tokens, cot):
    groups = n // CUBE
    rows, width = tokens.shape
    half = rows // 2
    count = CUBE * rows
    vm = pl.BlockSpec(memory_space=pltpu.VMEM)
    any_space = pl.BlockSpec(memory_space=pl.ANY)
    peers = max(groups - 1, 1)
    w_rows = (pack_a.shape[1], pack_b.shape[1])
    if width // n % 128:
        pack_a, pack_b = spread_call(n, pack_a, width, 4), spread_call(n, pack_b, width, 5)
        pack_o = spread_call(n, pack_o, width, 11)
    shape = (CUBE, 2, half, width)
    return pl.pallas_call(
        functools.partial(head_kernel, n),
        out_shape=[
            jax.ShapeDtypeStruct((w_rows[0], width), BF16),
            jax.ShapeDtypeStruct((128, width), BF16),
            jax.ShapeDtypeStruct((w_rows[1], width), BF16),
            jax.ShapeDtypeStruct(shape, BF16),
            jax.ShapeDtypeStruct(shape, BF16),
            jax.ShapeDtypeStruct((2, half, width), BF16),
            jax.ShapeDtypeStruct((2, half, width), F32),
            jax.ShapeDtypeStruct((count, FEAT), BF16),
            jax.ShapeDtypeStruct((count, FEAT), BF16),
            jax.ShapeDtypeStruct((count, 256), BF16),
            jax.ShapeDtypeStruct((count, 128), F32),
            jax.ShapeDtypeStruct((128, count), BF16),
            jax.ShapeDtypeStruct((count, 128), F32),
            jax.ShapeDtypeStruct((384, 256), F32),
        ],
        in_specs=[pl.BlockSpec(memory_space=pltpu.SMEM), vm] + [any_space] * 4 + [vm] * 3,
        out_specs=[vm, vm, any_space, any_space, any_space] + [vm] * 9,
        scratch_shapes=[
            pltpu.VMEM(shape, BF16),
            pltpu.VMEM(shape, BF16),
            pltpu.VMEM((15, half, width), BF16),
            pltpu.VMEM((2, half, width), F32),
            pltpu.VMEM((count, 256), BF16),
            pltpu.VMEM((384, 256), F32),
            pltpu.VMEM((peers, 384, 256), F32),
            pltpu.SemaphoreType.DMA((peers,)),
            pltpu.SemaphoreType.DMA((peers,)),
            pltpu.SemaphoreType.DMA((CUBE + 3,)),
            *sum_sems(),
            *gather_sems(),
            *gather_sems(),
            *spread_sems(n),
            *spread_sems(n),
            *spread_sems(n),
        ],
        compiler_params=pltpu.CompilerParams(collective_id=1, has_side_effects=True, vmem_limit_bytes=62 * MIB),
    )(lengths, tokens.reshape(2, half, width), pack_a, pack_o, pack_b, cot.reshape(2, half, width), *spreaders())


def mlp_kernel(
    n, own, w_ref, wo_ref, y_turned, mid_hbm, w_hbm, pack_d, cot_hbm,
    grads_u, tiles_d, tiles_g, out_half, grads_o, d_mid, dy_ref,
    wide, wide_g, part, heap, total, w_gu, hidden, down, by_gate, by_up, d_gate, d_up, grads_d, lsem, *sems,
):
    s, t, j, base = whereabouts()
    half, width = own.shape[1:]
    rows = 2 * half
    in_kernel = len(pack_d.shape) == 3
    two_sem, attn_sem, low_sem, out_sem = sems[0:5], sems[5:10], sems[10:16], sems[16:22]
    d_sem, back_d_sem, back_g_sem = sems[22:25], sems[25:28], sems[28:31]

    load_w = pltpu.make_async_copy(w_hbm, w_gu, lsem.at[0])
    load_mid = pltpu.make_async_copy(mid_hbm, d_mid, lsem.at[1])
    load_w.start()
    load_mid.start()
    greet_all(n)
    load_cot = pltpu.make_async_copy(cot_hbm, wide_g, lsem.at[6])
    load_cot.start()
    g_two = Gather(own, wide, two_sem)
    if in_kernel:
        spread_d = Spread(n, pack_d, down, d_sem)
        tick = Trickle(spread_d.trickle())
    else:
        copy_d = pltpu.make_async_copy(pack_d, down, lsem.at[2])
        tick = Trickle([copy_d])

    for r in g_two.blocks(lambda: tick(2)):
        if r == 0:
            load_w.wait()
        jj = flip(j, r)
        at = pl.ds(pl.multiple_of(jj * rows, rows), rows)
        low = wide[jj].reshape(rows, width)
        gate = dot_nt(w_gu[0:UNITS, :], low)
        up = dot_nt(w_gu[UNITS:, :], low)
        sigma = jax.nn.sigmoid(gate)
        silu = gate * sigma
        hidden[:, at] = (silu * up).astype(BF16)
        by_gate[:, at] = (up * sigma * (1.0 + gate * (1.0 - sigma))).astype(BF16)
        by_up[:, at] = silu.astype(BF16)
    tick.flush()
    load_cot.wait()
    if in_kernel:
        spread_d.finish()
    else:
        copy_d.wait()

    low_sum = Sum(part, heap, total, low_sem)
    for idx, r in enumerate(Sum.ORDER):
        jj = flip(j, r)
        at = pl.ds(pl.multiple_of(jj * rows, rows), rows)
        grad = dot_nt(down[...], wide_g[jj].reshape(rows, width))
        dg = (grad * by_gate[:, at].astype(F32)).astype(BF16)
        du = (grad * by_up[:, at].astype(F32)).astype(BF16)
        d_gate[:, at] = dg
        d_up[:, at] = du
        for col in range(0, width, 512):
            cols = pl.ds(col, 512)
            block = dot_tn(dg, w_gu[0:UNITS, cols]) + dot_tn(du, w_gu[UNITS:, cols])
            part[jj, :, :, cols] = block.astype(BF16).reshape(2, half, 512)
        low_sum.send(r)
        if idx:
            low_sum.take(Sum.ORDER[idx - 1])
    low_sum.take(Sum.ORDER[-1])

    def weight_grad(left, right, out, first_row):
        def one(m, c):
            cols = pl.ds(pl.multiple_of(m * 256, 256), 256)
            block = dot(left[...], right[:, :, :, cols].reshape(CUBE * rows, 256))
            out[first_row : first_row + UNITS, cols] = block.astype(BF16)
            return c

        lax.fori_loop(0, width // 256, one, 0)

    weight_grad(hidden, wide_g, grads_d, 0)
    if in_kernel:
        back_d = Back(n, grads_d, tiles_d, back_d_sem)
        back_g = Back(n, w_gu.at[pl.ds(0, UNITS)], tiles_g, back_g_sem)
        tick = Trickle(back_d.trickle())
    else:
        save_d = pltpu.make_async_copy(grads_d, tiles_d, lsem.at[4])
        save_g = pltpu.make_async_copy(w_gu.at[pl.ds(0, UNITS)], tiles_g, lsem.at[7])
        tick = Trickle([save_d])
    low_sum.phase(0, tick)
    weight_grad(d_gate, wide, w_gu, 0)
    low_sum.phase(1, tick)
    weight_grad(d_up, wide, w_gu, UNITS)
    save_u = pltpu.make_async_copy(w_gu.at[pl.ds(UNITS, UNITS)], grads_u, lsem.at[3])
    save_u.start()
    tick.flush()
    low_sum.close()
    low_sum.finish()
    load_mid.wait()

    gain_two = w_ref[161:162, :].astype(F32)
    for h in range(2):

        def norm_back_two(at):
            mid = d_mid[h, at]
            root = lax.rsqrt(jnp.mean(mid * mid, axis=-1, keepdims=True) + EPS)
            normed = mid * root
            scaled = total[h, at] * gain_two
            grad = wide_g[j, h, at].astype(F32) + root * (
                scaled - normed * jnp.mean(scaled * normed, axis=-1, keepdims=True)
            )
            d_mid[h, at] = grad
            own[h, at] = grad.astype(BF16)

        row_loop(half, 16, norm_back_two)

    tick = Trickle(back_g.trickle() if in_kernel else [save_g])
    out_sum = Sum(part, heap, total, out_sem)
    waiting = list(Sum.ORDER)
    crossing = []

    def out_block():
        if waiting:
            r = waiting.pop(0)
            jj = flip(j, r)
            at = pl.ds(pl.multiple_of(jj * rows, rows), rows)
            for col in range(0, width, 512):
                cols = pl.ds(col, 512)
                part[jj, :, :, cols] = dot_tn(hidden[:, at], down[:, cols]).astype(BF16).reshape(2, half, 512)
            out_sum.send(r)
            crossing.append(r)
        if len(crossing) > 1 or crossing and not waiting:
            out_sum.take(crossing.pop(0), leave=False)

    def between():
        tick(2)
        out_block()

    for r in Gather(own, wide_g, attn_sem, UP_FIRST, HALVES).blocks(between):
        jj = flip(j, r)
        at = pl.ds(pl.multiple_of(jj * rows, rows), rows)
        dy_ref[at, :] = dot_nt(wide_g[jj].reshape(rows, width), wo_ref[...]).astype(BF16)
    tick.flush()
    while waiting or crossing:
        out_block()
    out_sum.crossed()
    save_half = pltpu.make_async_copy(part.at[:, t], out_half, lsem.at[8])
    save_half.start()

    def output_grad(m, c):
        cols = pl.ds(pl.multiple_of(m * 256, 256), 256)
        block = dot(y_turned[...], wide_g[:, :, :, cols].reshape(CUBE * rows, 256))
        grads_o[:, cols] = block.astype(BF16)
        return c

    lax.fori_loop(0, width // 256, output_grad, 0)
    save_u.wait()
    save_half.wait()
    if in_kernel:
        back_d.finish()
        back_g.finish()
    else:
        save_d.wait()
        save_g.wait()


def mlp_call(n, own, w_a, w_o, y_turned, mid, w_gu, pack_d, cot_all):
    half, width = own.shape[1:]
    count = CUBE * 2 * half
    vm = pl.BlockSpec(memory_space=pltpu.VMEM)
    any_space = pl.BlockSpec(memory_space=pl.ANY)
    if width // n % 128:
        pack_d = spread_call(n, pack_d, width, 6)
    shape = (CUBE, 2, half, width)
    tiles = (UNITS, width) if width // n % 128 else (n, UNITS, width // n)
    return pl.pallas_call(
        functools.partial(mlp_with_own, n),
        out_shape=[
            jax.ShapeDtypeStruct((UNITS, width), BF16),
            jax.ShapeDtypeStruct(tiles, BF16),
            jax.ShapeDtypeStruct(tiles, BF16),
            jax.ShapeDtypeStruct((CUBE, half, width), BF16),
            jax.ShapeDtypeStruct((128, width), BF16),
            jax.ShapeDtypeStruct((2, half, width), F32),
            jax.ShapeDtypeStruct((count, 128), BF16),
        ],
        in_specs=[any_space, vm, vm, vm] + [any_space] * 4,
        out_specs=[any_space] * 4 + [vm] * 3,
        scratch_shapes=[
            pltpu.VMEM((2, half, width), BF16),
            pltpu.VMEM(shape, BF16),
            pltpu.VMEM(shape, BF16),
            pltpu.VMEM(shape, BF16),
            pltpu.VMEM((15, half, width), BF16),
            pltpu.VMEM((2, half, width), F32),
            pltpu.VMEM((2 * UNITS, width), BF16),
            pltpu.VMEM((UNITS, count), BF16),
            pltpu.VMEM((UNITS, width), BF16),
            pltpu.VMEM((UNITS, count), BF16),
            pltpu.VMEM((UNITS, count), BF16),
            pltpu.VMEM((UNITS, count), BF16),
            pltpu.VMEM((UNITS, count), BF16),
            pltpu.VMEM((UNITS, width), BF16),
            pltpu.SemaphoreType.DMA((9,)),
            *gather_sems(),
            *gather_sems(),
            *sum_sems(),
            *sum_sems(),
            *spread_sems(n),
            *spread_sems(n),
            *spread_sems(n),
        ],
        compiler_params=pltpu.CompilerParams(collective_id=3, has_side_effects=True, vmem_limit_bytes=63 * MIB),
    )(own, w_a, w_o, y_turned, mid, w_gu, pack_d, cot_all)


def mlp_with_own(n, own_hbm, w_ref, wo_ref, y_turned, mid_hbm, w_hbm, pack_d, cot_hbm, *rest):
    outs, (own, *scratch) = rest[:7], rest[7:]
    lsem = scratch[13]
    load = pltpu.make_async_copy(own_hbm, own, lsem.at[5])
    load.start()
    load.wait()
    mlp_kernel(n, own, w_ref, wo_ref, y_turned, mid_hbm, w_hbm, pack_d, cot_hbm, *outs, *scratch)


def tail_kernel(
    n, lengths, q_ref, k_ref, v_ref, y_ref, den_ref, state_ref, w_ref, tok_ref, dy_ref, grads_o,
    out_half, mid, d_mid, low_hbm, grads_b, first, second, third,
    output_ref, grad_ref, tiles_b, tiles_a,
    part, heap_a, heap_b, wide, total, c_ref, c_kept, v_kept, side, dv, turned, dqkv, grads_a,
    state_mine, state_theirs, xsend, xrecv, lsem, *sems,
):
    groups = n // CUBE
    s, t, j, base = whereabouts()
    tokens = q_ref.shape[0]
    rows = tokens // CUBE
    half = rows // 2
    width = w_ref.shape[1]
    two, three = lengths[0], lengths[0] + lengths[1]
    start = base * rows
    in_kernel = len(tiles_a.shape) == 3
    sum_out, sum_one, bsems, asems = sems[0:6], sems[6:12], sems[12:15], sems[15:18]

    load_low = pltpu.make_async_copy(low_hbm, wide, lsem.at[2])
    load_low.start()
    load_mid = pltpu.make_async_copy(mid, grad_ref, lsem.at[0])
    load_mid.start()
    load_out = pltpu.make_async_copy(out_half, part.at[:, t], lsem.at[4])
    load_out.start()
    greet_all(n)
    out_sum = Sum(part, heap_b, total, sum_out, UP_LAST, HALVES)
    back_b = Back(n, grads_b, tiles_b, bsems) if in_kernel else None

    tick = Trickle(back_b.trickle()) if in_kernel else Trickle([])

    state_mine[...] = jnp.zeros_like(state_mine)
    state = state_ref[...].astype(BF16)
    blocks = tokens // BLOCK

    def early(tb, carry):
        tq = pl.ds(pl.multiple_of(tb * BLOCK, BLOCK), BLOCK)
        _, seg = segments(two, three, start + tb * BLOCK, BLOCK, 0)
        keep = (seg == 1).astype(F32)
        c = (dy_ref[tq, :].astype(F32) / den_ref[tq, 0:1]).astype(BF16)
        m = -jnp.sum(c.astype(F32) * y_ref[tq, :], axis=-1, keepdims=True)
        m_high = m.astype(BF16).astype(F32)
        lane = lax.broadcasted_iota(jnp.int32, (BLOCK, 128), 1)
        extra = jnp.where(lane == 0, m_high, jnp.where(lane == 1, m - m_high, 0.0)).astype(BF16)
        c_ext = jnp.concatenate([c, extra], axis=1)
        c_ref[tq, :] = c_ext
        c_kept[tq, :] = c_ext * keep.astype(BF16)
        v_kept[tq, :] = v_ref[tq, :] * keep.astype(BF16)
        u = q_ref[tq, :]
        quad, line = lift(u, keep, first[...], second[...], third[...])
        state_mine[0:256, :] += dot_tn(quad, c_ext)
        state_mine[256:384, :] += dot_tn(line, c_ext)
        d_quad = dot_nt(c_ext, state[0:256]) * keep
        d_line = dot_nt(c_ext, state[256:384]) * keep
        side[tq, 0:FEAT] = lift_back(u, d_quad, d_line, first[...], second[...])
        return carry

    load_out.wait()
    for r in Sum.ORDER:
        out_sum.leave(r)
    tick(4)
    lax.fori_loop(0, blocks, early, 0)
    done = exchange(groups, state_mine, state_theirs, xsend, xrecv, False)
    for tb in range(blocks):
        tq = pl.ds(tb * BLOCK, BLOCK)
        qt = q_ref[tq, :] * BF16(0.25)
        score = dot_nt(qt, k_ref[tq, :])
        mask = pair_mask(two, three, start + tb * BLOCK, start + tb * BLOCK, BLOCK)
        grad = jnp.where(mask, dot_nt(c_ref[tq, :], v_ref[tq, :]) * (1.0 + score), 0.0).astype(BF16)
        acc = dot(grad, k_ref[tq, :])
        for lo in range(0, tb * BLOCK, 512):
            sq = pl.ds(lo, min(512, tb * BLOCK - lo))
            score = dot_nt(qt, k_ref[sq, :])
            grad = (dot_nt(c_kept[tq, :], v_kept[sq, :]) * (1.0 + score)).astype(BF16)
            acc = acc + dot(grad, k_ref[sq, :])
        side[tq, 0:FEAT] = (side[tq, 0:FEAT] + acc * 0.5) * 0.5
        tick()
    out_sum.phase(0)
    for sb in range(blocks):
        sq = pl.ds(sb * BLOCK, BLOCK)
        ks = k_ref[sq, :] * BF16(0.25)
        score = dot_nt(ks, q_ref[sq, :])
        mask = pair_mask_turned(two, three, start + sb * BLOCK, start + sb * BLOCK, BLOCK)
        grad = jnp.where(mask, dot_nt(v_ref[sq, :], c_ref[sq, :]) * (1.0 + score), 0.0).astype(BF16)
        weight = jnp.where(mask, pair_weight(score), 0.0).astype(BF16)
        acc = dot(grad, q_ref[sq, :])
        near = dot(weight, c_ref[sq, :])
        far = jnp.zeros((BLOCK, 256), F32)
        for lo in range((sb + 1) * BLOCK, tokens, 512):
            tq = pl.ds(lo, min(512, tokens - lo))
            score = dot_nt(ks, q_ref[tq, :])
            grad = (dot_nt(v_kept[sq, :], c_kept[tq, :]) * (1.0 + score)).astype(BF16)
            acc = acc + dot(grad, q_ref[tq, :])
            far = far + dot(pair_weight(score).astype(BF16), c_kept[tq, :])
        _, seg = segments(two, three, start + sb * BLOCK, BLOCK, 0)
        side[sq, FEAT : 2 * FEAT] = acc * 0.5
        dv[sq, :] = (near + far * (seg == 1).astype(F32))[:, :128]
        tick()
        if sb == blocks // 2:
            out_sum.phase(1)
    tick.flush()
    out_sum.close()
    state_back = done().astype(BF16)

    def late(sb, carry):
        sq = pl.ds(pl.multiple_of(sb * BLOCK, BLOCK), BLOCK)
        _, seg = segments(two, three, start + sb * BLOCK, BLOCK, 0)
        keep = (seg == 1).astype(F32)
        u = k_ref[sq, :]
        v = v_ref[sq, :]
        quad, line = lift(u, keep, first[...], second[...], third[...])
        d_quad = dot_nt(v, state_back[0:256]) * keep
        d_line = dot_nt(v, state_back[256:384]) * keep
        more = dot(quad, state_back[0:256]) + dot(line, state_back[256:384])
        dk = (side[sq, FEAT : 2 * FEAT] + lift_back(u, d_quad, d_line, first[...], second[...])) * 0.5
        dqkv[sq, 0:128] = (dv[sq, :] + more[:, :128]).astype(BF16)
        packed = dot(side[sq, 0:FEAT].astype(BF16), third[...]) + dot(dk.astype(BF16), third_shifted(third[...]))
        dqkv[sq, 128:256] = packed.astype(BF16)
        turned[:, sq] = dqkv[sq, :].T
        return carry

    lax.fori_loop(0, blocks, late, 0)
    out_sum.finish(crossed=True)
    load_mid.wait()
    for h in range(2):

        def finish_output(at):
            output_ref[h, at] = (grad_ref[h, at] + total[h, at]).astype(BF16)

        row_loop(half, 16, finish_output)
    load_mid = pltpu.make_async_copy(d_mid, grad_ref, lsem.at[1])
    load_mid.start()

    load_low.wait()
    one_sum = Sum(part, heap_a, total, sum_one)
    w_one = w_ref[0:160, :]
    for idx, r in enumerate(Sum.ORDER):
        jj = flip(j, r)
        for h in range(2):
            at = pl.ds(pl.multiple_of(jj * rows + h * half, half), half)
            part[jj, h] = dot(dqkv[at, 0:160], w_one).astype(BF16)
        one_sum.send(r)
        if idx:
            one_sum.take(Sum.ORDER[idx - 1])
    one_sum.take(Sum.ORDER[-1])

    def one_grad(m, c):
        cols = pl.ds(pl.multiple_of(m * 256, 256), 256)
        block = dot(turned[0:160, :], wide[:, :, :, cols].reshape(tokens, 256))
        grads_a[0:160, cols] = block.astype(BF16)
        return c

    lax.fori_loop(0, width // 256, one_grad, 0)
    grads_a[160:288, :] = grads_o[...]
    if in_kernel:
        back_a = Back(n, grads_a, tiles_a, asems)
        back_a.start()
    else:
        copy = pltpu.make_async_copy(grads_a, tiles_a, lsem.at[3])
        copy.start()
    one_sum.phase(0)
    one_sum.phase(1)
    one_sum.close()
    one_sum.finish()

    gain_one = w_ref[160:161, :].astype(F32)
    load_mid.wait()
    for h in range(2):

        def norm_back_one(at):
            x = tok_ref[h, at].astype(F32)
            root = lax.rsqrt(jnp.mean(x * x, axis=-1, keepdims=True) + EPS)
            normed = x * root
            scaled = total[h, at] * gain_one
            grad_ref[h, at] = grad_ref[h, at] + root * (
                scaled - normed * jnp.mean(scaled * normed, axis=-1, keepdims=True)
            )

        row_loop(half, 16, norm_back_one)

    if in_kernel:
        back_b.finish()
        back_a.finish()
    else:
        copy.wait()


def third_shifted(third):
    return jnp.concatenate([jnp.zeros_like(third[:, :FEAT]), third[:, : 128 - FEAT]], axis=1)


def tail_call(n, lengths, q, k, v, y, den, state, w_a, mid, tokens, d_mid, dy, grads_o, out_half, low_one, grads_b):
    groups = n // CUBE
    _, half, width = mid.shape
    rows = 2 * half
    count = CUBE * rows
    wide_columns = width // n % 128 == 0
    vm = pl.BlockSpec(memory_space=pltpu.VMEM)
    any_space = pl.BlockSpec(memory_space=pl.ANY)
    peers = max(groups - 1, 1)
    out_shape = [
        jax.ShapeDtypeStruct((2, half, width), BF16),
        jax.ShapeDtypeStruct((2, half, width), F32),
        jax.ShapeDtypeStruct((n, grads_b.shape[0], width // n) if wide_columns else (8, 128), BF16),
        jax.ShapeDtypeStruct((n, 288, width // n) if wide_columns else (288, width), BF16),
    ]
    output, grad, tiles_b, tiles_a = pl.pallas_call(
        functools.partial(tail_kernel, n),
        out_shape=out_shape,
        in_specs=[pl.BlockSpec(memory_space=pltpu.SMEM)] + [vm] * 10 + [any_space] * 5 + [vm] * 3,
        out_specs=[vm, vm, any_space, any_space],
        scratch_shapes=[
            pltpu.VMEM((CUBE, 2, half, width), BF16),
            pltpu.VMEM((15, half, width), BF16),
            pltpu.VMEM((15, half, width), BF16),
            pltpu.VMEM((CUBE, 2, half, width), BF16),
            pltpu.VMEM((2, half, width), F32),
            pltpu.VMEM((count, 256), BF16),
            pltpu.VMEM((count, 256), BF16),
            pltpu.VMEM((count, 256), BF16),
            pltpu.VMEM((count, 128), F32),
            pltpu.VMEM((count, 128), F32),
            pltpu.VMEM((256, count), BF16),
            pltpu.VMEM((count, 256), BF16),
            pltpu.VMEM((288, width), BF16),
            pltpu.VMEM((384, 256), F32),
            pltpu.VMEM((peers, 384, 256), F32),
            pltpu.SemaphoreType.DMA((peers,)),
            pltpu.SemaphoreType.DMA((peers,)),
            pltpu.SemaphoreType.DMA((5,)),
            *sum_sems(),
            *sum_sems(),
            *spread_sems(n),
            *spread_sems(n),
        ],
        compiler_params=pltpu.CompilerParams(collective_id=2, has_side_effects=True, vmem_limit_bytes=63 * MIB),
    )(
        lengths, q, k, v, y, den, state, w_a, tokens.reshape(2, half, width), dy, grads_o,
        out_half, mid, d_mid, low_one, grads_b, *spreaders(),
    )
    if not wide_columns:
        tiles_b = back_call(n, grads_b, 9)
        tiles_a = back_call(n, tiles_a, 10)
    return output.reshape(rows, width), grad.reshape(rows, width), tiles_b, tiles_a


def units_first(w):
    return jnp.pad(w, ((0, CUBE * UNITS - w.shape[0]), (0, 0))).reshape(CUBE, UNITS, w.shape[1])


def body(
    n, tokens, gain_attn, w_query, w_key, w_value, w_output, gain_mlp, w_gate, w_up, w_down, seq_lengths, cotangent
):
    per = HEADS // lax.axis_size("tensor")
    gains = jnp.concatenate([gain_attn[None], gain_mlp[None], jnp.zeros((14, gain_attn.shape[0]), BF16)], axis=0)
    pack_a = jnp.concatenate(
        [
            w_value.T.reshape(per, 128, -1),
            w_query.T.reshape(per, FEAT, -1),
            w_key.T.reshape(per, FEAT, -1),
            jnp.broadcast_to(gains[None], (per, *gains.shape)),
        ],
        axis=1,
    )
    pack_o = w_output.reshape(per, 128, -1)
    pack_b = jnp.concatenate([units_first(w_gate.T), units_first(w_up.T)], axis=1)
    w_a, w_o, w_gu, cot_all, low_one, low_two, mid, q, k, v, y, y_turned, den, state = head_call(
        n, seq_lengths, pack_a, pack_o, pack_b, tokens, cotangent
    )
    grads_u, tiles_d, tiles_g, out_half, grads_o, d_mid, dy = mlp_call(
        n, low_two, w_a, w_o, y_turned, mid, w_gu, units_first(w_down), cot_all
    )
    if tiles_d.ndim == 2:
        tiles_d, tiles_g = back_call(n, tiles_d, 7), back_call(n, tiles_g, 8)
    output, grad_tokens, tiles_u, tiles_a = tail_call(
        n, seq_lengths, q, k, v, y, den, state, w_a, mid, tokens, d_mid, dy, grads_o, out_half, low_one, grads_u
    )

    def arrived(tiles):
        return tiles.reshape(-1, CUBE, *tiles.shape[1:]).astype(F32).sum(axis=0)

    back_g, back_u, back_d, back_a = arrived(tiles_g), arrived(tiles_u), arrived(tiles_d), arrived(tiles_a)

    def units(part):
        return part.reshape(CUBE * UNITS, -1)[: w_gate.shape[1]]

    grad_gate = units(back_g).T
    grad_up = units(back_u).T
    grad_down = units(back_d)
    grad_value = back_a[:, 0:128].reshape(per * 128, -1).T
    grad_query = back_a[:, 128:144].reshape(per * FEAT, -1).T
    grad_key = back_a[:, 144:160].reshape(per * FEAT, -1).T
    grad_output = back_a[:, 160:288].reshape(per * 128, -1)

    def weighed(*pairs):
        return sum(jnp.sum(w.astype(F32) * g, axis=1) for w, g in pairs)

    gain_one_part = weighed((w_value, grad_value), (w_query, grad_query), (w_key, grad_key))
    gain_two_part = weighed((w_gate, grad_gate), (w_up, grad_up))
    both = lax.psum(jnp.stack([gain_one_part, gain_two_part]), "tensor")
    grad_gain_one = both[0] / gain_attn.astype(F32)
    grad_gain_two = both[1] / gain_mlp.astype(F32)
    return (
        output,
        grad_tokens,
        grad_gain_one,
        grad_query,
        grad_key,
        grad_value,
        grad_output,
        grad_gain_two,
        grad_gate,
        grad_up,
        grad_down,
    )


def solution(mesh):
    return jax.shard_map(
        functools.partial(body, mesh.shape["seq"]),
        mesh=mesh,
        in_specs=(
            P("seq", None),
            P("seq"),
            P("seq", "tensor"),
            P("seq", "tensor"),
            P("seq", "tensor"),
            P("tensor", "seq"),
            P("seq"),
            P("seq", "tensor"),
            P("seq", "tensor"),
            P("tensor", "seq"),
            P(),
            P("seq", None),
        ),
        out_specs=(
            P("seq", None),
            P("seq", None),
            P("seq"),
            P("seq", "tensor"),
            P("seq", "tensor"),
            P("seq", "tensor"),
            P("tensor", "seq"),
            P("seq"),
            P("seq", "tensor"),
            P("seq", "tensor"),
            P("tensor", "seq"),
        ),
        check_vma=False,
    )
```

```python
import functools

import jax
import jax.numpy as jnp
import numpy as np
from jax import lax
from jax.experimental import pallas as pl
from jax.experimental.pallas import tpu as pltpu
from jax.sharding import PartitionSpec as P

MESH = pl.DeviceIdType.MESH
HEADS = 16
FEAT = 16
CUBE = 8
UNITS = 352
EPS = 1e-06
F32 = jnp.float32
BF16 = jnp.bfloat16
ORDERS = ((0, 1, 2), (1, 2, 0), (2, 0, 1))
PIECES = ((0, 48), (48, 48), (96, 32))
WAVES = ((4, 1, 2), (6, 5, 3), (7,))
UP_FIRST = ((2, 0, 1), (2, 1, 0))
UP_LAST = ((0, 1, 2), (1, 0, 2))
HALVES = ((0, 64), (64, 64))
MIB = 1 << 20


def flip(place, mask):
    total = 0
    for b in range(3):
        bit = (place // (1 << b)) % 2
        total = total + ((1 - bit) if (mask >> b) & 1 else bit) * (1 << b)
    return total


def subsets(dims):
    out = [0]
    for d in dims:
        out = out + [r | (1 << d) for r in out]
    return out


def whereabouts():
    s = lax.axis_index("seq")
    t = lax.axis_index("tensor")
    j = s % CUBE
    return s, t, j, s - j


def remote(src, dst, send, recv, device):
    return pltpu.make_async_remote_copy(
        src_ref=src, dst_ref=dst, send_sem=send, recv_sem=recv, device_id=device, device_id_type=MESH
    )


def greet(devices):
    barrier = pltpu.get_barrier_semaphore()
    for device in devices:
        pl.semaphore_signal(barrier, inc=1, device_id=device, device_id_type=MESH)
    pl.semaphore_wait(barrier, len(devices))


def near():
    s, t, j, base = whereabouts()
    return [(base + flip(j, 1 << d), t) for d in range(3)] + [(s, 1 - t)]


def greet_all(n):
    s, t, _, _ = whereabouts()
    barrier = pltpu.get_barrier_semaphore()

    def one(k, carry):
        pl.semaphore_signal(barrier, inc=1, device_id=((s + k) % n, t), device_id_type=MESH)
        return carry

    lax.fori_loop(1, n, one, 0)
    pl.semaphore_signal(barrier, inc=1, device_id=(s, 1 - t), device_id_type=MESH)
    pl.semaphore_wait(barrier, n)


class Gather:
    def __init__(self, own, full, sems, orders=ORDERS, pieces=PIECES):
        self.own, self.full, self.orders, self.pieces = own, full, orders, pieces
        self.ssem, self.rsem, self.csend, self.crecv, self.lsem = sems
        self.s, self.t, self.j, self.base = whereabouts()

    def view(self, r, i):
        off, rows = self.pieces[i]
        return self.full.at[flip(self.j, r), self.t, pl.ds(off, rows)]

    def hop(self, p, i, r):
        d = self.orders[i][p]
        off, rows = self.pieces[i]
        src = self.own.at[self.t, pl.ds(off, rows)] if r == 0 else self.view(r, i)
        k = r | (1 << d)
        return remote(src, self.view(r, i), self.ssem.at[i, k], self.rsem.at[i, k], (self.base + flip(self.j, 1 << d), self.t))

    def came(self, i, k):
        p = max(q for q in range(3) if k >> self.orders[i][q] & 1)
        return p, k ^ (1 << self.orders[i][p])

    def arrival(self, i, k):
        p, _ = self.came(i, k)
        device = (self.base + flip(self.j, 1 << self.orders[i][p]), self.t)
        return remote(self.view(k, i), self.view(k, i), self.ssem.at[i, k], self.rsem.at[i, k], device)

    def across(self, r, mine):
        ref = self.full.at[flip(self.j, r), self.t if mine else 1 - self.t]
        return remote(ref, ref, self.csend.at[r], self.crecv.at[r], (self.s, 1 - self.t))

    def local(self):
        return pltpu.make_async_copy(self.own, self.full.at[self.j], self.lsem)

    def start(self):
        self.local().start()
        for q in range(3):
            for i in range(len(self.pieces)):
                self.hop(q, i, 0).start()

    def arrived(self, k):
        for i in range(len(self.pieces)):
            p, _ = self.came(i, k)
            self.arrival(i, k).wait_recv()
            for q in range(p + 1, 3):
                self.hop(q, i, k).start()
        self.across(k, True).start()

    def wave(self, w, tick=lambda: None):
        for k in WAVES[w]:
            self.arrived(k)
            tick()

    def settle(self, r):
        self.across(r, False).wait_recv()

    def sent(self):
        for k in range(1, CUBE):
            self.across(k, True).wait_send()
            for i in range(len(self.pieces)):
                p, r = self.came(i, k)
                self.hop(p, i, r).wait_send()

    def finish(self):
        for r in range(1, CUBE):
            self.settle(r)
        self.sent()
        self.local().wait()

    def blocks(self, tick=lambda: None):
        self.start()
        self.local().wait()
        yield 0
        before = None
        for k in WAVES[0] + WAVES[1] + WAVES[2]:
            self.arrived(k)
            tick()
            if before:
                self.settle(before)
                yield before
            before = k
        self.settle(before)
        yield before
        self.sent()


def gather_sems():
    return [pltpu.SemaphoreType.DMA((3, CUBE))] * 2 + [pltpu.SemaphoreType.DMA((CUBE,))] * 2 + [pltpu.SemaphoreType.DMA]


SLOT = {0: 0, 1: 4, 2: 6}


def slot_of(order, p, r):
    return SLOT[p] + subsets(order[p + 1 :]).index(r)


class Sum:
    ORDER = (7, 6, 5, 3, 4, 2, 1, 0)

    def __init__(self, part, heap, total, sems, orders=ORDERS, pieces=PIECES):
        self.part, self.heap, self.total = part, heap, total
        self.orders, self.pieces = orders, pieces
        self.csend, self.crecv, self.ssem, self.rsem, self.fsend, self.frecv = sems
        self.s, self.t, self.j, self.base = whereabouts()

    def across(self, r):
        src = self.part.at[flip(self.j, r), 1 - self.t]
        return remote(src, self.heap.at[r], self.csend.at[r], self.crecv.at[r], (self.s, 1 - self.t))

    def hop(self, p, i, r):
        d = self.orders[i][p]
        off, rows = self.pieces[i]
        k = slot_of(self.orders[i], p, r ^ (1 << d))
        return remote(
            self.part.at[flip(self.j, r), self.t, pl.ds(off, rows)],
            self.heap.at[CUBE + k, pl.ds(off, rows)],
            self.ssem.at[i, k],
            self.rsem.at[i, k],
            (self.base + flip(self.j, 1 << d), self.t),
        )

    def send(self, r):
        self.across(r).start()

    def take(self, r, leave=True):
        self.across(r).wait_recv()
        jj = flip(self.j, r)
        step = 32

        def one(m, c):
            at = pl.ds(pl.multiple_of(m * step, step), step)
            self.part[jj, self.t, at] = (
                self.part[jj, self.t, at].astype(F32) + self.heap[r, at].astype(F32)
            ).astype(BF16)
            return c

        lax.fori_loop(0, self.part.shape[2] // step, one, 0)
        if leave:
            self.leave(r)

    def leave(self, r):
        for i in range(len(self.pieces)):
            if r >> self.orders[i][0] & 1 and r != 1 << self.orders[i][0]:
                self.hop(0, i, r).start()

    def phase(self, p, tick=lambda: None):
        count = len(self.pieces)
        for i, r in [(i, subsets(self.orders[i][p + 1 :])[-1 - m]) for m in range((4 >> p) - 1) for i in range(count)]:
            d = self.orders[i][p]
            off, rows = self.pieces[i]
            self.hop(p, i, r | (1 << d)).wait_recv()
            jj = flip(self.j, r)
            k = slot_of(self.orders[i], p, r)
            for q in range(0, rows, 16):
                at = pl.ds(off + q, 16)
                new = self.part[jj, self.t, at].astype(F32) + self.heap[CUBE + k, at].astype(F32)
                self.part[jj, self.t, at] = new.astype(BF16)
            e = self.orders[i][p + 1]
            if r >> e & 1 and (p == 1 or r != 1 << e):
                self.hop(p + 1, i, r).start()
            tick()
        for i in range(count):
            self.hop(p, i, 1 << self.orders[i][p]).start()

    def close(self, tick=lambda: None):
        for i in range(len(self.pieces)):
            off, rows = self.pieces[i]
            for p in range(3):
                self.hop(p, i, 1 << self.orders[i][p]).wait_recv()
            slots = [CUBE + slot_of(self.orders[i], p, 0) for p in range(3)]
            for q in range(0, rows, 16):
                at = pl.ds(off + q, 16)
                new = self.part[self.j, self.t, at].astype(F32)
                for k in slots:
                    new = new + self.heap[k, at].astype(F32)
                self.total[self.t, at] = new
            tick()
        self.trade()

    def both(self, half):
        ref = self.total.at[half]
        return remote(ref, ref, self.fsend, self.frecv, (self.s, 1 - self.t))

    def trade(self):
        self.both(self.t).start()

    def crossed(self):
        for r in range(CUBE):
            self.across(r).wait_send()

    def finish(self, crossed=False):
        self.both(1 - self.t).wait_recv()
        self.both(self.t).wait_send()
        if not crossed:
            self.crossed()
        for p in range(3):
            for i in range(len(self.pieces)):
                d = self.orders[i][p]
                for r in subsets(self.orders[i][p + 1 :]):
                    self.hop(p, i, r | (1 << d)).wait_send()

    def run(self):
        for r in self.ORDER:
            self.send(r)
        for r in self.ORDER:
            self.take(r)
        self.phase(0)
        self.phase(1)
        self.close()
        self.finish()


def sum_sems():
    return [
        pltpu.SemaphoreType.DMA((CUBE,)),
        pltpu.SemaphoreType.DMA((CUBE,)),
        pltpu.SemaphoreType.DMA((3, CUBE)),
        pltpu.SemaphoreType.DMA((3, CUBE)),
        pltpu.SemaphoreType.DMA,
        pltpu.SemaphoreType.DMA,
    ]


def columns_of(ref, s):
    if len(ref.shape) == 3:
        return ref.at[s]
    return ref.at[:, pl.ds(pl.multiple_of(s * 128, 128), 128)]


def columns_apart(n, rows, width):
    return (rows, width) if width // n % 128 == 0 else (n, rows, width // n)


def together(x):
    return x if x.ndim == 2 else x.transpose(1, 0, 2).reshape(x.shape[1], -1)


def apart(n, x):
    return x if x.shape[1] // n % 128 == 0 else x.reshape(x.shape[0], n, -1).transpose(1, 0, 2)


class Trickle:
    def __init__(self, copies):
        self.copies = list(copies)

    def __call__(self, count=1):
        for _ in range(min(count, len(self.copies))):
            self.copies.pop(0).start()

    def flush(self):
        self(len(self.copies))


def far_and_near(n):
    near, far = list(range(1, n // 2)), list(range(n // 2, n))
    return [k for pair in zip(far, near + [None]) for k in pair if k is not None]


class Spread:
    def __init__(self, n, pack, full, sems):
        self.n, self.pack, self.full = n, pack, full
        self.ssem, self.rsem, self.lsem = sems
        self.s, self.t, self.j, self.base = whereabouts()

    def columns(self, s):
        return columns_of(self.full, s)

    def copy(self, k):
        to = (self.s + k) % self.n
        return remote(self.pack.at[to % CUBE], self.columns(self.s), self.ssem.at[k], self.rsem.at[k], (to, self.t))

    def arrival(self, k):
        at = (self.s + self.n - k) % self.n
        return remote(self.pack.at[0], self.columns(at), self.ssem.at[k], self.rsem.at[k], (at, self.t))

    def local(self):
        return pltpu.make_async_copy(self.pack.at[self.j], self.columns(self.s), self.lsem)

    def start(self):
        lax.fori_loop(1, self.n, lambda k, c: (self.copy(k).start(), c)[1], 0)
        self.local().start()

    def trickle(self):
        return [self.local()] + [self.copy(k) for k in far_and_near(self.n)]

    def finish(self):
        self.local().wait()
        lax.fori_loop(1, self.n, lambda k, c: (self.arrival(k).wait_recv(), c)[1], 0)
        lax.fori_loop(1, self.n, lambda k, c: (self.copy(k).wait_send(), c)[1], 0)


class Back:
    def __init__(self, n, grads, tiles, sems):
        self.n, self.grads, self.tiles = n, grads, tiles
        self.ssem, self.rsem, self.lsem = sems
        self.s, self.t, self.j, self.base = whereabouts()

    def columns(self, s):
        return columns_of(self.grads, s)

    def copy(self, k):
        to = (self.s + k) % self.n
        return remote(self.columns(to), self.tiles.at[self.s], self.ssem.at[k], self.rsem.at[k], (to, self.t))

    def arrival(self, k):
        at = (self.s + self.n - k) % self.n
        return remote(self.tiles.at[at], self.tiles.at[at], self.ssem.at[k], self.rsem.at[k], (at, self.t))

    def local(self):
        return pltpu.make_async_copy(self.columns(self.s), self.tiles.at[self.s], self.lsem)

    start = Spread.start
    trickle = Spread.trickle
    finish = Spread.finish


def spread_sems(n):
    return [pltpu.SemaphoreType.DMA((n,)), pltpu.SemaphoreType.DMA((n,)), pltpu.SemaphoreType.DMA]


def spread_kernel(n, pack, full, *sems):
    greet_all(n)
    spread = Spread(n, pack, full, sems)
    spread.start()
    spread.finish()


def spread_call(n, pack, width, number):
    any_space = pl.BlockSpec(memory_space=pl.ANY)
    full = pl.pallas_call(
        functools.partial(spread_kernel, n),
        out_shape=jax.ShapeDtypeStruct(columns_apart(n, pack.shape[1], width), BF16),
        in_specs=[any_space],
        out_specs=any_space,
        scratch_shapes=spread_sems(n),
        compiler_params=pltpu.CompilerParams(collective_id=number, has_side_effects=True),
    )(pack)
    return together(full)


def back_kernel(n, grads, tiles, *sems):
    greet_all(n)
    back = Back(n, grads, tiles, sems)
    back.start()
    back.finish()


def back_call(n, grads, number):
    rows, width = grads.shape
    any_space = pl.BlockSpec(memory_space=pl.ANY)
    return pl.pallas_call(
        functools.partial(back_kernel, n),
        out_shape=jax.ShapeDtypeStruct((n, rows, width // n), BF16),
        in_specs=[any_space],
        out_specs=any_space,
        scratch_shapes=spread_sems(n),
        compiler_params=pltpu.CompilerParams(collective_id=number, has_side_effects=True),
    )(apart(n, grads))


def dot(a, b):
    return jnp.dot(a, b, preferred_element_type=F32)


def dot_nt(a, b):
    return lax.dot_general(a, b, (((1,), (1,)), ((), ())), preferred_element_type=F32)


def dot_tn(a, b):
    return lax.dot_general(a, b, (((0,), (0,)), ((), ())), preferred_element_type=F32)


def spreaders():
    first = np.repeat(np.eye(FEAT), FEAT, axis=1)
    second = np.tile(np.eye(FEAT), (1, FEAT))
    third = np.eye(FEAT, 128)
    return [jnp.asarray(m, BF16) for m in (first, second, third)]


ROOT_HALF = 0.5**0.5


def lift(u, keep, first, second, third):
    quad = dot(u, first) * dot(u, second) * (0.25 * ROOT_HALF) * keep
    lane = lax.broadcasted_iota(jnp.int32, (u.shape[0], 128), 1)
    line = (dot(u, third) * 0.5 + jnp.where(lane == FEAT, 1.0, 0.0)) * keep
    return quad.astype(BF16), line.astype(BF16)


def lift_back(u, d_quad, d_line, first, second):
    one, two = dot(u, first) * 0.5, dot(u, second) * 0.5
    back = dot_nt((d_quad * two).astype(BF16), first) + dot_nt((d_quad * one).astype(BF16), second)
    return back * ROOT_HALF + d_line[:, :FEAT]


def two_terms(x):
    high = x.astype(BF16)
    return high, (x - high.astype(F32)).astype(BF16)


def segments(start_two, start_three, first_position, count, axis):
    shape = (count, 1) if axis == 0 else (1, count)
    position = first_position + lax.broadcasted_iota(jnp.int32, shape, axis)
    return position, (position >= start_two).astype(jnp.int32) + (position >= start_three).astype(jnp.int32)


def pair_mask(two, three, at_t, at_s, block):
    pos_t, seg_t = segments(two, three, at_t, block, 0)
    pos_s, seg_s = segments(two, three, at_s, block, 1)
    return (pos_s <= pos_t) & (seg_s == seg_t)


def pair_mask_turned(two, three, at_s, at_t, block):
    pos_s, seg_s = segments(two, three, at_s, block, 0)
    pos_t, seg_t = segments(two, three, at_t, block, 1)
    return (pos_s <= pos_t) & (seg_s == seg_t)


def other_groups(groups):
    s, t, j, base = whereabouts()
    return [((s + CUBE * k) % (CUBE * groups), t) for k in range(1, groups)]


def exchange(groups, mine, theirs, ssem, rsem, before):
    s, t, j, base = whereabouts()
    c = s // CUBE
    for k, device in enumerate(other_groups(groups)):
        remote(mine, theirs.at[k], ssem.at[k], rsem.at[k], device).start()

    def finish():
        total = jnp.zeros(mine.shape, F32)
        for k, device in enumerate(other_groups(groups)):
            remote(mine, theirs.at[k], ssem.at[k], rsem.at[k], device).wait_recv()
            source = (c + groups - (k + 1)) % groups
            counts = (source < c) if before else (source > c)
            total = total + jnp.where(counts, theirs[k], 0.0)
        for k, device in enumerate(other_groups(groups)):
            remote(mine, theirs.at[k], ssem.at[k], rsem.at[k], device).wait_send()
        return total

    return finish


BLOCK = 256


def row_loop(count, step, work):
    def one(m, c):
        work(pl.ds(pl.multiple_of(m * step, step), step))
        return c

    lax.fori_loop(0, count // step, one, 0)


def pair_weight(score):
    return (score * 0.5 + 1.0) * score + 1.0


def head_kernel(
    n, lengths, tok_ref, pack_a, pack_o, pack_b, cot_hbm, first, second, third,
    w_ref, wo_ref, w_b, cot_all, low_hbm, own, mid_ref, q_ref, k_ref, v_ref, y_ref, y_turned, den_ref, state_ref,
    wide, part, heap, total, kept, state_mine, state_theirs, xsend, xrecv, lsem, *sems,
):
    groups = n // CUBE
    s, t, j, base = whereabouts()
    half, width = tok_ref.shape[1:]
    rows = 2 * half
    tokens = CUBE * rows
    two, three = lengths[0], lengths[0] + lengths[1]
    start = base * rows
    in_kernel = len(pack_a.shape) == 3
    sum_sem, tok_sem, cot_sem = sems[0:6], sems[6:11], sems[11:16]
    a_sem, b_sem, o_sem = sems[16:19], sems[19:22], sems[22:25]

    greet_all(n)
    g_tok = Gather(tok_ref, wide, tok_sem)
    g_cot = Gather(cot_hbm, cot_all, cot_sem, UP_FIRST, HALVES)
    if in_kernel:
        spread_a = Spread(n, pack_a, w_ref, a_sem)
        spread_b = Spread(n, pack_b, w_b, b_sem)
        spread_o = Spread(n, pack_o, wo_ref, o_sem)
        spread_a.start()
        tick = Trickle(spread_o.trickle() + spread_b.trickle())
    else:
        copy_a = pltpu.make_async_copy(pack_a, w_ref, lsem.at[CUBE])
        copy_b = pltpu.make_async_copy(pack_b, w_b, lsem.at[CUBE + 1])
        copy_o = pltpu.make_async_copy(pack_o, wo_ref, lsem.at[CUBE + 2])
        copy_a.start()
        tick = Trickle([copy_o, copy_b])
    g_tok.start()
    for w in range(3):
        g_tok.wave(w)
    g_cot.start()
    g_tok.finish()
    if in_kernel:
        spread_a.finish()
    else:
        copy_a.wait()

    state_mine[...] = jnp.zeros_like(state_mine)
    gain_one = w_ref[160:161, :].astype(F32)

    def project(jj, c):
        for h in range(2):

            def norm(at):
                x = wide[jj, h, at].astype(F32)
                root = lax.rsqrt(jnp.mean(x * x, axis=-1, keepdims=True) + EPS)
                wide[jj, h, at] = (x * root * gain_one).astype(BF16)

            row_loop(half, 64, norm)
        at = pl.ds(pl.multiple_of(jj * rows, rows), rows)
        qkv = dot_nt(wide[jj].reshape(rows, width), w_ref[0:160, :]).astype(BF16)
        v, k = qkv[:, 0:128], qkv[:, 144:160]
        lane = lax.broadcasted_iota(jnp.int32, (rows, 128), 1)
        v_ext = jnp.concatenate([v, jnp.where(lane < 2, 1.0, 0.0).astype(BF16)], axis=1)
        q_ref[at, :] = qkv[:, 128:144]
        k_ref[at, :] = k
        v_ref[at, :] = v_ext
        _, seg = segments(two, three, start + jj * rows, rows, 0)
        keep = (seg == 1).astype(F32)
        kept[at, :] = v_ext * keep.astype(BF16)
        quad, line = lift(k, keep, first[...], second[...], third[...])
        state_mine[0:256, :] += dot_tn(quad, v_ext)
        state_mine[256:384, :] += dot_tn(line, v_ext)
        return c

    for jj in range(CUBE):
        tick(2)
        project(jj, 0)
    save = pltpu.make_async_copy(wide, low_hbm, lsem.at[0])
    save.start()
    done = exchange(groups, state_mine, state_theirs, xsend, xrecv, True)
    g_cot.wave(0)

    blocks = tokens // BLOCK
    for tb in range(blocks):
        tq = pl.ds(tb * BLOCK, BLOCK)
        qt = q_ref[tq, :] * BF16(0.25)
        score = dot_nt(qt, k_ref[tq, :])
        mask = pair_mask(two, three, start + tb * BLOCK, start + tb * BLOCK, BLOCK)
        acc = dot(jnp.where(mask, pair_weight(score), 0.0).astype(BF16), v_ref[tq, :])
        if tb:
            _, seg = segments(two, three, start + tb * BLOCK, BLOCK, 0)
            far = jnp.zeros((BLOCK, 256), F32)
            for lo in range(0, tb * BLOCK, 512):
                sq = pl.ds(lo, min(512, tb * BLOCK - lo))
                far = far + dot(pair_weight(dot_nt(qt, k_ref[sq, :])).astype(BF16), kept[sq, :])
            acc = acc + far * (seg == 1).astype(F32)
        y_ref[tq, :] = acc[:, :128]
        den_ref[tq, :] = acc[:, 128:]
        tick(2)

    g_cot.wave(1)
    state = done()
    state_ref[...] = state
    high, lowp = two_terms(state)
    out_sum = Sum(part, heap, total, sum_sem)
    if in_kernel:
        spread_o.finish()
    else:
        copy_o.wait()
    out_w = wo_ref[...]

    for idx, r in enumerate(Sum.ORDER):
        jj = flip(j, r)
        tq = pl.ds(pl.multiple_of(jj * rows, rows), rows)
        _, seg = segments(two, three, start + jj * rows, rows, 0)
        quad, line = lift(q_ref[tq, :], (seg == 1).astype(F32), first[...], second[...], third[...])
        more = dot(quad, high[0:256]) + dot(quad, lowp[0:256]) + dot(line, high[256:384]) + dot(line, lowp[256:384])
        den = den_ref[tq, :] + more[:, 128:]
        den_ref[tq, :] = den
        y = (y_ref[tq, :] + more[:, :128]) / den[:, 0:1]
        y_ref[tq, :] = y
        y_low = y.astype(BF16)
        y_turned[:, tq] = y_low.T
        for h in range(2):
            part[jj, h] = dot(y_low[h * half : (h + 1) * half], out_w).astype(BF16)
        out_sum.send(r)
        tick(1)
        if idx:
            out_sum.take(Sum.ORDER[idx - 1])
    out_sum.take(Sum.ORDER[-1])
    out_sum.phase(0, lambda: tick(1))
    tick.flush()
    out_sum.phase(1)
    out_sum.close()
    out_sum.finish()

    gain_two = w_ref[161:162, :].astype(F32)
    for h in range(2):

        def second_norm(at):
            mid = tok_ref[h, at].astype(F32) + total[h, at]
            mid_ref[h, at] = mid
            root = lax.rsqrt(jnp.mean(mid * mid, axis=-1, keepdims=True) + EPS)
            own[h, at] = (mid * root * gain_two).astype(BF16)

        row_loop(half, 16, second_norm)

    g_cot.wave(2)
    g_cot.finish()
    save.wait()
    if in_kernel:
        spread_b.finish()
    else:
        copy_b.wait()


def head_call(n, lengths, pack_a, pack_o, pack_b, tokens, cot):
    groups = n // CUBE
    rows, width = tokens.shape
    half = rows // 2
    count = CUBE * rows
    vm = pl.BlockSpec(memory_space=pltpu.VMEM)
    any_space = pl.BlockSpec(memory_space=pl.ANY)
    peers = max(groups - 1, 1)
    w_rows = (pack_a.shape[1], pack_b.shape[1])
    if width // n % 128:
        pack_a, pack_b = spread_call(n, pack_a, width, 4), spread_call(n, pack_b, width, 5)
        pack_o = spread_call(n, pack_o, width, 11)
    shape = (CUBE, 2, half, width)
    return pl.pallas_call(
        functools.partial(head_kernel, n),
        out_shape=[
            jax.ShapeDtypeStruct((w_rows[0], width), BF16),
            jax.ShapeDtypeStruct((128, width), BF16),
            jax.ShapeDtypeStruct((w_rows[1], width), BF16),
            jax.ShapeDtypeStruct(shape, BF16),
            jax.ShapeDtypeStruct(shape, BF16),
            jax.ShapeDtypeStruct((2, half, width), BF16),
            jax.ShapeDtypeStruct((2, half, width), F32),
            jax.ShapeDtypeStruct((count, FEAT), BF16),
            jax.ShapeDtypeStruct((count, FEAT), BF16),
            jax.ShapeDtypeStruct((count, 256), BF16),
            jax.ShapeDtypeStruct((count, 128), F32),
            jax.ShapeDtypeStruct((128, count), BF16),
            jax.ShapeDtypeStruct((count, 128), F32),
            jax.ShapeDtypeStruct((384, 256), F32),
        ],
        in_specs=[pl.BlockSpec(memory_space=pltpu.SMEM), vm] + [any_space] * 4 + [vm] * 3,
        out_specs=[vm, vm, any_space, any_space, any_space] + [vm] * 9,
        scratch_shapes=[
            pltpu.VMEM(shape, BF16),
            pltpu.VMEM(shape, BF16),
            pltpu.VMEM((15, half, width), BF16),
            pltpu.VMEM((2, half, width), F32),
            pltpu.VMEM((count, 256), BF16),
            pltpu.VMEM((384, 256), F32),
            pltpu.VMEM((peers, 384, 256), F32),
            pltpu.SemaphoreType.DMA((peers,)),
            pltpu.SemaphoreType.DMA((peers,)),
            pltpu.SemaphoreType.DMA((CUBE + 3,)),
            *sum_sems(),
            *gather_sems(),
            *gather_sems(),
            *spread_sems(n),
            *spread_sems(n),
            *spread_sems(n),
        ],
        compiler_params=pltpu.CompilerParams(collective_id=1, has_side_effects=True, vmem_limit_bytes=62 * MIB),
    )(lengths, tokens.reshape(2, half, width), pack_a, pack_o, pack_b, cot.reshape(2, half, width), *spreaders())


def mlp_kernel(
    n, own, w_ref, wo_ref, y_turned, mid_hbm, w_hbm, pack_d, cot_hbm,
    grads_u, tiles_d, tiles_g, out_half, grads_o, d_mid, dy_ref,
    wide, wide_g, part, heap, total, w_gu, hidden, down, by_gate, by_up, d_gate, d_up, grads_d, lsem, *sems,
):
    s, t, j, base = whereabouts()
    half, width = own.shape[1:]
    rows = 2 * half
    in_kernel = len(pack_d.shape) == 3
    two_sem, attn_sem, low_sem, out_sem = sems[0:5], sems[5:10], sems[10:16], sems[16:22]
    d_sem, back_d_sem, back_g_sem = sems[22:25], sems[25:28], sems[28:31]

    load_w = pltpu.make_async_copy(w_hbm, w_gu, lsem.at[0])
    load_mid = pltpu.make_async_copy(mid_hbm, d_mid, lsem.at[1])
    load_w.start()
    load_mid.start()
    greet_all(n)
    load_cot = pltpu.make_async_copy(cot_hbm, wide_g, lsem.at[6])
    load_cot.start()
    g_two = Gather(own, wide, two_sem)
    if in_kernel:
        spread_d = Spread(n, pack_d, down, d_sem)
        tick = Trickle(spread_d.trickle())
    else:
        copy_d = pltpu.make_async_copy(pack_d, down, lsem.at[2])
        tick = Trickle([copy_d])

    for r in g_two.blocks(lambda: tick(2)):
        if r == 0:
            load_w.wait()
        jj = flip(j, r)
        at = pl.ds(pl.multiple_of(jj * rows, rows), rows)
        low = wide[jj].reshape(rows, width)
        gate = dot_nt(w_gu[0:UNITS, :], low)
        up = dot_nt(w_gu[UNITS:, :], low)
        sigma = jax.nn.sigmoid(gate)
        silu = gate * sigma
        hidden[:, at] = (silu * up).astype(BF16)
        by_gate[:, at] = (up * sigma * (1.0 + gate * (1.0 - sigma))).astype(BF16)
        by_up[:, at] = silu.astype(BF16)
    tick.flush()
    load_cot.wait()
    if in_kernel:
        spread_d.finish()
    else:
        copy_d.wait()

    low_sum = Sum(part, heap, total, low_sem)
    for idx, r in enumerate(Sum.ORDER):
        jj = flip(j, r)
        at = pl.ds(pl.multiple_of(jj * rows, rows), rows)
        grad = dot_nt(down[...], wide_g[jj].reshape(rows, width))
        dg = (grad * by_gate[:, at].astype(F32)).astype(BF16)
        du = (grad * by_up[:, at].astype(F32)).astype(BF16)
        d_gate[:, at] = dg
        d_up[:, at] = du
        for col in range(0, width, 512):
            cols = pl.ds(col, 512)
            block = dot_tn(dg, w_gu[0:UNITS, cols]) + dot_tn(du, w_gu[UNITS:, cols])
            part[jj, :, :, cols] = block.astype(BF16).reshape(2, half, 512)
        low_sum.send(r)
        if idx:
            low_sum.take(Sum.ORDER[idx - 1])
    low_sum.take(Sum.ORDER[-1])

    def weight_grad(left, right, out, first_row):
        def one(m, c):
            cols = pl.ds(pl.multiple_of(m * 256, 256), 256)
            block = dot(left[...], right[:, :, :, cols].reshape(CUBE * rows, 256))
            out[first_row : first_row + UNITS, cols] = block.astype(BF16)
            return c

        lax.fori_loop(0, width // 256, one, 0)

    weight_grad(hidden, wide_g, grads_d, 0)
    if in_kernel:
        back_d = Back(n, grads_d, tiles_d, back_d_sem)
        back_g = Back(n, w_gu.at[pl.ds(0, UNITS)], tiles_g, back_g_sem)
        tick = Trickle(back_d.trickle())
    else:
        save_d = pltpu.make_async_copy(grads_d, tiles_d, lsem.at[4])
        save_g = pltpu.make_async_copy(w_gu.at[pl.ds(0, UNITS)], tiles_g, lsem.at[7])
        tick = Trickle([save_d])
    low_sum.phase(0, tick)
    weight_grad(d_gate, wide, w_gu, 0)
    low_sum.phase(1, tick)
    weight_grad(d_up, wide, w_gu, UNITS)
    save_u = pltpu.make_async_copy(w_gu.at[pl.ds(UNITS, UNITS)], grads_u, lsem.at[3])
    save_u.start()
    tick.flush()
    low_sum.close()
    low_sum.finish()
    load_mid.wait()

    gain_two = w_ref[161:162, :].astype(F32)
    for h in range(2):

        def norm_back_two(at):
            mid = d_mid[h, at]
            root = lax.rsqrt(jnp.mean(mid * mid, axis=-1, keepdims=True) + EPS)
            normed = mid * root
            scaled = total[h, at] * gain_two
            grad = wide_g[j, h, at].astype(F32) + root * (
                scaled - normed * jnp.mean(scaled * normed, axis=-1, keepdims=True)
            )
            d_mid[h, at] = grad
            own[h, at] = grad.astype(BF16)

        row_loop(half, 16, norm_back_two)

    tick = Trickle(back_g.trickle() if in_kernel else [save_g])
    out_sum = Sum(part, heap, total, out_sem)
    waiting = list(Sum.ORDER)
    crossing = []

    def out_block():
        if waiting:
            r = waiting.pop(0)
            jj = flip(j, r)
            at = pl.ds(pl.multiple_of(jj * rows, rows), rows)
            for col in range(0, width, 512):
                cols = pl.ds(col, 512)
                part[jj, :, :, cols] = dot_tn(hidden[:, at], down[:, cols]).astype(BF16).reshape(2, half, 512)
            out_sum.send(r)
            crossing.append(r)
        if len(crossing) > 1 or crossing and not waiting:
            out_sum.take(crossing.pop(0), leave=False)

    def between():
        tick(2)
        out_block()

    for r in Gather(own, wide_g, attn_sem, UP_FIRST, HALVES).blocks(between):
        jj = flip(j, r)
        at = pl.ds(pl.multiple_of(jj * rows, rows), rows)
        dy_ref[at, :] = dot_nt(wide_g[jj].reshape(rows, width), wo_ref[...]).astype(BF16)
    tick.flush()
    while waiting or crossing:
        out_block()
    out_sum.crossed()
    save_half = pltpu.make_async_copy(part.at[:, t], out_half, lsem.at[8])
    save_half.start()

    def output_grad(m, c):
        cols = pl.ds(pl.multiple_of(m * 256, 256), 256)
        block = dot(y_turned[...], wide_g[:, :, :, cols].reshape(CUBE * rows, 256))
        grads_o[:, cols] = block.astype(BF16)
        return c

    lax.fori_loop(0, width // 256, output_grad, 0)
    save_u.wait()
    save_half.wait()
    if in_kernel:
        back_d.finish()
        back_g.finish()
    else:
        save_d.wait()
        save_g.wait()


def mlp_call(n, own, w_a, w_o, y_turned, mid, w_gu, pack_d, cot_all):
    half, width = own.shape[1:]
    count = CUBE * 2 * half
    vm = pl.BlockSpec(memory_space=pltpu.VMEM)
    any_space = pl.BlockSpec(memory_space=pl.ANY)
    if width // n % 128:
        pack_d = spread_call(n, pack_d, width, 6)
    shape = (CUBE, 2, half, width)
    tiles = (UNITS, width) if width // n % 128 else (n, UNITS, width // n)
    return pl.pallas_call(
        functools.partial(mlp_with_own, n),
        out_shape=[
            jax.ShapeDtypeStruct((UNITS, width), BF16),
            jax.ShapeDtypeStruct(tiles, BF16),
            jax.ShapeDtypeStruct(tiles, BF16),
            jax.ShapeDtypeStruct((CUBE, half, width), BF16),
            jax.ShapeDtypeStruct((128, width), BF16),
            jax.ShapeDtypeStruct((2, half, width), F32),
            jax.ShapeDtypeStruct((count, 128), BF16),
        ],
        in_specs=[any_space, vm, vm, vm] + [any_space] * 4,
        out_specs=[any_space] * 4 + [vm] * 3,
        scratch_shapes=[
            pltpu.VMEM((2, half, width), BF16),
            pltpu.VMEM(shape, BF16),
            pltpu.VMEM(shape, BF16),
            pltpu.VMEM(shape, BF16),
            pltpu.VMEM((15, half, width), BF16),
            pltpu.VMEM((2, half, width), F32),
            pltpu.VMEM((2 * UNITS, width), BF16),
            pltpu.VMEM((UNITS, count), BF16),
            pltpu.VMEM((UNITS, width), BF16),
            pltpu.VMEM((UNITS, count), BF16),
            pltpu.VMEM((UNITS, count), BF16),
            pltpu.VMEM((UNITS, count), BF16),
            pltpu.VMEM((UNITS, count), BF16),
            pltpu.VMEM((UNITS, width), BF16),
            pltpu.SemaphoreType.DMA((9,)),
            *gather_sems(),
            *gather_sems(),
            *sum_sems(),
            *sum_sems(),
            *spread_sems(n),
            *spread_sems(n),
            *spread_sems(n),
        ],
        compiler_params=pltpu.CompilerParams(collective_id=3, has_side_effects=True, vmem_limit_bytes=63 * MIB),
    )(own, w_a, w_o, y_turned, mid, w_gu, pack_d, cot_all)


def mlp_with_own(n, own_hbm, w_ref, wo_ref, y_turned, mid_hbm, w_hbm, pack_d, cot_hbm, *rest):
    outs, (own, *scratch) = rest[:7], rest[7:]
    lsem = scratch[13]
    load = pltpu.make_async_copy(own_hbm, own, lsem.at[5])
    load.start()
    load.wait()
    mlp_kernel(n, own, w_ref, wo_ref, y_turned, mid_hbm, w_hbm, pack_d, cot_hbm, *outs, *scratch)


def tail_kernel(
    n, lengths, q_ref, k_ref, v_ref, y_ref, den_ref, state_ref, w_ref, tok_ref, dy_ref, grads_o,
    out_half, mid, d_mid, low_hbm, grads_b, first, second, third,
    output_ref, grad_ref, tiles_b, tiles_a,
    part, heap_a, heap_b, wide, total, c_ref, c_kept, v_kept, side, dv, turned, dqkv, grads_a,
    state_mine, state_theirs, xsend, xrecv, lsem, *sems,
):
    groups = n // CUBE
    s, t, j, base = whereabouts()
    tokens = q_ref.shape[0]
    rows = tokens // CUBE
    half = rows // 2
    width = w_ref.shape[1]
    two, three = lengths[0], lengths[0] + lengths[1]
    start = base * rows
    in_kernel = len(tiles_a.shape) == 3
    sum_out, sum_one, bsems, asems = sems[0:6], sems[6:12], sems[12:15], sems[15:18]

    load_low = pltpu.make_async_copy(low_hbm, wide, lsem.at[2])
    load_low.start()
    load_mid = pltpu.make_async_copy(mid, grad_ref, lsem.at[0])
    load_mid.start()
    load_out = pltpu.make_async_copy(out_half, part.at[:, t], lsem.at[4])
    load_out.start()
    greet_all(n)
    out_sum = Sum(part, heap_b, total, sum_out, UP_LAST, HALVES)
    back_b = Back(n, grads_b, tiles_b, bsems) if in_kernel else None

    tick = Trickle(back_b.trickle()) if in_kernel else Trickle([])

    state_mine[...] = jnp.zeros_like(state_mine)
    state = state_ref[...].astype(BF16)
    blocks = tokens // BLOCK

    def early(tb, carry):
        tq = pl.ds(pl.multiple_of(tb * BLOCK, BLOCK), BLOCK)
        _, seg = segments(two, three, start + tb * BLOCK, BLOCK, 0)
        keep = (seg == 1).astype(F32)
        c = (dy_ref[tq, :].astype(F32) / den_ref[tq, 0:1]).astype(BF16)
        m = -jnp.sum(c.astype(F32) * y_ref[tq, :], axis=-1, keepdims=True)
        m_high = m.astype(BF16).astype(F32)
        lane = lax.broadcasted_iota(jnp.int32, (BLOCK, 128), 1)
        extra = jnp.where(lane == 0, m_high, jnp.where(lane == 1, m - m_high, 0.0)).astype(BF16)
        c_ext = jnp.concatenate([c, extra], axis=1)
        c_ref[tq, :] = c_ext
        c_kept[tq, :] = c_ext * keep.astype(BF16)
        v_kept[tq, :] = v_ref[tq, :] * keep.astype(BF16)
        u = q_ref[tq, :]
        quad, line = lift(u, keep, first[...], second[...], third[...])
        state_mine[0:256, :] += dot_tn(quad, c_ext)
        state_mine[256:384, :] += dot_tn(line, c_ext)
        d_quad = dot_nt(c_ext, state[0:256]) * keep
        d_line = dot_nt(c_ext, state[256:384]) * keep
        side[tq, 0:FEAT] = lift_back(u, d_quad, d_line, first[...], second[...])
        return carry

    load_out.wait()
    for r in Sum.ORDER:
        out_sum.leave(r)
    tick(4)
    lax.fori_loop(0, blocks, early, 0)
    done = exchange(groups, state_mine, state_theirs, xsend, xrecv, False)
    for tb in range(blocks):
        tq = pl.ds(tb * BLOCK, BLOCK)
        qt = q_ref[tq, :] * BF16(0.25)
        score = dot_nt(qt, k_ref[tq, :])
        mask = pair_mask(two, three, start + tb * BLOCK, start + tb * BLOCK, BLOCK)
        grad = jnp.where(mask, dot_nt(c_ref[tq, :], v_ref[tq, :]) * (1.0 + score), 0.0).astype(BF16)
        acc = dot(grad, k_ref[tq, :])
        for lo in range(0, tb * BLOCK, 512):
            sq = pl.ds(lo, min(512, tb * BLOCK - lo))
            score = dot_nt(qt, k_ref[sq, :])
            grad = (dot_nt(c_kept[tq, :], v_kept[sq, :]) * (1.0 + score)).astype(BF16)
            acc = acc + dot(grad, k_ref[sq, :])
        side[tq, 0:FEAT] = (side[tq, 0:FEAT] + acc * 0.5) * 0.5
        tick()
    out_sum.phase(0)
    for sb in range(blocks):
        sq = pl.ds(sb * BLOCK, BLOCK)
        ks = k_ref[sq, :] * BF16(0.25)
        score = dot_nt(ks, q_ref[sq, :])
        mask = pair_mask_turned(two, three, start + sb * BLOCK, start + sb * BLOCK, BLOCK)
        grad = jnp.where(mask, dot_nt(v_ref[sq, :], c_ref[sq, :]) * (1.0 + score), 0.0).astype(BF16)
        weight = jnp.where(mask, pair_weight(score), 0.0).astype(BF16)
        acc = dot(grad, q_ref[sq, :])
        near = dot(weight, c_ref[sq, :])
        far = jnp.zeros((BLOCK, 256), F32)
        for lo in range((sb + 1) * BLOCK, tokens, 512):
            tq = pl.ds(lo, min(512, tokens - lo))
            score = dot_nt(ks, q_ref[tq, :])
            grad = (dot_nt(v_kept[sq, :], c_kept[tq, :]) * (1.0 + score)).astype(BF16)
            acc = acc + dot(grad, q_ref[tq, :])
            far = far + dot(pair_weight(score).astype(BF16), c_kept[tq, :])
        _, seg = segments(two, three, start + sb * BLOCK, BLOCK, 0)
        side[sq, FEAT : 2 * FEAT] = acc * 0.5
        dv[sq, :] = (near + far * (seg == 1).astype(F32))[:, :128]
        tick()
        if sb == blocks // 2:
            out_sum.phase(1)
    tick.flush()
    out_sum.close()
    state_back = done().astype(BF16)

    def late(sb, carry):
        sq = pl.ds(pl.multiple_of(sb * BLOCK, BLOCK), BLOCK)
        _, seg = segments(two, three, start + sb * BLOCK, BLOCK, 0)
        keep = (seg == 1).astype(F32)
        u = k_ref[sq, :]
        v = v_ref[sq, :]
        quad, line = lift(u, keep, first[...], second[...], third[...])
        d_quad = dot_nt(v, state_back[0:256]) * keep
        d_line = dot_nt(v, state_back[256:384]) * keep
        more = dot(quad, state_back[0:256]) + dot(line, state_back[256:384])
        dk = (side[sq, FEAT : 2 * FEAT] + lift_back(u, d_quad, d_line, first[...], second[...])) * 0.5
        dqkv[sq, 0:128] = (dv[sq, :] + more[:, :128]).astype(BF16)
        packed = dot(side[sq, 0:FEAT].astype(BF16), third[...]) + dot(dk.astype(BF16), third_shifted(third[...]))
        dqkv[sq, 128:256] = packed.astype(BF16)
        turned[:, sq] = dqkv[sq, :].T
        return carry

    lax.fori_loop(0, blocks, late, 0)
    out_sum.finish(crossed=True)
    load_mid.wait()
    for h in range(2):

        def finish_output(at):
            output_ref[h, at] = (grad_ref[h, at] + total[h, at]).astype(BF16)

        row_loop(half, 16, finish_output)
    load_mid = pltpu.make_async_copy(d_mid, grad_ref, lsem.at[1])
    load_mid.start()

    load_low.wait()
    one_sum = Sum(part, heap_a, total, sum_one)
    w_one = w_ref[0:160, :]
    for idx, r in enumerate(Sum.ORDER):
        jj = flip(j, r)
        for h in range(2):
            at = pl.ds(pl.multiple_of(jj * rows + h * half, half), half)
            part[jj, h] = dot(dqkv[at, 0:160], w_one).astype(BF16)
        one_sum.send(r)
        if idx:
            one_sum.take(Sum.ORDER[idx - 1])
    one_sum.take(Sum.ORDER[-1])

    def one_grad(m, c):
        cols = pl.ds(pl.multiple_of(m * 256, 256), 256)
        block = dot(turned[0:160, :], wide[:, :, :, cols].reshape(tokens, 256))
        grads_a[0:160, cols] = block.astype(BF16)
        return c

    lax.fori_loop(0, width // 256, one_grad, 0)
    grads_a[160:288, :] = grads_o[...]
    if in_kernel:
        back_a = Back(n, grads_a, tiles_a, asems)
        back_a.start()
    else:
        copy = pltpu.make_async_copy(grads_a, tiles_a, lsem.at[3])
        copy.start()
    one_sum.phase(0)
    one_sum.phase(1)
    one_sum.close()
    one_sum.finish()

    gain_one = w_ref[160:161, :].astype(F32)
    load_mid.wait()
    for h in range(2):

        def norm_back_one(at):
            x = tok_ref[h, at].astype(F32)
            root = lax.rsqrt(jnp.mean(x * x, axis=-1, keepdims=True) + EPS)
            normed = x * root
            scaled = total[h, at] * gain_one
            grad_ref[h, at] = grad_ref[h, at] + root * (
                scaled - normed * jnp.mean(scaled * normed, axis=-1, keepdims=True)
            )

        row_loop(half, 16, norm_back_one)

    if in_kernel:
        back_b.finish()
        back_a.finish()
    else:
        copy.wait()


def third_shifted(third):
    return jnp.concatenate([jnp.zeros_like(third[:, :FEAT]), third[:, : 128 - FEAT]], axis=1)


def tail_call(n, lengths, q, k, v, y, den, state, w_a, mid, tokens, d_mid, dy, grads_o, out_half, low_one, grads_b):
    groups = n // CUBE
    _, half, width = mid.shape
    rows = 2 * half
    count = CUBE * rows
    wide_columns = width // n % 128 == 0
    vm = pl.BlockSpec(memory_space=pltpu.VMEM)
    any_space = pl.BlockSpec(memory_space=pl.ANY)
    peers = max(groups - 1, 1)
    out_shape = [
        jax.ShapeDtypeStruct((2, half, width), BF16),
        jax.ShapeDtypeStruct((2, half, width), F32),
        jax.ShapeDtypeStruct((n, grads_b.shape[0], width // n) if wide_columns else (8, 128), BF16),
        jax.ShapeDtypeStruct((n, 288, width // n) if wide_columns else (288, width), BF16),
    ]
    output, grad, tiles_b, tiles_a = pl.pallas_call(
        functools.partial(tail_kernel, n),
        out_shape=out_shape,
        in_specs=[pl.BlockSpec(memory_space=pltpu.SMEM)] + [vm] * 10 + [any_space] * 5 + [vm] * 3,
        out_specs=[vm, vm, any_space, any_space],
        scratch_shapes=[
            pltpu.VMEM((CUBE, 2, half, width), BF16),
            pltpu.VMEM((15, half, width), BF16),
            pltpu.VMEM((15, half, width), BF16),
            pltpu.VMEM((CUBE, 2, half, width), BF16),
            pltpu.VMEM((2, half, width), F32),
            pltpu.VMEM((count, 256), BF16),
            pltpu.VMEM((count, 256), BF16),
            pltpu.VMEM((count, 256), BF16),
            pltpu.VMEM((count, 128), F32),
            pltpu.VMEM((count, 128), F32),
            pltpu.VMEM((256, count), BF16),
            pltpu.VMEM((count, 256), BF16),
            pltpu.VMEM((288, width), BF16),
            pltpu.VMEM((384, 256), F32),
            pltpu.VMEM((peers, 384, 256), F32),
            pltpu.SemaphoreType.DMA((peers,)),
            pltpu.SemaphoreType.DMA((peers,)),
            pltpu.SemaphoreType.DMA((5,)),
            *sum_sems(),
            *sum_sems(),
            *spread_sems(n),
            *spread_sems(n),
        ],
        compiler_params=pltpu.CompilerParams(collective_id=2, has_side_effects=True, vmem_limit_bytes=63 * MIB),
    )(
        lengths, q, k, v, y, den, state, w_a, tokens.reshape(2, half, width), dy, grads_o,
        out_half, mid, d_mid, low_one, grads_b, *spreaders(),
    )
    if not wide_columns:
        tiles_b = back_call(n, grads_b, 9)
        tiles_a = back_call(n, tiles_a, 10)
    return output.reshape(rows, width), grad.reshape(rows, width), tiles_b, tiles_a


def units_first(w):
    return jnp.pad(w, ((0, CUBE * UNITS - w.shape[0]), (0, 0))).reshape(CUBE, UNITS, w.shape[1])


def body(
    n, tokens, gain_attn, w_query, w_key, w_value, w_output, gain_mlp, w_gate, w_up, w_down, seq_lengths, cotangent
):
    per = HEADS // lax.axis_size("tensor")
    gains = jnp.concatenate([gain_attn[None], gain_mlp[None], jnp.zeros((14, gain_attn.shape[0]), BF16)], axis=0)
    pack_a = jnp.concatenate(
        [
            w_value.T.reshape(per, 128, -1),
            w_query.T.reshape(per, FEAT, -1),
            w_key.T.reshape(per, FEAT, -1),
            jnp.broadcast_to(gains[None], (per, *gains.shape)),
        ],
        axis=1,
    )
    pack_o = w_output.reshape(per, 128, -1)
    pack_b = jnp.concatenate([units_first(w_gate.T), units_first(w_up.T)], axis=1)
    w_a, w_o, w_gu, cot_all, low_one, low_two, mid, q, k, v, y, y_turned, den, state = head_call(
        n, seq_lengths, pack_a, pack_o, pack_b, tokens, cotangent
    )
    grads_u, tiles_d, tiles_g, out_half, grads_o, d_mid, dy = mlp_call(
        n, low_two, w_a, w_o, y_turned, mid, w_gu, units_first(w_down), cot_all
    )
    if tiles_d.ndim == 2:
        tiles_d, tiles_g = back_call(n, tiles_d, 7), back_call(n, tiles_g, 8)
    output, grad_tokens, tiles_u, tiles_a = tail_call(
        n, seq_lengths, q, k, v, y, den, state, w_a, mid, tokens, d_mid, dy, grads_o, out_half, low_one, grads_u
    )

    def arrived(tiles):
        return tiles.reshape(-1, CUBE, *tiles.shape[1:]).astype(F32).sum(axis=0)

    back_g, back_u, back_d, back_a = arrived(tiles_g), arrived(tiles_u), arrived(tiles_d), arrived(tiles_a)

    def units(part):
        return part.reshape(CUBE * UNITS, -1)[: w_gate.shape[1]]

    grad_gate = units(back_g).T
    grad_up = units(back_u).T
    grad_down = units(back_d)
    grad_value = back_a[:, 0:128].reshape(per * 128, -1).T
    grad_query = back_a[:, 128:144].reshape(per * FEAT, -1).T
    grad_key = back_a[:, 144:160].reshape(per * FEAT, -1).T
    grad_output = back_a[:, 160:288].reshape(per * 128, -1)

    def weighed(*pairs):
        return sum(jnp.sum(w.astype(F32) * g, axis=1) for w, g in pairs)

    gain_one_part = weighed((w_value, grad_value), (w_query, grad_query), (w_key, grad_key))
    gain_two_part = weighed((w_gate, grad_gate), (w_up, grad_up))
    both = lax.psum(jnp.stack([gain_one_part, gain_two_part]), "tensor")
    grad_gain_one = both[0] / gain_attn.astype(F32)
    grad_gain_two = both[1] / gain_mlp.astype(F32)
    return (
        output,
        grad_tokens,
        grad_gain_one,
        grad_query,
        grad_key,
        grad_value,
        grad_output,
        grad_gain_two,
        grad_gate,
        grad_up,
        grad_down,
    )


def solution(mesh):
    return jax.shard_map(
        functools.partial(body, mesh.shape["seq"]),
        mesh=mesh,
        in_specs=(
            P("seq", None),
            P("seq"),
            P("seq", "tensor"),
            P("seq", "tensor"),
            P("seq", "tensor"),
            P("tensor", "seq"),
            P("seq"),
            P("seq", "tensor"),
            P("seq", "tensor"),
            P("tensor", "seq"),
            P(),
            P("seq", None),
        ),
        out_specs=(
            P("seq", None),
            P("seq", None),
            P("seq"),
            P("seq", "tensor"),
            P("seq", "tensor"),
            P("seq", "tensor"),
            P("tensor", "seq"),
            P("seq"),
            P("seq", "tensor"),
            P("seq", "tensor"),
            P("tensor", "seq"),
        ),
        check_vma=False,
    )
```

```python
import functools

import jax
import jax.numpy as jnp
import numpy as np
from jax import lax
from jax.experimental import pallas as pl
from jax.experimental.pallas import tpu as pltpu
from jax.sharding import PartitionSpec as P

MESH = pl.DeviceIdType.MESH
HEADS = 16
FEAT = 16
CUBE = 8
UNITS = 352
EPS = 1e-06
F32 = jnp.float32
BF16 = jnp.bfloat16
ORDERS = ((0, 1, 2), (1, 2, 0), (2, 0, 1))
PIECES = ((0, 48), (48, 48), (96, 32))
WAVES = ((4, 1, 2), (6, 5, 3), (7,))
UP_FIRST = ((2, 0, 1), (2, 1, 0))
UP_LAST = ((0, 1, 2), (1, 0, 2))
HALVES = ((0, 64), (64, 64))
MIB = 1 << 20


def flip(place, mask):
    total = 0
    for b in range(3):
        bit = (place // (1 << b)) % 2
        total = total + ((1 - bit) if (mask >> b) & 1 else bit) * (1 << b)
    return total


def subsets(dims):
    out = [0]
    for d in dims:
        out = out + [r | (1 << d) for r in out]
    return out


def whereabouts():
    s = lax.axis_index("seq")
    t = lax.axis_index("tensor")
    j = s % CUBE
    return s, t, j, s - j


def remote(src, dst, send, recv, device):
    return pltpu.make_async_remote_copy(
        src_ref=src, dst_ref=dst, send_sem=send, recv_sem=recv, device_id=device, device_id_type=MESH
    )


def greet(devices):
    barrier = pltpu.get_barrier_semaphore()
    for device in devices:
        pl.semaphore_signal(barrier, inc=1, device_id=device, device_id_type=MESH)
    pl.semaphore_wait(barrier, len(devices))


def near():
    s, t, j, base = whereabouts()
    return [(base + flip(j, 1 << d), t) for d in range(3)] + [(s, 1 - t)]


def greet_all(n):
    s, t, _, _ = whereabouts()
    barrier = pltpu.get_barrier_semaphore()

    def one(k, carry):
        pl.semaphore_signal(barrier, inc=1, device_id=((s + k) % n, t), device_id_type=MESH)
        return carry

    lax.fori_loop(1, n, one, 0)
    pl.semaphore_signal(barrier, inc=1, device_id=(s, 1 - t), device_id_type=MESH)
    pl.semaphore_wait(barrier, n)


class Gather:
    def __init__(self, own, full, sems, orders=ORDERS, pieces=PIECES):
        self.own, self.full, self.orders, self.pieces = own, full, orders, pieces
        self.ssem, self.rsem, self.csend, self.crecv, self.lsem = sems
        self.s, self.t, self.j, self.base = whereabouts()

    def view(self, r, i):
        off, rows = self.pieces[i]
        return self.full.at[flip(self.j, r), self.t, pl.ds(off, rows)]

    def hop(self, p, i, r):
        d = self.orders[i][p]
        off, rows = self.pieces[i]
        src = self.own.at[self.t, pl.ds(off, rows)] if r == 0 else self.view(r, i)
        k = r | (1 << d)
        return remote(src, self.view(r, i), self.ssem.at[i, k], self.rsem.at[i, k], (self.base + flip(self.j, 1 << d), self.t))

    def came(self, i, k):
        p = max(q for q in range(3) if k >> self.orders[i][q] & 1)
        return p, k ^ (1 << self.orders[i][p])

    def arrival(self, i, k):
        p, _ = self.came(i, k)
        device = (self.base + flip(self.j, 1 << self.orders[i][p]), self.t)
        return remote(self.view(k, i), self.view(k, i), self.ssem.at[i, k], self.rsem.at[i, k], device)

    def across(self, r, mine):
        ref = self.full.at[flip(self.j, r), self.t if mine else 1 - self.t]
        return remote(ref, ref, self.csend.at[r], self.crecv.at[r], (self.s, 1 - self.t))

    def local(self):
        return pltpu.make_async_copy(self.own, self.full.at[self.j], self.lsem)

    def start(self):
        self.local().start()
        for q in range(3):
            for i in range(len(self.pieces)):
                self.hop(q, i, 0).start()

    def arrived(self, k):
        for i in range(len(self.pieces)):
            p, _ = self.came(i, k)
            self.arrival(i, k).wait_recv()
            for q in range(p + 1, 3):
                self.hop(q, i, k).start()
        self.across(k, True).start()

    def wave(self, w, tick=lambda: None):
        for k in WAVES[w]:
            self.arrived(k)
            tick()

    def settle(self, r):
        self.across(r, False).wait_recv()

    def sent(self):
        for k in range(1, CUBE):
            self.across(k, True).wait_send()
            for i in range(len(self.pieces)):
                p, r = self.came(i, k)
                self.hop(p, i, r).wait_send()

    def finish(self):
        for r in range(1, CUBE):
            self.settle(r)
        self.sent()
        self.local().wait()

    def blocks(self, tick=lambda: None):
        self.start()
        self.local().wait()
        yield 0
        before = None
        for k in WAVES[0] + WAVES[1] + WAVES[2]:
            self.arrived(k)
            tick()
            if before:
                self.settle(before)
                yield before
            before = k
        self.settle(before)
        yield before
        self.sent()


def gather_sems():
    return [pltpu.SemaphoreType.DMA((3, CUBE))] * 2 + [pltpu.SemaphoreType.DMA((CUBE,))] * 2 + [pltpu.SemaphoreType.DMA]


SLOT = {0: 0, 1: 4, 2: 6}


def slot_of(order, p, r):
    return SLOT[p] + subsets(order[p + 1 :]).index(r)


class Sum:
    ORDER = (7, 6, 5, 3, 4, 2, 1, 0)

    def __init__(self, part, heap, total, sems, orders=ORDERS, pieces=PIECES):
        self.part, self.heap, self.total = part, heap, total
        self.orders, self.pieces = orders, pieces
        self.csend, self.crecv, self.ssem, self.rsem, self.fsend, self.frecv = sems
        self.s, self.t, self.j, self.base = whereabouts()

    def across(self, r):
        src = self.part.at[flip(self.j, r), 1 - self.t]
        return remote(src, self.heap.at[r], self.csend.at[r], self.crecv.at[r], (self.s, 1 - self.t))

    def hop(self, p, i, r):
        d = self.orders[i][p]
        off, rows = self.pieces[i]
        k = slot_of(self.orders[i], p, r ^ (1 << d))
        return remote(
            self.part.at[flip(self.j, r), self.t, pl.ds(off, rows)],
            self.heap.at[CUBE + k, pl.ds(off, rows)],
            self.ssem.at[i, k],
            self.rsem.at[i, k],
            (self.base + flip(self.j, 1 << d), self.t),
        )

    def send(self, r):
        self.across(r).start()

    def take(self, r, leave=True):
        self.across(r).wait_recv()
        jj = flip(self.j, r)
        step = 32

        def one(m, c):
            at = pl.ds(pl.multiple_of(m * step, step), step)
            self.part[jj, self.t, at] = (
                self.part[jj, self.t, at].astype(F32) + self.heap[r, at].astype(F32)
            ).astype(BF16)
            return c

        lax.fori_loop(0, self.part.shape[2] // step, one, 0)
        if leave:
            self.leave(r)

    def leave(self, r):
        for i in range(len(self.pieces)):
            if r >> self.orders[i][0] & 1 and r != 1 << self.orders[i][0]:
                self.hop(0, i, r).start()

    def phase(self, p, tick=lambda: None):
        count = len(self.pieces)
        for i, r in [(i, subsets(self.orders[i][p + 1 :])[-1 - m]) for m in range((4 >> p) - 1) for i in range(count)]:
            d = self.orders[i][p]
            off, rows = self.pieces[i]
            self.hop(p, i, r | (1 << d)).wait_recv()
            jj = flip(self.j, r)
            k = slot_of(self.orders[i], p, r)
            for q in range(0, rows, 16):
                at = pl.ds(off + q, 16)
                new = self.part[jj, self.t, at].astype(F32) + self.heap[CUBE + k, at].astype(F32)
                self.part[jj, self.t, at] = new.astype(BF16)
            e = self.orders[i][p + 1]
            if r >> e & 1 and (p == 1 or r != 1 << e):
                self.hop(p + 1, i, r).start()
            tick()
        for i in range(count):
            self.hop(p, i, 1 << self.orders[i][p]).start()

    def close(self, tick=lambda: None):
        for i in range(len(self.pieces)):
            off, rows = self.pieces[i]
            for p in range(3):
                self.hop(p, i, 1 << self.orders[i][p]).wait_recv()
            slots = [CUBE + slot_of(self.orders[i], p, 0) for p in range(3)]
            for q in range(0, rows, 16):
                at = pl.ds(off + q, 16)
                new = self.part[self.j, self.t, at].astype(F32)
                for k in slots:
                    new = new + self.heap[k, at].astype(F32)
                self.total[self.t, at] = new
            tick()
        self.trade()

    def both(self, half):
        ref = self.total.at[half]
        return remote(ref, ref, self.fsend, self.frecv, (self.s, 1 - self.t))

    def trade(self):
        self.both(self.t).start()

    def crossed(self):
        for r in range(CUBE):
            self.across(r).wait_send()

    def finish(self, crossed=False):
        self.both(1 - self.t).wait_recv()
        self.both(self.t).wait_send()
        if not crossed:
            self.crossed()
        for p in range(3):
            for i in range(len(self.pieces)):
                d = self.orders[i][p]
                for r in subsets(self.orders[i][p + 1 :]):
                    self.hop(p, i, r | (1 << d)).wait_send()

    def run(self):
        for r in self.ORDER:
            self.send(r)
        for r in self.ORDER:
            self.take(r)
        self.phase(0)
        self.phase(1)
        self.close()
        self.finish()


def sum_sems():
    return [
        pltpu.SemaphoreType.DMA((CUBE,)),
        pltpu.SemaphoreType.DMA((CUBE,)),
        pltpu.SemaphoreType.DMA((3, CUBE)),
        pltpu.SemaphoreType.DMA((3, CUBE)),
        pltpu.SemaphoreType.DMA,
        pltpu.SemaphoreType.DMA,
    ]


def columns_of(ref, s):
    if len(ref.shape) == 3:
        return ref.at[s]
    return ref.at[:, pl.ds(pl.multiple_of(s * 128, 128), 128)]


def columns_apart(n, rows, width):
    return (rows, width) if width // n % 128 == 0 else (n, rows, width // n)


def together(x):
    return x if x.ndim == 2 else x.transpose(1, 0, 2).reshape(x.shape[1], -1)


def apart(n, x):
    return x if x.shape[1] // n % 128 == 0 else x.reshape(x.shape[0], n, -1).transpose(1, 0, 2)


class Trickle:
    def __init__(self, copies):
        self.copies = list(copies)

    def __call__(self, count=1):
        for _ in range(min(count, len(self.copies))):
            self.copies.pop(0).start()

    def flush(self):
        self(len(self.copies))


def far_and_near(n):
    near, far = list(range(1, n // 2)), list(range(n // 2, n))
    return [k for pair in zip(far, near + [None]) for k in pair if k is not None]


class Spread:
    def __init__(self, n, pack, full, sems):
        self.n, self.pack, self.full = n, pack, full
        self.ssem, self.rsem, self.lsem = sems
        self.s, self.t, self.j, self.base = whereabouts()

    def columns(self, s):
        return columns_of(self.full, s)

    def copy(self, k):
        to = (self.s + k) % self.n
        return remote(self.pack.at[to % CUBE], self.columns(self.s), self.ssem.at[k], self.rsem.at[k], (to, self.t))

    def arrival(self, k):
        at = (self.s + self.n - k) % self.n
        return remote(self.pack.at[0], self.columns(at), self.ssem.at[k], self.rsem.at[k], (at, self.t))

    def local(self):
        return pltpu.make_async_copy(self.pack.at[self.j], self.columns(self.s), self.lsem)

    def start(self):
        lax.fori_loop(1, self.n, lambda k, c: (self.copy(k).start(), c)[1], 0)
        self.local().start()

    def trickle(self):
        return [self.local()] + [self.copy(k) for k in far_and_near(self.n)]

    def finish(self):
        self.local().wait()
        lax.fori_loop(1, self.n, lambda k, c: (self.arrival(k).wait_recv(), c)[1], 0)
        lax.fori_loop(1, self.n, lambda k, c: (self.copy(k).wait_send(), c)[1], 0)


class Back:
    def __init__(self, n, grads, tiles, sems):
        self.n, self.grads, self.tiles = n, grads, tiles
        self.ssem, self.rsem, self.lsem = sems
        self.s, self.t, self.j, self.base = whereabouts()

    def columns(self, s):
        return columns_of(self.grads, s)

    def copy(self, k):
        to = (self.s + k) % self.n
        return remote(self.columns(to), self.tiles.at[self.s], self.ssem.at[k], self.rsem.at[k], (to, self.t))

    def arrival(self, k):
        at = (self.s + self.n - k) % self.n
        return remote(self.tiles.at[at], self.tiles.at[at], self.ssem.at[k], self.rsem.at[k], (at, self.t))

    def local(self):
        return pltpu.make_async_copy(self.columns(self.s), self.tiles.at[self.s], self.lsem)

    start = Spread.start
    trickle = Spread.trickle
    finish = Spread.finish


def spread_sems(n):
    return [pltpu.SemaphoreType.DMA((n,)), pltpu.SemaphoreType.DMA((n,)), pltpu.SemaphoreType.DMA]


def spread_kernel(n, pack, full, *sems):
    greet_all(n)
    spread = Spread(n, pack, full, sems)
    spread.start()
    spread.finish()


def spread_call(n, pack, width, number):
    any_space = pl.BlockSpec(memory_space=pl.ANY)
    full = pl.pallas_call(
        functools.partial(spread_kernel, n),
        out_shape=jax.ShapeDtypeStruct(columns_apart(n, pack.shape[1], width), BF16),
        in_specs=[any_space],
        out_specs=any_space,
        scratch_shapes=spread_sems(n),
        compiler_params=pltpu.CompilerParams(collective_id=number, has_side_effects=True),
    )(pack)
    return together(full)


def back_kernel(n, grads, tiles, *sems):
    greet_all(n)
    back = Back(n, grads, tiles, sems)
    back.start()
    back.finish()


def back_call(n, grads, number):
    rows, width = grads.shape
    any_space = pl.BlockSpec(memory_space=pl.ANY)
    return pl.pallas_call(
        functools.partial(back_kernel, n),
        out_shape=jax.ShapeDtypeStruct((n, rows, width // n), BF16),
        in_specs=[any_space],
        out_specs=any_space,
        scratch_shapes=spread_sems(n),
        compiler_params=pltpu.CompilerParams(collective_id=number, has_side_effects=True),
    )(apart(n, grads))


def dot(a, b):
    return jnp.dot(a, b, preferred_element_type=F32)


def dot_nt(a, b):
    return lax.dot_general(a, b, (((1,), (1,)), ((), ())), preferred_element_type=F32)


def dot_tn(a, b):
    return lax.dot_general(a, b, (((0,), (0,)), ((), ())), preferred_element_type=F32)


def spreaders():
    first = np.repeat(np.eye(FEAT), FEAT, axis=1)
    second = np.tile(np.eye(FEAT), (1, FEAT))
    third = np.eye(FEAT, 128)
    return [jnp.asarray(m, BF16) for m in (first, second, third)]


ROOT_HALF = 0.5**0.5


def lift(u, keep, first, second, third):
    quad = dot(u, first) * dot(u, second) * (0.25 * ROOT_HALF) * keep
    lane = lax.broadcasted_iota(jnp.int32, (u.shape[0], 128), 1)
    line = (dot(u, third) * 0.5 + jnp.where(lane == FEAT, 1.0, 0.0)) * keep
    return quad.astype(BF16), line.astype(BF16)


def lift_back(u, d_quad, d_line, first, second):
    one, two = dot(u, first) * 0.5, dot(u, second) * 0.5
    back = dot_nt((d_quad * two).astype(BF16), first) + dot_nt((d_quad * one).astype(BF16), second)
    return back * ROOT_HALF + d_line[:, :FEAT]


def two_terms(x):
    high = x.astype(BF16)
    return high, (x - high.astype(F32)).astype(BF16)


def segments(start_two, start_three, first_position, count, axis):
    shape = (count, 1) if axis == 0 else (1, count)
    position = first_position + lax.broadcasted_iota(jnp.int32, shape, axis)
    return position, (position >= start_two).astype(jnp.int32) + (position >= start_three).astype(jnp.int32)


def pair_mask(two, three, at_t, at_s, block):
    pos_t, seg_t = segments(two, three, at_t, block, 0)
    pos_s, seg_s = segments(two, three, at_s, block, 1)
    return (pos_s <= pos_t) & (seg_s == seg_t)


def pair_mask_turned(two, three, at_s, at_t, block):
    pos_s, seg_s = segments(two, three, at_s, block, 0)
    pos_t, seg_t = segments(two, three, at_t, block, 1)
    return (pos_s <= pos_t) & (seg_s == seg_t)


def other_groups(groups):
    s, t, j, base = whereabouts()
    return [((s + CUBE * k) % (CUBE * groups), t) for k in range(1, groups)]


def exchange(groups, mine, theirs, ssem, rsem, before):
    s, t, j, base = whereabouts()
    c = s // CUBE
    for k, device in enumerate(other_groups(groups)):
        remote(mine, theirs.at[k], ssem.at[k], rsem.at[k], device).start()

    def finish():
        total = jnp.zeros(mine.shape, F32)
        for k, device in enumerate(other_groups(groups)):
            remote(mine, theirs.at[k], ssem.at[k], rsem.at[k], device).wait_recv()
            source = (c + groups - (k + 1)) % groups
            counts = (source < c) if before else (source > c)
            total = total + jnp.where(counts, theirs[k], 0.0)
        for k, device in enumerate(other_groups(groups)):
            remote(mine, theirs.at[k], ssem.at[k], rsem.at[k], device).wait_send()
        return total

    return finish


BLOCK = 256


def row_loop(count, step, work):
    def one(m, c):
        work(pl.ds(pl.multiple_of(m * step, step), step))
        return c

    lax.fori_loop(0, count // step, one, 0)


def pair_weight(score):
    return (score * 0.5 + 1.0) * score + 1.0


def head_kernel(
    n, lengths, tok_ref, pack_a, pack_o, pack_b, cot_hbm, first, second, third,
    w_ref, wo_ref, w_b, cot_all, low_hbm, own, mid_ref, q_ref, k_ref, v_ref, y_ref, y_turned, den_ref, state_ref,
    wide, part, heap, total, kept, state_mine, state_theirs, xsend, xrecv, lsem, *sems, results,
):
    groups = n // CUBE
    s, t, j, base = whereabouts()
    half, width = tok_ref.shape[1:]
    rows = 2 * half
    tokens = CUBE * rows
    two, three = lengths[0], lengths[0] + lengths[1]
    start = base * rows
    in_kernel = len(pack_a.shape) == 3
    sum_sem, tok_sem, cot_sem = sems[0:6], sems[6:11], sems[11:16]
    a_sem, b_sem, o_sem = sems[16:19], sems[19:22], sems[22:25]

    greet_all(n)
    g_tok = Gather(tok_ref, wide, tok_sem)
    g_cot = Gather(cot_hbm, cot_all, cot_sem, UP_FIRST, HALVES)
    if in_kernel:
        spread_a = Spread(n, pack_a, w_ref, a_sem)
        spread_b = Spread(n, pack_b, w_b, b_sem)
        spread_o = Spread(n, pack_o, wo_ref, o_sem)
        spread_a.start()
        tick = Trickle(spread_o.trickle() + spread_b.trickle())
    else:
        copy_a = pltpu.make_async_copy(pack_a, w_ref, lsem.at[CUBE])
        copy_b = pltpu.make_async_copy(pack_b, w_b, lsem.at[CUBE + 1])
        copy_o = pltpu.make_async_copy(pack_o, wo_ref, lsem.at[CUBE + 2])
        copy_a.start()
        tick = Trickle([copy_o, copy_b])
    g_tok.start()
    for w in range(3):
        g_tok.wave(w)
    g_cot.start()
    g_tok.finish()
    if in_kernel:
        spread_a.finish()
    else:
        copy_a.wait()

    state_mine[...] = jnp.zeros_like(state_mine)
    gain_one = w_ref[160:161, :].astype(F32)

    def project(jj, c):
        for h in range(2):

            def norm(at):
                x = wide[jj, h, at].astype(F32)
                root = lax.rsqrt(jnp.mean(x * x, axis=-1, keepdims=True) + EPS)
                wide[jj, h, at] = (x * root * gain_one).astype(BF16)

            row_loop(half, 64, norm)
        at = pl.ds(pl.multiple_of(jj * rows, rows), rows)
        qkv = dot_nt(wide[jj].reshape(rows, width), w_ref[0:160, :]).astype(BF16)
        v, k = qkv[:, 0:128], qkv[:, 144:160]
        lane = lax.broadcasted_iota(jnp.int32, (rows, 128), 1)
        v_ext = jnp.concatenate([v, jnp.where(lane < 2, 1.0, 0.0).astype(BF16)], axis=1)
        q_ref[at, :] = qkv[:, 128:144]
        k_ref[at, :] = k
        v_ref[at, :] = v_ext
        _, seg = segments(two, three, start + jj * rows, rows, 0)
        keep = (seg == 1).astype(F32)
        kept[at, :] = v_ext * keep.astype(BF16)
        quad, line = lift(k, keep, first[...], second[...], third[...])
        state_mine[0:256, :] += dot_tn(quad, v_ext)
        state_mine[256:384, :] += dot_tn(line, v_ext)
        return c

    for jj in range(CUBE):
        tick(2)
        project(jj, 0)
    save = pltpu.make_async_copy(wide, low_hbm, lsem.at[0])
    save.start()
    done = exchange(groups, state_mine, state_theirs, xsend, xrecv, True)
    g_cot.wave(0)

    blocks = tokens // BLOCK
    for tb in range(blocks):
        tq = pl.ds(tb * BLOCK, BLOCK)
        qt = q_ref[tq, :] * BF16(0.25)
        score = dot_nt(qt, k_ref[tq, :])
        mask = pair_mask(two, three, start + tb * BLOCK, start + tb * BLOCK, BLOCK)
        acc = dot(jnp.where(mask, pair_weight(score), 0.0).astype(BF16), v_ref[tq, :])
        if tb:
            _, seg = segments(two, three, start + tb * BLOCK, BLOCK, 0)
            far = jnp.zeros((BLOCK, 256), F32)
            for lo in range(0, tb * BLOCK, 512):
                sq = pl.ds(lo, min(512, tb * BLOCK - lo))
                far = far + dot(pair_weight(dot_nt(qt, k_ref[sq, :])).astype(BF16), kept[sq, :])
            acc = acc + far * (seg == 1).astype(F32)
        y_ref[tq, :] = acc[:, :128]
        den_ref[tq, :] = acc[:, 128:]
        tick(2)

    g_cot.wave(1)
    state = done()
    state_ref[...] = state
    high, lowp = two_terms(state)
    out_sum = Sum(part, heap, total, sum_sem)
    if in_kernel:
        spread_o.finish()
    else:
        copy_o.wait()
    out_w = wo_ref[...]

    for idx, r in enumerate(Sum.ORDER):
        jj = flip(j, r)
        tq = pl.ds(pl.multiple_of(jj * rows, rows), rows)
        _, seg = segments(two, three, start + jj * rows, rows, 0)
        quad, line = lift(q_ref[tq, :], (seg == 1).astype(F32), first[...], second[...], third[...])
        more = dot(quad, high[0:256]) + dot(quad, lowp[0:256]) + dot(line, high[256:384]) + dot(line, lowp[256:384])
        den = den_ref[tq, :] + more[:, 128:]
        den_ref[tq, :] = den
        y = (y_ref[tq, :] + more[:, :128]) / den[:, 0:1]
        y_ref[tq, :] = y
        y_low = y.astype(BF16)
        y_turned[:, tq] = y_low.T
        for h in range(2):
            part[jj, h] = dot(y_low[h * half : (h + 1) * half], out_w).astype(BF16)
        out_sum.send(r)
        tick(1)
        if idx:
            out_sum.take(Sum.ORDER[idx - 1])
    out_sum.take(Sum.ORDER[-1])
    for copy in results:
        copy.start()
    out_sum.phase(0, lambda: tick(1))
    tick.flush()
    out_sum.phase(1)
    out_sum.close()
    out_sum.finish()

    gain_two = w_ref[161:162, :].astype(F32)
    for h in range(2):

        def second_norm(at):
            mid = tok_ref[h, at].astype(F32) + total[h, at]
            mid_ref[h, at] = mid
            root = lax.rsqrt(jnp.mean(mid * mid, axis=-1, keepdims=True) + EPS)
            own[h, at] = (mid * root * gain_two).astype(BF16)

        row_loop(half, 16, second_norm)

    g_cot.wave(2)
    g_cot.finish()
    save.wait()
    for copy in results:
        copy.wait()
    if in_kernel:
        spread_b.finish()
    else:
        copy_b.wait()


HELD = (0, 1, 7, 8, 9, 10, 11, 12, 13)


def head_with_results(n, *refs):
    ins, outs, held, sem, rest = refs[:9], list(refs[9:23]), refs[23:32], refs[32], refs[33:]
    results = [pltpu.make_async_copy(ref, outs[at], sem.at[m]) for m, (at, ref) in enumerate(zip(HELD, held))]
    for at, ref in zip(HELD, held):
        outs[at] = ref
    head_kernel(n, *ins, *outs, *rest, results=results)


def head_call(n, lengths, pack_a, pack_o, pack_b, tokens, cot):
    groups = n // CUBE
    rows, width = tokens.shape
    half = rows // 2
    count = CUBE * rows
    vm = pl.BlockSpec(memory_space=pltpu.VMEM)
    any_space = pl.BlockSpec(memory_space=pl.ANY)
    peers = max(groups - 1, 1)
    w_rows = (pack_a.shape[1], pack_b.shape[1])
    if width // n % 128:
        pack_a, pack_b = spread_call(n, pack_a, width, 4), spread_call(n, pack_b, width, 5)
        pack_o = spread_call(n, pack_o, width, 11)
    shape = (CUBE, 2, half, width)
    return pl.pallas_call(
        functools.partial(head_with_results, n),
        out_shape=[
            jax.ShapeDtypeStruct((w_rows[0], width), BF16),
            jax.ShapeDtypeStruct((128, width), BF16),
            jax.ShapeDtypeStruct((w_rows[1], width), BF16),
            jax.ShapeDtypeStruct(shape, BF16),
            jax.ShapeDtypeStruct(shape, BF16),
            jax.ShapeDtypeStruct((2, half, width), BF16),
            jax.ShapeDtypeStruct((2, half, width), F32),
            jax.ShapeDtypeStruct((count, FEAT), BF16),
            jax.ShapeDtypeStruct((count, FEAT), BF16),
            jax.ShapeDtypeStruct((count, 256), BF16),
            jax.ShapeDtypeStruct((count, 128), F32),
            jax.ShapeDtypeStruct((128, count), BF16),
            jax.ShapeDtypeStruct((count, 128), F32),
            jax.ShapeDtypeStruct((384, 256), F32),
        ],
        in_specs=[pl.BlockSpec(memory_space=pltpu.SMEM), vm] + [any_space] * 4 + [vm] * 3,
        out_specs=[any_space] * 5 + [vm] * 2 + [any_space] * 7,
        scratch_shapes=[
            pltpu.VMEM((w_rows[0], width), BF16),
            pltpu.VMEM((128, width), BF16),
            pltpu.VMEM((count, FEAT), BF16),
            pltpu.VMEM((count, FEAT), BF16),
            pltpu.VMEM((count, 256), BF16),
            pltpu.VMEM((count, 128), F32),
            pltpu.VMEM((128, count), BF16),
            pltpu.VMEM((count, 128), F32),
            pltpu.VMEM((384, 256), F32),
            pltpu.SemaphoreType.DMA((len(HELD),)),
            pltpu.VMEM(shape, BF16),
            pltpu.VMEM(shape, BF16),
            pltpu.VMEM((15, half, width), BF16),
            pltpu.VMEM((2, half, width), F32),
            pltpu.VMEM((count, 256), BF16),
            pltpu.VMEM((384, 256), F32),
            pltpu.VMEM((peers, 384, 256), F32),
            pltpu.SemaphoreType.DMA((peers,)),
            pltpu.SemaphoreType.DMA((peers,)),
            pltpu.SemaphoreType.DMA((CUBE + 3,)),
            *sum_sems(),
            *gather_sems(),
            *gather_sems(),
            *spread_sems(n),
            *spread_sems(n),
            *spread_sems(n),
        ],
        compiler_params=pltpu.CompilerParams(collective_id=1, has_side_effects=True, vmem_limit_bytes=62 * MIB),
    )(lengths, tokens.reshape(2, half, width), pack_a, pack_o, pack_b, cot.reshape(2, half, width), *spreaders())


def mlp_kernel(
    n, load_own, own, w_ref, wo_ref, y_turned, mid_hbm, w_hbm, pack_d, cot_hbm,
    grads_u, tiles_d, tiles_g, out_half, grads_o, d_mid, dy_ref,
    wide, wide_g, part, heap, total, w_gu, hidden, down, by_gate, by_up, d_gate, d_up, grads_d, lsem, *sems,
):
    s, t, j, base = whereabouts()
    half, width = own.shape[1:]
    rows = 2 * half
    in_kernel = len(pack_d.shape) == 3
    two_sem, attn_sem, low_sem, out_sem = sems[0:5], sems[5:10], sems[10:16], sems[16:22]
    d_sem, back_d_sem, back_g_sem = sems[22:25], sems[25:28], sems[28:31]

    load_w = pltpu.make_async_copy(w_hbm, w_gu, lsem.at[0])
    load_mid = pltpu.make_async_copy(mid_hbm, d_mid, lsem.at[1])
    load_w.start()
    load_mid.start()
    greet_all(n)
    load_own.wait()
    load_cot = pltpu.make_async_copy(cot_hbm, wide_g, lsem.at[6])
    load_cot.start()
    g_two = Gather(own, wide, two_sem)
    if in_kernel:
        spread_d = Spread(n, pack_d, down, d_sem)
        tick = Trickle(spread_d.trickle())
    else:
        copy_d = pltpu.make_async_copy(pack_d, down, lsem.at[2])
        tick = Trickle([copy_d])

    for r in g_two.blocks(lambda: tick(2)):
        if r == 0:
            load_w.wait()
        jj = flip(j, r)
        at = pl.ds(pl.multiple_of(jj * rows, rows), rows)
        low = wide[jj].reshape(rows, width)
        gate = dot_nt(w_gu[0:UNITS, :], low)
        up = dot_nt(w_gu[UNITS:, :], low)
        sigma = jax.nn.sigmoid(gate)
        silu = gate * sigma
        hidden[:, at] = (silu * up).astype(BF16)
        by_gate[:, at] = (up * sigma * (1.0 + gate * (1.0 - sigma))).astype(BF16)
        by_up[:, at] = silu.astype(BF16)
    tick.flush()
    load_cot.wait()
    if in_kernel:
        spread_d.finish()
    else:
        copy_d.wait()

    low_sum = Sum(part, heap, total, low_sem)
    for idx, r in enumerate(Sum.ORDER):
        jj = flip(j, r)
        at = pl.ds(pl.multiple_of(jj * rows, rows), rows)
        grad = dot_nt(down[...], wide_g[jj].reshape(rows, width))
        dg = (grad * by_gate[:, at].astype(F32)).astype(BF16)
        du = (grad * by_up[:, at].astype(F32)).astype(BF16)
        d_gate[:, at] = dg
        d_up[:, at] = du
        for col in range(0, width, 512):
            cols = pl.ds(col, 512)
            block = dot_tn(dg, w_gu[0:UNITS, cols]) + dot_tn(du, w_gu[UNITS:, cols])
            part[jj, :, :, cols] = block.astype(BF16).reshape(2, half, 512)
        low_sum.send(r)
        if idx:
            low_sum.take(Sum.ORDER[idx - 1])
    low_sum.take(Sum.ORDER[-1])

    def weight_grad(left, right, out, first_row):
        def one(m, c):
            cols = pl.ds(pl.multiple_of(m * 256, 256), 256)
            block = dot(left[...], right[:, :, :, cols].reshape(CUBE * rows, 256))
            out[first_row : first_row + UNITS, cols] = block.astype(BF16)
            return c

        lax.fori_loop(0, width // 256, one, 0)

    weight_grad(hidden, wide_g, grads_d, 0)
    if in_kernel:
        back_d = Back(n, grads_d, tiles_d, back_d_sem)
        back_g = Back(n, w_gu.at[pl.ds(0, UNITS)], tiles_g, back_g_sem)
        tick = Trickle(back_d.trickle())
    else:
        save_d = pltpu.make_async_copy(grads_d, tiles_d, lsem.at[4])
        save_g = pltpu.make_async_copy(w_gu.at[pl.ds(0, UNITS)], tiles_g, lsem.at[7])
        tick = Trickle([save_d])
    low_sum.phase(0, tick)
    weight_grad(d_gate, wide, w_gu, 0)
    low_sum.phase(1, tick)
    weight_grad(d_up, wide, w_gu, UNITS)
    save_u = pltpu.make_async_copy(w_gu.at[pl.ds(UNITS, UNITS)], grads_u, lsem.at[3])
    save_u.start()
    tick.flush()
    low_sum.close()
    low_sum.finish()
    load_mid.wait()

    gain_two = w_ref[161:162, :].astype(F32)
    for h in range(2):

        def norm_back_two(at):
            mid = d_mid[h, at]
            root = lax.rsqrt(jnp.mean(mid * mid, axis=-1, keepdims=True) + EPS)
            normed = mid * root
            scaled = total[h, at] * gain_two
            grad = wide_g[j, h, at].astype(F32) + root * (
                scaled - normed * jnp.mean(scaled * normed, axis=-1, keepdims=True)
            )
            d_mid[h, at] = grad
            own[h, at] = grad.astype(BF16)

        row_loop(half, 16, norm_back_two)

    tick = Trickle(back_g.trickle() if in_kernel else [save_g])
    out_sum = Sum(part, heap, total, out_sem)
    waiting = list(Sum.ORDER)
    crossing = []

    def out_block():
        if waiting:
            r = waiting.pop(0)
            jj = flip(j, r)
            at = pl.ds(pl.multiple_of(jj * rows, rows), rows)
            for col in range(0, width, 512):
                cols = pl.ds(col, 512)
                part[jj, :, :, cols] = dot_tn(hidden[:, at], down[:, cols]).astype(BF16).reshape(2, half, 512)
            out_sum.send(r)
            crossing.append(r)
        if len(crossing) > 1 or crossing and not waiting:
            out_sum.take(crossing.pop(0), leave=False)

    def between():
        tick(2)
        out_block()

    for r in Gather(own, wide_g, attn_sem, UP_FIRST, HALVES).blocks(between):
        jj = flip(j, r)
        at = pl.ds(pl.multiple_of(jj * rows, rows), rows)
        dy_ref[at, :] = dot_nt(wide_g[jj].reshape(rows, width), wo_ref[...]).astype(BF16)
    tick.flush()
    while waiting or crossing:
        out_block()
    out_sum.crossed()
    save_half = pltpu.make_async_copy(part.at[:, t], out_half, lsem.at[8])
    save_half.start()

    def output_grad(m, c):
        cols = pl.ds(pl.multiple_of(m * 256, 256), 256)
        block = dot(y_turned[...], wide_g[:, :, :, cols].reshape(CUBE * rows, 256))
        grads_o[:, cols] = block.astype(BF16)
        return c

    lax.fori_loop(0, width // 256, output_grad, 0)
    save_u.wait()
    save_half.wait()
    if in_kernel:
        back_d.finish()
        back_g.finish()
    else:
        save_d.wait()
        save_g.wait()


def mlp_call(n, own, w_a, w_o, y_turned, mid, w_gu, pack_d, cot_all):
    half, width = own.shape[1:]
    count = CUBE * 2 * half
    vm = pl.BlockSpec(memory_space=pltpu.VMEM)
    any_space = pl.BlockSpec(memory_space=pl.ANY)
    if width // n % 128:
        pack_d = spread_call(n, pack_d, width, 6)
    shape = (CUBE, 2, half, width)
    tiles = (UNITS, width) if width // n % 128 else (n, UNITS, width // n)
    return pl.pallas_call(
        functools.partial(mlp_with_own, n),
        out_shape=[
            jax.ShapeDtypeStruct((UNITS, width), BF16),
            jax.ShapeDtypeStruct(tiles, BF16),
            jax.ShapeDtypeStruct(tiles, BF16),
            jax.ShapeDtypeStruct((CUBE, half, width), BF16),
            jax.ShapeDtypeStruct((128, width), BF16),
            jax.ShapeDtypeStruct((2, half, width), F32),
            jax.ShapeDtypeStruct((count, 128), BF16),
        ],
        in_specs=[any_space, vm, vm, vm] + [any_space] * 4,
        out_specs=[any_space] * 4 + [vm] * 3,
        scratch_shapes=[
            pltpu.VMEM((2, half, width), BF16),
            pltpu.VMEM(shape, BF16),
            pltpu.VMEM(shape, BF16),
            pltpu.VMEM(shape, BF16),
            pltpu.VMEM((15, half, width), BF16),
            pltpu.VMEM((2, half, width), F32),
            pltpu.VMEM((2 * UNITS, width), BF16),
            pltpu.VMEM((UNITS, count), BF16),
            pltpu.VMEM((UNITS, width), BF16),
            pltpu.VMEM((UNITS, count), BF16),
            pltpu.VMEM((UNITS, count), BF16),
            pltpu.VMEM((UNITS, count), BF16),
            pltpu.VMEM((UNITS, count), BF16),
            pltpu.VMEM((UNITS, width), BF16),
            pltpu.SemaphoreType.DMA((9,)),
            *gather_sems(),
            *gather_sems(),
            *sum_sems(),
            *sum_sems(),
            *spread_sems(n),
            *spread_sems(n),
            *spread_sems(n),
        ],
        compiler_params=pltpu.CompilerParams(collective_id=3, has_side_effects=True, vmem_limit_bytes=63 * MIB),
    )(own, w_a, w_o, y_turned, mid, w_gu, pack_d, cot_all)


def mlp_with_own(n, own_hbm, w_ref, wo_ref, y_turned, mid_hbm, w_hbm, pack_d, cot_hbm, *rest):
    outs, (own, *scratch) = rest[:7], rest[7:]
    lsem = scratch[13]
    load = pltpu.make_async_copy(own_hbm, own, lsem.at[5])
    load.start()
    mlp_kernel(n, load, own, w_ref, wo_ref, y_turned, mid_hbm, w_hbm, pack_d, cot_hbm, *outs, *scratch)


def tail_kernel(
    n, lengths, q_ref, k_ref, v_ref, y_ref, den_ref, state_ref, w_ref, tok_ref, dy_ref, grads_o,
    out_half, mid, d_mid, low_hbm, grads_b, first, second, third,
    output_ref, grad_ref, tiles_b, tiles_a,
    part, heap_a, heap_b, wide, total, c_ref, c_kept, v_kept, side, dv, turned, dqkv, grads_a,
    state_mine, state_theirs, xsend, xrecv, lsem, *sems,
):
    groups = n // CUBE
    s, t, j, base = whereabouts()
    tokens = q_ref.shape[0]
    rows = tokens // CUBE
    half = rows // 2
    width = w_ref.shape[1]
    two, three = lengths[0], lengths[0] + lengths[1]
    start = base * rows
    in_kernel = len(tiles_a.shape) == 3
    sum_out, sum_one, bsems, asems = sems[0:6], sems[6:12], sems[12:15], sems[15:18]

    load_low = pltpu.make_async_copy(low_hbm, wide, lsem.at[2])
    load_low.start()
    load_mid = pltpu.make_async_copy(mid, grad_ref, lsem.at[0])
    load_mid.start()
    load_out = pltpu.make_async_copy(out_half, part.at[:, t], lsem.at[4])
    load_out.start()
    greet_all(n)
    out_sum = Sum(part, heap_b, total, sum_out, UP_LAST, HALVES)
    back_b = Back(n, grads_b, tiles_b, bsems) if in_kernel else None

    tick = Trickle(back_b.trickle()) if in_kernel else Trickle([])

    state_mine[...] = jnp.zeros_like(state_mine)
    state = state_ref[...].astype(BF16)
    blocks = tokens // BLOCK

    def early(tb, carry):
        tq = pl.ds(pl.multiple_of(tb * BLOCK, BLOCK), BLOCK)
        _, seg = segments(two, three, start + tb * BLOCK, BLOCK, 0)
        keep = (seg == 1).astype(F32)
        c = (dy_ref[tq, :].astype(F32) / den_ref[tq, 0:1]).astype(BF16)
        m = -jnp.sum(c.astype(F32) * y_ref[tq, :], axis=-1, keepdims=True)
        m_high = m.astype(BF16).astype(F32)
        lane = lax.broadcasted_iota(jnp.int32, (BLOCK, 128), 1)
        extra = jnp.where(lane == 0, m_high, jnp.where(lane == 1, m - m_high, 0.0)).astype(BF16)
        c_ext = jnp.concatenate([c, extra], axis=1)
        c_ref[tq, :] = c_ext
        c_kept[tq, :] = c_ext * keep.astype(BF16)
        v_kept[tq, :] = v_ref[tq, :] * keep.astype(BF16)
        u = q_ref[tq, :]
        quad, line = lift(u, keep, first[...], second[...], third[...])
        state_mine[0:256, :] += dot_tn(quad, c_ext)
        state_mine[256:384, :] += dot_tn(line, c_ext)
        d_quad = dot_nt(c_ext, state[0:256]) * keep
        d_line = dot_nt(c_ext, state[256:384]) * keep
        side[tq, 0:FEAT] = lift_back(u, d_quad, d_line, first[...], second[...])
        return carry

    load_out.wait()
    for r in Sum.ORDER:
        out_sum.leave(r)
    tick(4)
    lax.fori_loop(0, blocks, early, 0)
    done = exchange(groups, state_mine, state_theirs, xsend, xrecv, False)
    for tb in range(blocks):
        tq = pl.ds(tb * BLOCK, BLOCK)
        qt = q_ref[tq, :] * BF16(0.25)
        score = dot_nt(qt, k_ref[tq, :])
        mask = pair_mask(two, three, start + tb * BLOCK, start + tb * BLOCK, BLOCK)
        grad = jnp.where(mask, dot_nt(c_ref[tq, :], v_ref[tq, :]) * (1.0 + score), 0.0).astype(BF16)
        acc = dot(grad, k_ref[tq, :])
        for lo in range(0, tb * BLOCK, 512):
            sq = pl.ds(lo, min(512, tb * BLOCK - lo))
            score = dot_nt(qt, k_ref[sq, :])
            grad = (dot_nt(c_kept[tq, :], v_kept[sq, :]) * (1.0 + score)).astype(BF16)
            acc = acc + dot(grad, k_ref[sq, :])
        side[tq, 0:FEAT] = (side[tq, 0:FEAT] + acc * 0.5) * 0.5
        tick()
    out_sum.phase(0)
    for sb in range(blocks):
        sq = pl.ds(sb * BLOCK, BLOCK)
        ks = k_ref[sq, :] * BF16(0.25)
        score = dot_nt(ks, q_ref[sq, :])
        mask = pair_mask_turned(two, three, start + sb * BLOCK, start + sb * BLOCK, BLOCK)
        grad = jnp.where(mask, dot_nt(v_ref[sq, :], c_ref[sq, :]) * (1.0 + score), 0.0).astype(BF16)
        weight = jnp.where(mask, pair_weight(score), 0.0).astype(BF16)
        acc = dot(grad, q_ref[sq, :])
        near = dot(weight, c_ref[sq, :])
        far = jnp.zeros((BLOCK, 256), F32)
        for lo in range((sb + 1) * BLOCK, tokens, 512):
            tq = pl.ds(lo, min(512, tokens - lo))
            score = dot_nt(ks, q_ref[tq, :])
            grad = (dot_nt(v_kept[sq, :], c_kept[tq, :]) * (1.0 + score)).astype(BF16)
            acc = acc + dot(grad, q_ref[tq, :])
            far = far + dot(pair_weight(score).astype(BF16), c_kept[tq, :])
        _, seg = segments(two, three, start + sb * BLOCK, BLOCK, 0)
        side[sq, FEAT : 2 * FEAT] = acc * 0.5
        dv[sq, :] = (near + far * (seg == 1).astype(F32))[:, :128]
        tick()
        if sb == blocks // 2:
            out_sum.phase(1)
    tick.flush()
    out_sum.close()
    state_back = done().astype(BF16)

    def late(sb, carry):
        sq = pl.ds(pl.multiple_of(sb * BLOCK, BLOCK), BLOCK)
        _, seg = segments(two, three, start + sb * BLOCK, BLOCK, 0)
        keep = (seg == 1).astype(F32)
        u = k_ref[sq, :]
        v = v_ref[sq, :]
        quad, line = lift(u, keep, first[...], second[...], third[...])
        d_quad = dot_nt(v, state_back[0:256]) * keep
        d_line = dot_nt(v, state_back[256:384]) * keep
        more = dot(quad, state_back[0:256]) + dot(line, state_back[256:384])
        dk = (side[sq, FEAT : 2 * FEAT] + lift_back(u, d_quad, d_line, first[...], second[...])) * 0.5
        dqkv[sq, 0:128] = (dv[sq, :] + more[:, :128]).astype(BF16)
        packed = dot(side[sq, 0:FEAT].astype(BF16), third[...]) + dot(dk.astype(BF16), third_shifted(third[...]))
        dqkv[sq, 128:256] = packed.astype(BF16)
        turned[:, sq] = dqkv[sq, :].T
        return carry

    lax.fori_loop(0, blocks, late, 0)
    out_sum.finish(crossed=True)
    load_mid.wait()
    for h in range(2):

        def finish_output(at):
            output_ref[h, at] = (grad_ref[h, at] + total[h, at]).astype(BF16)

        row_loop(half, 16, finish_output)
    load_mid = pltpu.make_async_copy(d_mid, grad_ref, lsem.at[1])
    load_mid.start()

    load_low.wait()
    one_sum = Sum(part, heap_a, total, sum_one)
    w_one = w_ref[0:160, :]
    for idx, r in enumerate(Sum.ORDER):
        jj = flip(j, r)
        for h in range(2):
            at = pl.ds(pl.multiple_of(jj * rows + h * half, half), half)
            part[jj, h] = dot(dqkv[at, 0:160], w_one).astype(BF16)
        one_sum.send(r)
        if idx:
            one_sum.take(Sum.ORDER[idx - 1])
    one_sum.take(Sum.ORDER[-1])

    def one_grad(m, c):
        cols = pl.ds(pl.multiple_of(m * 256, 256), 256)
        block = dot(turned[0:160, :], wide[:, :, :, cols].reshape(tokens, 256))
        grads_a[0:160, cols] = block.astype(BF16)
        return c

    lax.fori_loop(0, width // 256, one_grad, 0)
    grads_a[160:288, :] = grads_o[...]
    if in_kernel:
        back_a = Back(n, grads_a, tiles_a, asems)
        back_a.start()
    else:
        copy = pltpu.make_async_copy(grads_a, tiles_a, lsem.at[3])
        copy.start()
    one_sum.phase(0)
    one_sum.phase(1)
    one_sum.close()
    one_sum.finish()

    gain_one = w_ref[160:161, :].astype(F32)
    load_mid.wait()
    for h in range(2):

        def norm_back_one(at):
            x = tok_ref[h, at].astype(F32)
            root = lax.rsqrt(jnp.mean(x * x, axis=-1, keepdims=True) + EPS)
            normed = x * root
            scaled = total[h, at] * gain_one
            grad_ref[h, at] = grad_ref[h, at] + root * (
                scaled - normed * jnp.mean(scaled * normed, axis=-1, keepdims=True)
            )

        row_loop(half, 16, norm_back_one)

    if in_kernel:
        back_b.finish()
        back_a.finish()
    else:
        copy.wait()


def third_shifted(third):
    return jnp.concatenate([jnp.zeros_like(third[:, :FEAT]), third[:, : 128 - FEAT]], axis=1)


def tail_call(n, lengths, q, k, v, y, den, state, w_a, mid, tokens, d_mid, dy, grads_o, out_half, low_one, grads_b):
    groups = n // CUBE
    _, half, width = mid.shape
    rows = 2 * half
    count = CUBE * rows
    wide_columns = width // n % 128 == 0
    vm = pl.BlockSpec(memory_space=pltpu.VMEM)
    any_space = pl.BlockSpec(memory_space=pl.ANY)
    peers = max(groups - 1, 1)
    out_shape = [
        jax.ShapeDtypeStruct((2, half, width), BF16),
        jax.ShapeDtypeStruct((2, half, width), F32),
        jax.ShapeDtypeStruct((n, grads_b.shape[0], width // n) if wide_columns else (8, 128), BF16),
        jax.ShapeDtypeStruct((n, 288, width // n) if wide_columns else (288, width), BF16),
    ]
    output, grad, tiles_b, tiles_a = pl.pallas_call(
        functools.partial(tail_kernel, n),
        out_shape=out_shape,
        in_specs=[pl.BlockSpec(memory_space=pltpu.SMEM)] + [vm] * 10 + [any_space] * 5 + [vm] * 3,
        out_specs=[vm, vm, any_space, any_space],
        scratch_shapes=[
            pltpu.VMEM((CUBE, 2, half, width), BF16),
            pltpu.VMEM((15, half, width), BF16),
            pltpu.VMEM((15, half, width), BF16),
            pltpu.VMEM((CUBE, 2, half, width), BF16),
            pltpu.VMEM((2, half, width), F32),
            pltpu.VMEM((count, 256), BF16),
            pltpu.VMEM((count, 256), BF16),
            pltpu.VMEM((count, 256), BF16),
            pltpu.VMEM((count, 128), F32),
            pltpu.VMEM((count, 128), F32),
            pltpu.VMEM((256, count), BF16),
            pltpu.VMEM((count, 256), BF16),
            pltpu.VMEM((288, width), BF16),
            pltpu.VMEM((384, 256), F32),
            pltpu.VMEM((peers, 384, 256), F32),
            pltpu.SemaphoreType.DMA((peers,)),
            pltpu.SemaphoreType.DMA((peers,)),
            pltpu.SemaphoreType.DMA((5,)),
            *sum_sems(),
            *sum_sems(),
            *spread_sems(n),
            *spread_sems(n),
        ],
        compiler_params=pltpu.CompilerParams(collective_id=2, has_side_effects=True, vmem_limit_bytes=63 * MIB),
    )(
        lengths, q, k, v, y, den, state, w_a, tokens.reshape(2, half, width), dy, grads_o,
        out_half, mid, d_mid, low_one, grads_b, *spreaders(),
    )
    if not wide_columns:
        tiles_b = back_call(n, grads_b, 9)
        tiles_a = back_call(n, tiles_a, 10)
    return output.reshape(rows, width), grad.reshape(rows, width), tiles_b, tiles_a


def units_first(w):
    return jnp.pad(w, ((0, CUBE * UNITS - w.shape[0]), (0, 0))).reshape(CUBE, UNITS, w.shape[1])


def body(
    n, tokens, gain_attn, w_query, w_key, w_value, w_output, gain_mlp, w_gate, w_up, w_down, seq_lengths, cotangent
):
    per = HEADS // lax.axis_size("tensor")
    gains = jnp.concatenate([gain_attn[None], gain_mlp[None], jnp.zeros((14, gain_attn.shape[0]), BF16)], axis=0)
    pack_a = jnp.concatenate(
        [
            w_value.T.reshape(per, 128, -1),
            w_query.T.reshape(per, FEAT, -1),
            w_key.T.reshape(per, FEAT, -1),
            jnp.broadcast_to(gains[None], (per, *gains.shape)),
        ],
        axis=1,
    )
    pack_o = w_output.reshape(per, 128, -1)
    pack_b = jnp.concatenate([units_first(w_gate.T), units_first(w_up.T)], axis=1)
    w_a, w_o, w_gu, cot_all, low_one, low_two, mid, q, k, v, y, y_turned, den, state = head_call(
        n, seq_lengths, pack_a, pack_o, pack_b, tokens, cotangent
    )
    grads_u, tiles_d, tiles_g, out_half, grads_o, d_mid, dy = mlp_call(
        n, low_two, w_a, w_o, y_turned, mid, w_gu, units_first(w_down), cot_all
    )
    if tiles_d.ndim == 2:
        tiles_d, tiles_g = back_call(n, tiles_d, 7), back_call(n, tiles_g, 8)
    output, grad_tokens, tiles_u, tiles_a = tail_call(
        n, seq_lengths, q, k, v, y, den, state, w_a, mid, tokens, d_mid, dy, grads_o, out_half, low_one, grads_u
    )

    def arrived(tiles):
        return tiles.reshape(-1, CUBE, *tiles.shape[1:]).astype(F32).sum(axis=0)

    back_g, back_u, back_d, back_a = arrived(tiles_g), arrived(tiles_u), arrived(tiles_d), arrived(tiles_a)

    def units(part):
        return part.reshape(CUBE * UNITS, -1)[: w_gate.shape[1]]

    grad_gate = units(back_g).T
    grad_up = units(back_u).T
    grad_down = units(back_d)
    grad_value = back_a[:, 0:128].reshape(per * 128, -1).T
    grad_query = back_a[:, 128:144].reshape(per * FEAT, -1).T
    grad_key = back_a[:, 144:160].reshape(per * FEAT, -1).T
    grad_output = back_a[:, 160:288].reshape(per * 128, -1)

    def weighed(*pairs):
        return sum(jnp.sum(w.astype(F32) * g, axis=1) for w, g in pairs)

    gain_one_part = weighed((w_value, grad_value), (w_query, grad_query), (w_key, grad_key))
    gain_two_part = weighed((w_gate, grad_gate), (w_up, grad_up))
    both = lax.psum(jnp.stack([gain_one_part, gain_two_part]), "tensor")
    grad_gain_one = both[0] / gain_attn.astype(F32)
    grad_gain_two = both[1] / gain_mlp.astype(F32)
    return (
        output,
        grad_tokens,
        grad_gain_one,
        grad_query,
        grad_key,
        grad_value,
        grad_output,
        grad_gain_two,
        grad_gate,
        grad_up,
        grad_down,
    )


def solution(mesh):
    return jax.shard_map(
        functools.partial(body, mesh.shape["seq"]),
        mesh=mesh,
        in_specs=(
            P("seq", None),
            P("seq"),
            P("seq", "tensor"),
            P("seq", "tensor"),
            P("seq", "tensor"),
            P("tensor", "seq"),
            P("seq"),
            P("seq", "tensor"),
            P("seq", "tensor"),
            P("tensor", "seq"),
            P(),
            P("seq", None),
        ),
        out_specs=(
            P("seq", None),
            P("seq", None),
            P("seq"),
            P("seq", "tensor"),
            P("seq", "tensor"),
            P("seq", "tensor"),
            P("tensor", "seq"),
            P("seq"),
            P("seq", "tensor"),
            P("seq", "tensor"),
            P("tensor", "seq"),
        ),
        check_vma=False,
    )
```
